32 devices in a mesh: dp: 4 (over z), tensor: 8 (over y, x, core).
Axes of the slice: x: 2, y: 2, z: 4, core: 2. Of those that a mesh axis runs over, the one named last changes fastest.
Arguments:
- tokens: bfloat16 [8, 1024, 2048], P('dp', 'tensor'), may hold values from -6 to 6
- lengths: int32 [8], P('dp'), may hold values from 256 to 1024, as said below
- query_weight: bfloat16 [2048, 2048], P(None, 'tensor'), may hold values from -0.125 to 0.125
- key_weight: bfloat16 [2048, 128], replicated, may hold values from -0.125 to 0.125
- value_weight: bfloat16 [2048, 128], replicated, may hold values from -0.125 to 0.125
- output_weight: bfloat16 [2048, 2048], P('tensor'), may hold values from -2 to 2
- gate_weight: bfloat16 [2048, 5632], P(None, 'tensor'), may hold values from -0.125 to 0.125
- up_weight: bfloat16 [2048, 5632], P(None, 'tensor'), may hold values from -0.125 to 0.125
- down_weight: bfloat16 [5632, 2048], P('tensor'), may hold values from -0.078125 to 0.078125
- gain_attn: bfloat16 [2048], replicated, may hold values from 0.5 to 1.5
- gain_mlp: bfloat16 [2048], replicated, may hold values from 0.5 to 1.5
- pair_grad: float32 [4, 8, 2048, 256], P('dp', 'tensor'), may hold values from -240 to 240
- cotangent: bfloat16 [8, 1024, 2048], P('dp', 'tensor'), may hold values from -6 to 6
Outputs:
- output: bfloat16 [8, 1024, 2048], P('dp', 'tensor')
- grad_tokens: float32 [8, 1024, 2048], P('dp', 'tensor')
- grad_query: float32 [2048, 2048], P(None, 'tensor')
- grad_key: float32 [2048, 128], replicated
- grad_value: float32 [2048, 128], replicated
- output_weight_gradient: float32 [2048, 2048], P('tensor')
- grad_gate: float32 [2048, 5632], P(None, 'tensor')
- grad_up: float32 [2048, 5632], P(None, 'tensor')
- down_weight_gradient: float32 [5632, 2048], P('tensor')
- grad_gain_attn: float32 [2048], replicated
- grad_gain_mlp: float32 [2048], replicated
The draws below stay inside these ranges and needn't reach their ends.
Inputs may be any that keep to these rules, and one draw needn't show every extreme that they name: `lengths`: in every draw at least one sequence fills its whole slot of 1024 positions.
All inputs are finite; a program needn't handle non-finite values.
Results may differ from the reference program's by a relative error of at most 0.013.
Values may be sent and summed in bfloat16 or wider, within the bound.
No kernel may reach another device: no remote copies, remote signals or barrier semaphores. Data moves between devices by JAX's collectives and lax.ppermute only.
A program may use at most 256 MiB of HBM per device.

```python
import jax
import jax.numpy as jnp
from jax import lax

D = 2048
HEADS = 16
HEAD = 128
FF = 5632
LMAX = 1024
SEQ_GRP = 2
SEQS = 8
N_DP = 4
N_TENSOR = 8


def draw_lengths(key, part):
    first_key, second_key = jax.random.split(key)
    drawn_len = jax.random.randint(first_key, (SEQS,), LMAX // 4, LMAX + 1)
    longest = jax.random.randint(second_key, (), 0, SEQS)
    return jnp.where(jnp.arange(SEQS) == longest, LMAX, drawn_len).astype(jnp.int32)


def shard_levels(key, dims, pieces, least, high):
    factor_of = 1.0
    for position, shards_of in pieces:
        draws = jax.random.uniform(jax.random.fold_in(jax.random.fold_in(key, 6), position), (shards_of,), jnp.float32, least / len(pieces), high / len(pieces))
        factor_of = factor_of * jnp.repeat(jnp.exp(draws), dims[position] // shards_of).reshape((-1,) + (1,) * (len(dims) - 1 - position))
    return factor_of


def normal_values(rng, shape, spread, reach, pieces=(), kind=jnp.bfloat16):
    values = jax.random.normal(rng, shape, jnp.float32) * spread
    if len(pieces) > 0:
        values = shard_levels(rng, shape, pieces, -0.22, 0.18) * values
    return jnp.clip(values, min=-reach, max=reach).astype(kind)


def setup_inputs(seed: int = 0) -> dict:
    arg_keys = jax.random.split(jax.random.key(seed), 14)
    tokens = normal_values(arg_keys[0], (SEQS, LMAX, D), 1.0, 6.0, ((0, 4), (1, 8)))
    lengths = draw_lengths(jax.random.fold_in(arg_keys[13], 71), 0)
    query_weight = normal_values(arg_keys[2], (D, HEADS * HEAD), D ** -0.5, 0.125, ((1, 8),))
    key_weight = normal_values(arg_keys[3], (D, HEAD), D ** -0.5, 0.125)
    value_weight = normal_values(arg_keys[4], (D, HEAD), D ** -0.5, 0.125)
    output_weight = normal_values(arg_keys[5], (HEADS * HEAD, D), (max(HEADS * HEAD // 256, 1)) ** -0.5, 2.0, ((0, 8),))
    gate_weight = normal_values(arg_keys[6], (D, FF), D ** -0.5, 0.125, ((1, 8),))
    up_weight = normal_values(arg_keys[7], (D, FF), D ** -0.5, 0.125, ((1, 8),))
    down_weight = normal_values(arg_keys[8], (FF, D), FF ** -0.5, 0.078125, ((0, 8),))
    gain_attn = jnp.clip(1.0 + 0.1 * jax.random.normal(arg_keys[9], (D,), jnp.float32), 0.5, 1.5).astype(jnp.bfloat16)
    gain_mlp = jnp.clip(1.0 + 0.1 * jax.random.normal(arg_keys[10], (D,), jnp.float32), 0.5, 1.5).astype(jnp.bfloat16)
    pair_grad = normal_values(arg_keys[11], (N_DP, N_TENSOR, D, 2 * HEAD), 40.0, 240.0, ((0, 4), (1, 8)), jnp.float32)
    cotangent = normal_values(arg_keys[12], (SEQS, LMAX, D), 1.0, 6.0, ((0, 4), (1, 8)))
    return {"tokens": tokens, "lengths": lengths, "query_weight": query_weight, "key_weight": key_weight, "value_weight": value_weight, "output_weight": output_weight, "gate_weight": gate_weight, "up_weight": up_weight, "down_weight": down_weight, "gain_attn": gain_attn, "gain_mlp": gain_mlp, "pair_grad": pair_grad, "cotangent": cotangent}


SMALL_SHIFT = 1e-05
ROPE_BASE = 10000.0
NEG_FILL = -1e+30
exact_precision = lax.Precision.HIGHEST

@jax.custom_vjp
def low(v):
    return lax.optimization_barrier(v.astype(jnp.bfloat16)).astype(jnp.float32)

@jax.custom_vjp
def lowered_backward(v):
    return v

def low_keep(v):
    return (low(v), None)

def low_pass(kept, grad):
    return (grad,)

def back_keep(v):
    return (v, None)

def back_low(kept, grad):
    return (low(grad),)
low.defvjp(low_keep, low_pass)
lowered_backward.defvjp(back_keep, back_low)

def rms_scale(values):
    return lax.rsqrt(lax.optimization_barrier(jnp.mean(values * values, axis=-1, keepdims=True)) + SMALL_SHIFT)

def rope_tables(span_len, head_width):
    half_width = head_width // 2
    frequency = ROPE_BASE ** (-2.0 * jnp.arange(half_width, dtype=jnp.float32) / head_width)
    angles = jnp.arange(span_len, dtype=jnp.float32)[:, None] * frequency[None, :]
    angles = jnp.concatenate([angles, angles], axis=1)
    return (jnp.cos(angles), jnp.sin(angles))

def rotate(values, cosine, sine_tab):
    half_width = values.shape[-1] // 2
    turned = jnp.concatenate([-values[..., half_width:], values[..., :half_width]], axis=-1)
    return values * cosine + turned * sine_tab

def attend(packed):
    query_seq, key_seq, value_seq, seq_len = packed
    scores = lowered_backward(jnp.einsum('qhc,hkc->hqk', query_seq, key_seq, precision=exact_precision) * HEAD ** (-0.5))
    query_pos = jnp.arange(LMAX)[:, None]
    key_pos = jnp.arange(LMAX)[None, :]
    allowed = ((key_pos <= query_pos) & (key_pos < seq_len))[None]
    masked = jnp.where(allowed, scores, NEG_FILL)
    top_score = lax.optimization_barrier(jnp.max(masked, axis=-1, keepdims=True))
    exp_terms = jnp.exp(masked - top_score)
    probs_all = exp_terms / lax.optimization_barrier(jnp.sum(exp_terms, axis=-1, keepdims=True))
    merged_channel_matrix = jnp.einsum('hqk,hkc->qhc', low(probs_all), value_seq, precision=exact_precision)
    return merged_channel_matrix.reshape(LMAX, HEADS * HEAD)

def forward(group_x, weight_set, valid_rows, group_len):
    query_weight, key_weight, value_weight, output_weight, gate_weight, up_weight, down_weight, gain_attn, gain_mlp = weight_set
    seq_count = group_x.shape[0]
    cosine, sine_tab = rope_tables(LMAX, HEAD)
    normalized_input = low(group_x * rms_scale(group_x) * gain_attn)
    unrotated_query = lowered_backward(jnp.einsum('wav,vh->wah', normalized_input, query_weight, precision=exact_precision))
    shared_head_unrotated = lowered_backward(jnp.einsum('wav,vh->wah', normalized_input, jnp.concatenate([key_weight, value_weight], axis=1), precision=exact_precision))
    kv_heads = jnp.broadcast_to(shared_head_unrotated[:, None], (seq_count, HEADS, LMAX, 2 * HEAD))
    query_heads = low(rotate(unrotated_query.reshape(seq_count, LMAX, HEADS, HEAD), cosine[:, None, :], sine_tab[:, None, :]))
    key_heads = low(rotate(kv_heads[..., :HEAD], cosine, sine_tab))
    value_heads = low(kv_heads[..., HEAD:])
    combined_everything = lax.map(jax.checkpoint(attend), (query_heads, key_heads, value_heads, group_len))
    combined_everything = lowered_backward(low(combined_everything))
    attention_result = lowered_backward(jnp.einsum('ago,ok->agk', combined_everything, output_weight, precision=exact_precision))
    hidden = group_x + valid_rows * attention_result
    normalized_middle = low(hidden * rms_scale(hidden) * gain_mlp)
    gate_entries = lowered_backward(jnp.einsum('kcj,jr->kcr', normalized_middle, gate_weight, precision=exact_precision))
    up_entries = lowered_backward(jnp.einsum('kcj,jr->kcr', normalized_middle, up_weight, precision=exact_precision))
    activation_entries = low(jax.nn.silu(gate_entries) * up_entries)
    feedforward_result = lowered_backward(jnp.einsum('aeo,ok->aek', activation_entries, down_weight, precision=exact_precision))
    return hidden + valid_rows * feedforward_result

def reference(tokens, lengths, query_weight, key_weight, value_weight, output_weight, gate_weight, up_weight, down_weight, gain_attn, gain_mlp, pair_grad, cotangent):
    weights = tuple((weight_item.astype(jnp.float32) for weight_item in (query_weight, key_weight, value_weight, output_weight, gate_weight, up_weight, down_weight, gain_attn, gain_mlp)))
    group_tokens = tokens.astype(jnp.float32).reshape(N_DP, SEQ_GRP, LMAX, D)
    group_grads = cotangent.astype(jnp.float32).reshape(N_DP, SEQ_GRP, LMAX, D)
    group_lens = lengths.reshape(N_DP, SEQ_GRP)

    def one_group(totals, inputs):
        group_x, group_len, group_dy = inputs
        valid_rows = (jnp.arange(LMAX)[None, :] < group_len[:, None]).astype(jnp.float32)[..., None]
        result, pull_back = jax.vjp(lambda group_in, weight_set: forward(group_in, weight_set, valid_rows, group_len), group_x, weights)
        grad_in, grad_set = pull_back(group_dy)
        totals = tuple((total_item + grad_item for total_item, grad_item in zip(totals, grad_set)))
        return (totals, (result.astype(jnp.bfloat16), grad_in))
    zeros_set = tuple((jnp.zeros(weight_item.shape, jnp.float32) for weight_item in weights))
    totals, (outputs, grad_tokens) = lax.scan(one_group, zeros_set, (group_tokens, group_lens, group_grads))
    pair_total = lax.optimization_barrier(jnp.sum(pair_grad, axis=(0, 1)))
    return (outputs.reshape(SEQS, LMAX, D), grad_tokens.reshape(SEQS, LMAX, D), totals[0], totals[1] + pair_total[:, :HEAD], totals[2] + pair_total[:, HEAD:], totals[3], totals[4], totals[5], totals[6], totals[7], totals[8])
```

```python
import functools

import jax
import jax.numpy as jnp
from jax import lax
from jax.experimental import pallas as pl
from jax.experimental.pallas import tpu as pltpu
from jax.sharding import PartitionSpec as P

HEAD = 128
KEY_BLOCK = 256
SMALL_SHIFT = 1e-05
ROPE_BASE = 10000.0
NEG_FILL = -1e30
LOG2E = 1.4426950408889634
F32 = jnp.float32
BF16 = jnp.bfloat16


def rms_scale(values):
    return lax.rsqrt(jnp.mean(values * values, axis=-1, keepdims=True) + SMALL_SHIFT)


def normed(values, gain_vec):
    return values * rms_scale(values) * gain_vec


def norm_back(values, gain_vec, grad_vals):
    scale_vals = rms_scale(values)
    scaled = grad_vals * gain_vec
    inner_mean = jnp.mean(scaled * values, axis=-1, keepdims=True)
    grad_values = scale_vals * scaled - values * (scale_vals * scale_vals * scale_vals) * inner_mean
    grad_gain = jnp.sum(grad_vals * values * scale_vals, axis=(0, 1))
    return grad_values, grad_gain


def rope_block(start, rows):
    half = HEAD // 2
    frequency = ROPE_BASE ** (-2.0 * jnp.arange(half, dtype=F32) / HEAD)
    angles = (start + jnp.arange(rows)).astype(F32)[:, None] * frequency[None, :]
    cosine, sine = jnp.cos(angles), jnp.sin(angles)
    return jnp.concatenate([cosine, cosine], 1), jnp.concatenate([-sine, sine], 1)


def swap(values, bit):
    n = lax.axis_size("tensor")
    return lax.ppermute(values, "tensor", [(i, i ^ bit) for i in range(n)])


def dot(a, b, dims, out=F32):
    return lax.dot_general(a, b, (dims, ((), ())), preferred_element_type=F32).astype(out)


def add_up(*parts):
    total = parts[0].astype(F32)
    for part in parts[1:]:
        total = total + part.astype(F32)
    return total


def key_branches(start, rows, span, body):
    blocks = span // KEY_BLOCK
    needed = (start + rows + KEY_BLOCK - 1) // KEY_BLOCK
    for count in range(1, blocks + 1):
        pl.when(needed == count)(functools.partial(body, count * KEY_BLOCK))


def stack_heads(values, heads):
    return jnp.concatenate([values[:, h * HEAD : (h + 1) * HEAD] for h in range(heads)], axis=0)


def matmul(a, b, contract):
    return lax.dot_general(a, b, (contract, ((), ())), preferred_element_type=F32)


def masked_scores(keys, query, start, rows, heads, count):
    scores = matmul(keys, query, ((1,), (1,)))
    key_pos = lax.broadcasted_iota(jnp.int32, (KEY_BLOCK, rows), 0) + (count - KEY_BLOCK)
    row_pos = lax.broadcasted_iota(jnp.int32, (KEY_BLOCK, rows), 1) + start
    allowed = key_pos <= row_pos
    last = scores[count - KEY_BLOCK :]
    last = jnp.concatenate(
        [jnp.where(allowed, last[:, h * rows : (h + 1) * rows], NEG_FILL) for h in range(heads)], axis=1
    )
    if count == KEY_BLOCK:
        return last
    return jnp.concatenate([scores[: count - KEY_BLOCK], last], axis=0)


def forward_kernel(
    place, lengths, x0_ref, x1_ref, wq_ref, kv_ref, cos_ref, sin_ref, mixed_ref, query_ref, lse_ref, raw_ref, vt_ref
):
    a = pl.program_id(0)
    seqs, span = kv_ref.shape[0], kv_ref.shape[1]
    rows = x0_ref.shape[0] // seqs
    heads = wq_ref.shape[1] // HEAD
    start = place[a] * rows
    cosine, sine = cos_ref[0], sin_ref[0]
    factor = HEAD ** (-0.5) * LOG2E

    @pl.when(a == 0)
    def _():
        raw_ref[...] = matmul(x0_ref[...], wq_ref[...], ((1,), (0,)))
        for s in range(seqs):
            vt_ref[s] = kv_ref[s, :, HEAD:].T

    @pl.when(a == 1)
    def _():
        raw_ref[...] = matmul(x1_ref[...], wq_ref[...], ((1,), (0,)))

    for s in range(seqs):
        here = slice(s * rows, (s + 1) * rows)
        pieces = []
        for h in range(heads):
            raw = raw_ref[here, h * HEAD : (h + 1) * HEAD]
            pieces.append((raw * cosine + pltpu.roll(raw, HEAD // 2, 1) * sine).astype(BF16))
        query = jnp.concatenate(pieces, axis=0)
        query_ref[0, s] = query
        live = start < lengths[s]

        def body(count, s=s, here=here, query=query):
            scores = masked_scores(kv_ref[s, :count, :HEAD], query, start, rows, heads, count)
            top = jnp.max(scores, axis=0, keepdims=True)
            terms = jnp.exp2((scores - top) * factor)
            total = jnp.sum(terms, axis=0, keepdims=True)
            out = matmul(vt_ref[s, :, :count], terms.astype(BF16), ((1,), (0,))) / total
            lse_ref[0, s] = jnp.broadcast_to(top * factor + jnp.log2(total), lse_ref.shape[2:])
            for h in range(heads):
                piece = out[:, h * rows : (h + 1) * rows].T
                mixed_ref[0, here, h * HEAD : (h + 1) * HEAD] = piece.astype(BF16)

        @pl.when(live)
        def _(body=body):
            key_branches(start, rows, span, body)

        @pl.when(jnp.logical_not(live))
        def _(s=s, here=here):
            mixed_ref[0, here] = jnp.zeros((rows, heads * HEAD), BF16)
            lse_ref[0, s] = jnp.zeros(lse_ref.shape[2:], F32)


def whole(shape):
    return pl.BlockSpec(shape, lambda a, *_: (0,) * len(shape))


def blocked(shape):
    return pl.BlockSpec((1, *shape[1:]), lambda a, *_: (a,) + (0,) * (len(shape) - 1))


def attention_forward(place, lengths, parts, query_weights, kv, cosine, sine):
    flat, width = parts[0].shape
    seqs, span = kv.shape[0], kv.shape[1]
    rows, wide = flat // seqs, query_weights.shape[1]
    heads = wide // HEAD
    shapes = [(2, flat, wide), (2, seqs, heads * rows, HEAD), (2, seqs, 8, heads * rows)]
    return pl.pallas_call(
        forward_kernel,
        grid_spec=pltpu.PrefetchScalarGridSpec(
            num_scalar_prefetch=2,
            grid=(2,),
            in_specs=[
                whole(parts[0].shape),
                whole(parts[1].shape),
                whole(query_weights.shape),
                whole(kv.shape),
                blocked(cosine.shape),
                blocked(sine.shape),
            ],
            out_specs=[blocked(shape) for shape in shapes],
            scratch_shapes=[pltpu.VMEM((flat, wide), F32), pltpu.VMEM((seqs, HEAD, span), BF16)],
        ),
        out_shape=[jax.ShapeDtypeStruct(s, t) for s, t in zip(shapes, (BF16, BF16, F32))],
        compiler_params=pltpu.CompilerParams(vmem_limit_bytes=48 * 1024 * 1024),
        cost_estimate=pl.CostEstimate(flops=flat * wide * span, bytes_accessed=kv.size, transcendentals=0),
        name="attention_forward",
    )(place, lengths, *parts, query_weights, kv, cosine, sine)


def backward_kernel(
    place, lengths, g0_ref, g1_ref, wo_ref, wq_ref, query_ref, lse_ref, kv_ref, cos_ref, sin_ref,
    gq_ref, in_ref, gkv_ref, gm_ref, kt_ref,
):
    a = pl.program_id(0)
    seqs, span = kv_ref.shape[0], kv_ref.shape[1]
    rows = g0_ref.shape[0] // seqs
    heads = wq_ref.shape[1] // HEAD
    start = place[a] * rows
    scale = HEAD ** (-0.5)
    factor = scale * LOG2E

    @pl.when(a == 0)
    def _():
        gm_ref[...] = matmul(g0_ref[...], wo_ref[...], ((1,), (1,))).astype(BF16)
        gkv_ref[...] = jnp.zeros(gkv_ref.shape, F32)
        for s in range(seqs):
            kt_ref[s] = kv_ref[s, :, :HEAD].T

    @pl.when(a == 1)
    def _():
        gm_ref[...] = matmul(g1_ref[...], wo_ref[...], ((1,), (1,))).astype(BF16)

    for s in range(seqs):
        here = slice(s * rows, (s + 1) * rows)
        live = start < lengths[s]

        def body(count, s=s, here=here):
            query = query_ref[0, s]
            grad = stack_heads(gm_ref[here, :], heads)
            scores = masked_scores(kv_ref[s, :count, :HEAD], query, start, rows, heads, count)
            probs = jnp.exp2(scores * factor - lse_ref[0, s, 0:1, :])
            grad_probs = matmul(kv_ref[s, :count, HEAD:], grad, ((1,), (1,)))
            row_dots = jnp.sum(probs * grad_probs, axis=0, keepdims=True)
            grad_scores = (probs * (grad_probs - row_dots)).astype(BF16)
            gkv_ref[s, :count, :HEAD] += scale * matmul(grad_scores, query, ((1,), (0,)))
            gkv_ref[s, :count, HEAD:] += matmul(probs.astype(BF16), grad, ((1,), (0,)))
            grad_query = matmul(kt_ref[s, :, :count], grad_scores, ((1,), (0,)))
            cosine, sine = cos_ref[0], sin_ref[0]
            for h in range(heads):
                piece = grad_query[:, h * rows : (h + 1) * rows].T * scale
                piece = piece * cosine - pltpu.roll(piece, HEAD // 2, 1) * sine
                gq_ref[0, here, h * HEAD : (h + 1) * HEAD] = piece.astype(BF16)

        @pl.when(live)
        def _(body=body):
            key_branches(start, rows, span, body)

        @pl.when(jnp.logical_not(live))
        def _(here=here):
            gq_ref[0, here] = jnp.zeros((rows, heads * HEAD), BF16)

    in_ref[0] = matmul(gq_ref[0], wq_ref[...], ((1,), (1,))).astype(BF16)


def attention_backward(place, lengths, grads, output_weights, query_weights, query, lse, kv, cosine, sine):
    flat, width = grads[0].shape
    seqs, span = kv.shape[0], kv.shape[1]
    wide = query_weights.shape[1]
    operands = (*grads, output_weights, query_weights, query, lse, kv, cosine, sine)
    specs = [whole(v.shape) for v in operands]
    for k in (4, 5, 7, 8):
        specs[k] = blocked(operands[k].shape)
    return pl.pallas_call(
        backward_kernel,
        grid_spec=pltpu.PrefetchScalarGridSpec(
            num_scalar_prefetch=2,
            grid=(2,),
            in_specs=specs,
            out_specs=[blocked((2, flat, wide)), blocked((2, flat, width)), whole(kv.shape)],
            scratch_shapes=[pltpu.VMEM((flat, wide), BF16), pltpu.VMEM((seqs, HEAD, span), BF16)],
        ),
        out_shape=[
            jax.ShapeDtypeStruct((2, flat, wide), BF16),
            jax.ShapeDtypeStruct((2, flat, width), BF16),
            jax.ShapeDtypeStruct(kv.shape, F32),
        ],
        compiler_params=pltpu.CompilerParams(vmem_limit_bytes=56 * 1024 * 1024),
        cost_estimate=pl.CostEstimate(flops=flat * wide * span, bytes_accessed=kv.size, transcendentals=0),
        name="attention_backward",
    )(place, lengths, *operands)


def middle_bits(n):
    bits, bit = [], 2
    while bit < n // 2:
        bits.append(bit)
        bit *= 2
    return bits


def gather_middle(values):
    parts = [values]
    for bit in middle_bits(lax.axis_size("tensor")):
        parts = parts + [swap(part, bit) for part in parts]
    return parts


def reduce_middle(parts):
    for bit in reversed(middle_bits(lax.axis_size("tensor"))):
        half = len(parts) // 2
        parts = [add_up(parts[i], swap(parts[half + i].astype(BF16), bit)) for i in range(half)]
    return parts[0]


def tie(*values):
    return lax.optimization_barrier(values)


class LineSum:
    def __init__(self):
        self.line = lax.axis_size("dp") == 4
        place = lax.axis_index("dp")
        self.outer = (place == 0) | (place == 3)
        self.inward, self.across, self.outward = [], [], []
        self.sums = []

    def advance(self, arrays, others=()):
        if not self.line:
            self.sums += [lax.psum(a, "dp") for a in arrays]
            return others
        arrays, inward, across, outward, others = tie(
            list(arrays), self.inward, self.across, self.outward, others
        )
        self.inward = [(a, lax.ppermute(a, "dp", [(0, 1), (3, 2)])) for a in arrays]
        pairs = [add_up(own, sent).astype(BF16) for own, sent in inward]
        self.across = [(a, lax.ppermute(a, "dp", [(1, 2), (2, 1)])) for a in pairs]
        totals = [add_up(own, sent).astype(BF16) for own, sent in across]
        self.outward = [(a, lax.ppermute(a, "dp", [(1, 0), (2, 3)])) for a in totals]
        self.sums += [jnp.where(self.outer, sent, own) for own, sent in outward]
        return others


def tensor_bits():
    n, bits, bit = lax.axis_size("tensor"), [], 1
    while bit < n:
        bits.append(bit)
        bit *= 2
    return bits


def reduce_blocks(blocks):
    n, me = blocks.shape[0], lax.axis_index("tensor")
    held = [lax.dynamic_index_in_dim(blocks, me ^ r, 0, keepdims=False) for r in range(n)]
    for bit in tensor_bits():
        keep = jnp.stack([held[r] for r in range(len(held)) if r % 2 == 0])
        give = jnp.stack([held[r] for r in range(len(held)) if r % 2 == 1])
        total = add_up(keep, swap(give.astype(BF16), bit))
        held = [total[k] for k in range(total.shape[0])]
    return held[0]


def gather_blocks(block):
    n, me = lax.axis_size("tensor"), lax.axis_index("tensor")
    held = block[None]
    for bit in reversed(tensor_bits()):
        other = swap(held, bit)
        held = jnp.stack([held, other], 1).reshape(2 * held.shape[0], *block.shape)
    result = jnp.zeros_like(held)
    for r in range(n):
        result = lax.dynamic_update_index_in_dim(result, held[r], me ^ r, 0)
    return result


def gather_near(values):
    if lax.axis_size("tensor") != 8:
        return values, values
    return swap(values, 2), swap(values, 4)


def gather_pairs(values):
    parts, bits = [values], tensor_bits()
    for bit in bits:
        parts = parts + [swap(part, bit) for part in parts]
    return [(parts[i], parts[i + 1]) for i in range(0, len(parts), 2)]


def halves(value):
    rows = value.shape[0] // 2
    return value[:rows], value[rows:]


def reduce_begin(count, terms):
    n = lax.axis_size("tensor")
    if n != 8:
        parts = []
        for i in range(count):
            own, other = halves(terms(i, None))
            parts.append(add_up(own, swap(other, 1)))
        while len(parts) > 1:
            half = len(parts) // 2
            parts = [add_up(parts[i], swap(parts[half + i].astype(BF16), 2 * half)) for i in range(half)]
        return parts[0], ()
    own_d, other_d = halves(terms(3, None))
    core_d = swap(other_d, 1)
    own_y, other_y = halves(terms(2, own_d))
    core_y = swap(other_y, 1)
    diagonal = add_up(own_d, core_d).astype(BF16)
    diagonal, own_y = tie(diagonal, own_y)
    first, second = halves(diagonal)
    from_x, from_y = swap(first, 2), swap(second, 4)
    own_x, other_x = halves(terms(1, diagonal))
    core_x = swap(other_x, 1)
    own, other = halves(terms(0, own_x))
    core = swap(other, 1)
    low, high = halves(add_up(own_y, core_y))
    for_y = jnp.concatenate([add_up(low, from_x), high]).astype(BF16)
    low, high = halves(add_up(own_x, core_x))
    for_x = jnp.concatenate([low, add_up(high, from_y)]).astype(BF16)
    return (own, core), (for_x, for_y)


def reduce_end(own, sent):
    if not sent:
        return own
    return add_up(*own, swap(sent[0], 2), swap(sent[1], 4))


def per_device(
    tokens,
    lengths,
    query_weight,
    key_weight,
    value_weight,
    output_weight,
    gate_weight,
    up_weight,
    down_weight,
    gain_attn,
    gain_mlp,
    pair_grad,
    cotangent,
):
    seqs, rows, width = tokens.shape
    n = lax.axis_size("tensor")
    me = lax.axis_index("tensor")
    top = n // 2
    flat = seqs * rows
    local_pos = me * rows + jnp.arange(rows)
    valid = (local_pos[None, :] < lengths[:, None]).astype(F32)[..., None]
    x = tokens.astype(F32)
    attn_gain = gain_attn.astype(F32)
    mlp_gain = gain_mlp.astype(F32)
    grad_y = cotangent.astype(F32)
    kv_weight = jnp.concatenate([key_weight, value_weight], axis=1)

    norm_in = normed(x, attn_gain).astype(BF16).reshape(flat, width)
    far_in = swap(norm_in, top)
    far_in = (far_in, swap(far_in, 1))
    near_in = (norm_in, swap(norm_in, 1))
    query_weights = jnp.concatenate(gather_middle(query_weight), axis=1)
    output_weight, query_weights = tie(output_weight, query_weights)
    output_parts = gather_middle(output_weight)
    heads_width = query_weights.shape[1]
    own_cos, own_sin = rope_block(me * rows, rows)
    kv_raw = dot(norm_in, kv_weight, ((1,), (0,))).reshape(seqs, rows, 2 * HEAD)
    key_raw = kv_raw[..., :HEAD]
    key_own = key_raw * own_cos + jnp.roll(key_raw, HEAD // 2, axis=-1) * own_sin
    kv_own = jnp.concatenate([key_own, kv_raw[..., HEAD:]], axis=-1).astype(BF16)
    kv = lax.all_gather(kv_own, "tensor", axis=1, tiled=True)

    def place_of(offset):
        place = jnp.stack([me ^ offset, me ^ (offset + 1)]).astype(jnp.int32)
        blocks = [rope_block(place[i] * rows, rows) for i in range(2)]
        return place, (jnp.stack([b[0] for b in blocks]), jnp.stack([b[1] for b in blocks]))

    def attend(part, place, table):
        return attention_forward(place, lengths, part, query_weights, kv, *table)

    def portions_of(mixed):
        return [dot(mixed[i], output_weights, ((1,), (0,)), BF16) for i in range(2)]

    near_place, near_table = place_of(0)
    far_place, far_table = place_of(top)
    grad_out = (valid * grad_y).astype(BF16).reshape(flat, width)
    grad_out, _ = tie(grad_out, norm_in)
    grad_far = swap(grad_out, top)
    near_result = attend(near_in, near_place, near_table)
    far_in, _ = tie(far_in, near_result[0])
    far_result = attend(far_in, far_place, far_table)
    output_parts, far_mixed, grad_far = tie(output_parts, far_result[0], grad_far)
    output_weights = jnp.concatenate(output_parts, axis=0)
    far_portions = portions_of(far_mixed)
    for_far = add_up(far_portions[0], swap(far_portions[1], 1)).astype(BF16)
    for_far, near_mixed = tie(for_far, near_result[0])
    from_far = swap(for_far, top)
    near_portions = portions_of(near_mixed)
    near_core = swap(near_portions[1], 1)
    if n == 8:
        grad_out, _ = tie(grad_out, far_mixed)
        grad_parts = [grad_out, swap(grad_out, 2), grad_far, swap(grad_far, 2)]
        from_far, grad_parts = tie(from_far, grad_parts)
        grad_pairs = [(part, swap(part, 1)) for part in grad_parts]
    else:
        grad_pairs = gather_pairs(grad_out)
    grad_chunks = [jnp.concatenate(c) for c in grad_pairs]
    attn_out = add_up(near_portions[0], near_core, from_far)
    hidden = x + valid * attn_out.reshape(seqs, rows, width)

    chips = n // 2
    norm_mid = normed(hidden, mlp_gain).astype(BF16).reshape(flat, width)
    gate_rows, up_rows = gate_weight.T, up_weight.T
    mid_chunks, acts, g_gates, g_ups = [], [], [], []

    def slope_of(i):
        return dot(grad_chunks[i], down_weight, ((1,), (1,)))

    def forward_chunk(pair, slope):
        mid = jnp.concatenate(pair)
        gate = dot(mid, gate_rows, ((1,), (1,)))
        up = dot(mid, up_rows, ((1,), (1,)))
        sig = 1.0 / (1.0 + jnp.exp(-gate))
        silu = gate * sig
        mid_chunks.append(mid)
        acts.append((silu * up).astype(BF16))
        g_gates.append((slope * up * sig * (1.0 + gate * (1.0 - sig))).astype(BF16))
        g_ups.append((slope * silu).astype(BF16))

    if n == 8:
        at_x, at_y = gather_near(norm_mid)
        forward_chunk((norm_mid, swap(norm_mid, 1)), slope_of(0))
        slopes = [slope_of(i) for i in range(1, 4)]
        at_x, at_y, slopes, acts[0] = tie(at_x, at_y, slopes, acts[0])
        size = flat // 2
        diagonal = [swap(at_x[:size], 4), swap(at_y[size:], 2)]
        for i, part in enumerate((at_x, at_y)):
            forward_chunk((part, swap(part, 1)), slopes[i])
        diagonal, acts[1], acts[2] = tie(diagonal, acts[1], acts[2])
        forward_chunk((*diagonal, *[swap(part, 1) for part in diagonal]), slopes[2])
    else:
        for i, pair in enumerate(gather_pairs(norm_mid)):
            forward_chunk(pair, slope_of(i))

    def mid_terms(i, after):
        left, right = g_gates[i], g_ups[i]
        if after is not None:
            left, right, _ = tie(left, right, after)
        terms = dot(left, gate_rows, ((1,), (0,))) + dot(right, up_rows, ((1,), (0,)))
        return terms.astype(BF16)

    sums = LineSum()
    act_all, grad_all = jnp.concatenate(acts), jnp.concatenate(grad_chunks)
    cut = (act_all.shape[1] // 2 + 127) // 128 * 128
    grad_down = dot(act_all[:, :cut], grad_all, ((0,), (0,)), BF16)

    g_gates, g_ups, act_all = sums.advance([grad_down], (g_gates, g_ups, act_all))
    mid_own, mid_sent = reduce_begin(chips, mid_terms)
    grad_rest = dot(act_all[:, cut:], grad_all, ((0,), (0,)), BF16)

    mid_sent, g_gates, g_ups = sums.advance([grad_rest], (mid_sent, g_gates, g_ups))
    mid_all = jnp.concatenate(mid_chunks)
    grad_gate = halves(dot(jnp.concatenate(g_gates), mid_all, ((0,), (0,)), BF16))
    grad_mid = reduce_end(mid_own, mid_sent).reshape(seqs, rows, width)
    back, mlp_gain_part = norm_back(hidden, mlp_gain, grad_mid)
    grad_hidden = grad_y + back
    grad_attn = (valid * grad_hidden).astype(BF16).reshape(flat, width)

    grad_attn, g_ups = sums.advance([grad_gate[0]], (grad_attn, g_ups))
    far_grad = swap(grad_attn, top)
    near_grad = (grad_attn, swap(grad_attn, 1))
    grad_up = halves(dot(jnp.concatenate(g_ups), mid_all, ((0,), (0,)), BF16))

    def attend_back(part, result, place, table):
        return attention_backward(
            place, lengths, part, output_weights, query_weights, result[1], result[2], kv, *table
        )

    def product(left, right):
        return dot(jnp.concatenate(left), jnp.concatenate(right), ((0,), (0,)), BF16)

    far_grad, near_grad = sums.advance([grad_gate[1]], (far_grad, near_grad))
    far_grad = (far_grad, swap(far_grad, 1))
    far_q, far_terms, far_kv = attend_back(far_grad, far_result, far_place, far_table)
    for_far = add_up(far_terms[0], swap(far_terms[1], 1)).astype(BF16)

    for_far, near_grad, far_grad = sums.advance([grad_up[0]], (for_far, near_grad, far_grad))
    from_far = swap(for_far, top)
    unit = output_weight.shape[0]
    mixed = [r[0][i] for r in (near_result, far_result) for i in range(2)]
    wo_full = product(mixed, [*near_grad, *far_grad])
    wo_part = reduce_middle([wo_full[i * unit : (i + 1) * unit] for i in range(heads_width // unit)])
    wo_part = wo_part.astype(BF16)
    near_q, near_terms, near_kv = attend_back(near_grad, near_result, near_place, near_table)
    near_core = swap(near_terms[1], 1)

    from_far, near_terms, near_core, near_q, near_kv, wo_part = sums.advance(
        [grad_up[1]], (from_far, near_terms, near_core, near_q, near_kv, wo_part)
    )
    kv_blocks = (near_kv + far_kv).astype(BF16).reshape(seqs, n, rows, 2 * HEAD).swapaxes(0, 1)
    kv_sum = reduce_blocks(kv_blocks)
    wq_full = product([*near_in, *far_in], [near_q[0], near_q[1], far_q[0], far_q[1]])
    wq_full, kv_sum = tie(wq_full, kv_sum)
    wq_part = reduce_middle([wq_full[:, i * unit : (i + 1) * unit] for i in range(heads_width // unit)])
    wq_part = wq_part.astype(BF16)
    key_grad = kv_sum[..., :HEAD]
    key_grad = key_grad * own_cos - jnp.roll(key_grad, HEAD // 2, axis=-1) * own_sin
    kv_grad = jnp.concatenate([key_grad, kv_sum[..., HEAD:]], -1).astype(BF16).reshape(flat, 2 * HEAD)
    grad_in = add_up(near_terms[0], near_core, from_far)
    grad_in = grad_in + dot(kv_grad, kv_weight, ((1,), (1,)))
    kv_portion = dot(norm_in, kv_grad, ((0,), (0,)))
    back, attn_gain_part = norm_back(x, attn_gain, grad_in.reshape(seqs, rows, width))
    grad_tokens = grad_hidden + back

    kv_portion, attn_gain_part, wq_part, acts = sums.advance(
        [wo_part], (kv_portion, attn_gain_part, wq_part, acts)
    )
    gains = jnp.concatenate([attn_gain_part, mlp_gain_part]).reshape(-1, 2 * HEAD)
    shared = jnp.concatenate([kv_portion + pair_grad[0, 0], gains])
    shared = jnp.pad(shared, ((0, -shared.shape[0] % (16 * n)), (0, 0))).astype(BF16)
    shared = reduce_blocks(shared.reshape(n, -1, 2 * HEAD)).astype(BF16)

    def out_terms(i, after):
        left = acts[i] if after is None else tie(acts[i], after)[0]
        return dot(left, down_weight, ((1,), (0,)), BF16)

    acts, shared = tie(acts, shared)
    out_own, out_sent = reduce_begin(chips, out_terms)

    out_sent = sums.advance([wq_part, shared], out_sent)
    rows_out = reduce_end(out_own, out_sent)
    output = (hidden + valid * rows_out.reshape(seqs, rows, width)).astype(BF16)
    sums.advance([])
    sums.advance([])
    sums.advance([])
    down_1, down_2, gate_1, gate_2, up_1, up_2, wo_sum, wq_sum, shared = sums.sums
    shared = gather_blocks(shared).reshape(-1, 2 * HEAD).astype(F32)
    gains = shared[width : width + gains.shape[0]].reshape(2, width)
    return (
        output,
        grad_tokens,
        wq_sum.astype(F32),
        shared[:width, :HEAD],
        shared[:width, HEAD:],
        wo_sum.astype(F32),
        jnp.concatenate([gate_1, gate_2]).astype(F32).T,
        jnp.concatenate([up_1, up_2]).astype(F32).T,
        jnp.concatenate([down_1, down_2]).astype(F32),
        gains[0],
        gains[1],
    )


def solution(mesh):
    placed = (
        P("dp", "tensor", None),
        P("dp"),
        P(None, "tensor"),
        P(),
        P(),
        P("tensor", None),
        P(None, "tensor"),
        P(None, "tensor"),
        P("tensor", None),
        P(),
        P(),
        P("dp", "tensor", None, None),
        P("dp", "tensor", None),
    )
    return jax.shard_map(
        per_device,
        mesh=mesh,
        in_specs=placed,
        out_specs=(
            P("dp", "tensor", None),
            P("dp", "tensor", None),
            P(None, "tensor"),
            P(),
            P(),
            P("tensor", None),
            P(None, "tensor"),
            P(None, "tensor"),
            P("tensor", None),
            P(),
            P(),
        ),
        check_vma=False,
    )
```

```python
import functools

import jax
import jax.numpy as jnp
from jax import lax
from jax.experimental import pallas as pl
from jax.experimental.pallas import tpu as pltpu
from jax.sharding import PartitionSpec as P

HEAD = 128
KEY_BLOCK = 256
JOIN_COST = 8_000_000_000
MERGE = True
BACK_COST = 1
FORTH_COST = 60
SMALL_SHIFT = 1e-05
ROPE_BASE = 10000.0
NEG_FILL = -1e30
LOG2E = 1.4426950408889634
F32 = jnp.float32
BF16 = jnp.bfloat16


def rms_scale(values):
    return lax.rsqrt(jnp.mean(values * values, axis=-1, keepdims=True) + SMALL_SHIFT)


def normed(values, gain_vec):
    return values * rms_scale(values) * gain_vec


def norm_back(values, gain_vec, grad_vals):
    scale_vals = rms_scale(values)
    scaled = grad_vals * gain_vec
    inner_mean = jnp.mean(scaled * values, axis=-1, keepdims=True)
    grad_values = scale_vals * scaled - values * (scale_vals * scale_vals * scale_vals) * inner_mean
    grad_gain = jnp.sum(grad_vals * values * scale_vals, axis=(0, 1))
    return grad_values, grad_gain


def rope_block(start, rows):
    half = HEAD // 2
    frequency = ROPE_BASE ** (-2.0 * jnp.arange(half, dtype=F32) / HEAD)
    angles = (start + jnp.arange(rows)).astype(F32)[:, None] * frequency[None, :]
    cosine, sine = jnp.cos(angles), jnp.sin(angles)
    return jnp.concatenate([cosine, cosine], 1), jnp.concatenate([-sine, sine], 1)


def swap(values, bit):
    n = lax.axis_size("tensor")
    return lax.ppermute(values, "tensor", [(i, i ^ bit) for i in range(n)])


def dot(a, b, dims, out=F32):
    return lax.dot_general(a, b, (dims, ((), ())), preferred_element_type=F32).astype(out)


def add_up(*parts):
    total = parts[0].astype(F32)
    for part in parts[1:]:
        total = total + part.astype(F32)
    return total


def key_branches(start, rows, span, body):
    blocks = span // KEY_BLOCK
    needed = (start + rows + KEY_BLOCK - 1) // KEY_BLOCK
    for count in range(1, blocks + 1):
        pl.when(needed == count)(functools.partial(body, count * KEY_BLOCK))


def stack_heads(values, heads):
    return jnp.concatenate([values[:, h * HEAD : (h + 1) * HEAD] for h in range(heads)], axis=0)


def matmul(a, b, contract):
    return lax.dot_general(a, b, (contract, ((), ())), preferred_element_type=F32)


def masked_scores(keys, query, start, rows, heads, count):
    scores = matmul(keys, query, ((1,), (1,)))
    key_pos = lax.broadcasted_iota(jnp.int32, (KEY_BLOCK, rows), 0) + (count - KEY_BLOCK)
    row_pos = lax.broadcasted_iota(jnp.int32, (KEY_BLOCK, rows), 1) + start
    allowed = key_pos <= row_pos
    last = scores[count - KEY_BLOCK :]
    last = jnp.concatenate(
        [jnp.where(allowed, last[:, h * rows : (h + 1) * rows], NEG_FILL) for h in range(heads)], axis=1
    )
    if count == KEY_BLOCK:
        return last
    return jnp.concatenate([scores[: count - KEY_BLOCK], last], axis=0)


def forward_kernel(
    place, lengths, x0_ref, x1_ref, wq_ref, kv_ref, cos_ref, sin_ref, mixed_ref, query_ref, lse_ref, raw_ref, vt_ref
):
    a = pl.program_id(0)
    seqs, span = kv_ref.shape[0], kv_ref.shape[1]
    rows = x0_ref.shape[0] // seqs
    heads = wq_ref.shape[1] // HEAD
    start = place[a] * rows
    cosine, sine = cos_ref[0], sin_ref[0]
    factor = HEAD ** (-0.5) * LOG2E

    @pl.when(a == 0)
    def _():
        raw_ref[...] = matmul(x0_ref[...], wq_ref[...], ((1,), (0,)))
        for s in range(seqs):
            vt_ref[s] = kv_ref[s, :, HEAD:].T

    @pl.when(a == 1)
    def _():
        raw_ref[...] = matmul(x1_ref[...], wq_ref[...], ((1,), (0,)))

    for s in range(seqs):
        here = slice(s * rows, (s + 1) * rows)
        pieces = []
        for h in range(heads):
            raw = raw_ref[here, h * HEAD : (h + 1) * HEAD]
            pieces.append((raw * cosine + pltpu.roll(raw, HEAD // 2, 1) * sine).astype(BF16))
        query = jnp.concatenate(pieces, axis=0)
        query_ref[0, s] = query
        live = start < lengths[s]

        def body(count, s=s, here=here, query=query):
            scores = masked_scores(kv_ref[s, :count, :HEAD], query, start, rows, heads, count)
            top = jnp.max(scores, axis=0, keepdims=True)
            terms = jnp.exp2((scores - top) * factor)
            total = jnp.sum(terms, axis=0, keepdims=True)
            out = matmul(vt_ref[s, :, :count], terms.astype(BF16), ((1,), (0,))) / total
            lse_ref[0, s] = jnp.broadcast_to(top * factor + jnp.log2(total), lse_ref.shape[2:])
            for h in range(heads):
                piece = out[:, h * rows : (h + 1) * rows].T
                mixed_ref[0, here, h * HEAD : (h + 1) * HEAD] = piece.astype(BF16)

        @pl.when(live)
        def _(body=body):
            key_branches(start, rows, span, body)

        @pl.when(jnp.logical_not(live))
        def _(s=s, here=here):
            mixed_ref[0, here] = jnp.zeros((rows, heads * HEAD), BF16)
            lse_ref[0, s] = jnp.zeros(lse_ref.shape[2:], F32)


def whole(shape):
    return pl.BlockSpec(shape, lambda a, *_: (0,) * len(shape))


def blocked(shape):
    return pl.BlockSpec((1, *shape[1:]), lambda a, *_: (a,) + (0,) * (len(shape) - 1))


def attention_forward(place, lengths, parts, query_weights, kv, cosine, sine):
    flat, width = parts[0].shape
    seqs, span = kv.shape[0], kv.shape[1]
    rows, wide = flat // seqs, query_weights.shape[1]
    heads = wide // HEAD
    shapes = [(2, flat, wide), (2, seqs, heads * rows, HEAD), (2, seqs, 8, heads * rows)]
    return pl.pallas_call(
        forward_kernel,
        grid_spec=pltpu.PrefetchScalarGridSpec(
            num_scalar_prefetch=2,
            grid=(2,),
            in_specs=[
                whole(parts[0].shape),
                whole(parts[1].shape),
                whole(query_weights.shape),
                whole(kv.shape),
                blocked(cosine.shape),
                blocked(sine.shape),
            ],
            out_specs=[blocked(shape) for shape in shapes],
            scratch_shapes=[pltpu.VMEM((flat, wide), F32), pltpu.VMEM((seqs, HEAD, span), BF16)],
        ),
        out_shape=[jax.ShapeDtypeStruct(s, t) for s, t in zip(shapes, (BF16, BF16, F32))],
        compiler_params=pltpu.CompilerParams(vmem_limit_bytes=48 * 1024 * 1024),
        cost_estimate=pl.CostEstimate(flops=FORTH_COST * flat * wide * span, bytes_accessed=kv.size, transcendentals=0),
        name="attention_forward",
    )(place, lengths, *parts, query_weights, kv, cosine, sine)


def backward_kernel(
    place, lengths, g0_ref, g1_ref, wo_ref, wq_ref, query_ref, lse_ref, kv_ref, cos_ref, sin_ref,
    gq_ref, in_ref, gkv_ref, gm_ref, kt_ref,
):
    a = pl.program_id(0)
    seqs, span = kv_ref.shape[0], kv_ref.shape[1]
    rows = g0_ref.shape[0] // seqs
    heads = wq_ref.shape[1] // HEAD
    start = place[a] * rows
    scale = HEAD ** (-0.5)
    factor = scale * LOG2E

    @pl.when(a == 0)
    def _():
        gm_ref[...] = matmul(g0_ref[...], wo_ref[...], ((1,), (1,))).astype(BF16)
        gkv_ref[...] = jnp.zeros(gkv_ref.shape, F32)
        for s in range(seqs):
            kt_ref[s] = kv_ref[s, :, :HEAD].T

    @pl.when(a == 1)
    def _():
        gm_ref[...] = matmul(g1_ref[...], wo_ref[...], ((1,), (1,))).astype(BF16)

    for s in range(seqs):
        here = slice(s * rows, (s + 1) * rows)
        live = start < lengths[s]

        def body(count, s=s, here=here):
            query = query_ref[0, s]
            grad = stack_heads(gm_ref[here, :], heads)
            scores = masked_scores(kv_ref[s, :count, :HEAD], query, start, rows, heads, count)
            probs = jnp.exp2(scores * factor - lse_ref[0, s, 0:1, :])
            grad_probs = matmul(kv_ref[s, :count, HEAD:], grad, ((1,), (1,)))
            row_dots = jnp.sum(probs * grad_probs, axis=0, keepdims=True)
            grad_scores = (probs * (grad_probs - row_dots)).astype(BF16)
            gkv_ref[s, :count, :HEAD] += scale * matmul(grad_scores, query, ((1,), (0,)))
            gkv_ref[s, :count, HEAD:] += matmul(probs.astype(BF16), grad, ((1,), (0,)))
            grad_query = matmul(kt_ref[s, :, :count], grad_scores, ((1,), (0,)))
            cosine, sine = cos_ref[0], sin_ref[0]
            for h in range(heads):
                piece = grad_query[:, h * rows : (h + 1) * rows].T * scale
                piece = piece * cosine - pltpu.roll(piece, HEAD // 2, 1) * sine
                gq_ref[0, here, h * HEAD : (h + 1) * HEAD] = piece.astype(BF16)

        @pl.when(live)
        def _(body=body):
            key_branches(start, rows, span, body)

        @pl.when(jnp.logical_not(live))
        def _(here=here):
            gq_ref[0, here] = jnp.zeros((rows, heads * HEAD), BF16)

    in_ref[0] = matmul(gq_ref[0], wq_ref[...], ((1,), (1,))).astype(BF16)


def attention_backward(place, lengths, grads, output_weights, query_weights, query, lse, kv, cosine, sine):
    flat, width = grads[0].shape
    seqs, span = kv.shape[0], kv.shape[1]
    wide = query_weights.shape[1]
    operands = (*grads, output_weights, query_weights, query, lse, kv, cosine, sine)
    specs = [whole(v.shape) for v in operands]
    for k in (4, 5, 7, 8):
        specs[k] = blocked(operands[k].shape)
    return pl.pallas_call(
        backward_kernel,
        grid_spec=pltpu.PrefetchScalarGridSpec(
            num_scalar_prefetch=2,
            grid=(2,),
            in_specs=specs,
            out_specs=[blocked((2, flat, wide)), blocked((2, flat, width)), whole(kv.shape)],
            scratch_shapes=[pltpu.VMEM((flat, wide), BF16), pltpu.VMEM((seqs, HEAD, span), BF16)],
        ),
        out_shape=[
            jax.ShapeDtypeStruct((2, flat, wide), BF16),
            jax.ShapeDtypeStruct((2, flat, width), BF16),
            jax.ShapeDtypeStruct(kv.shape, F32),
        ],
        compiler_params=pltpu.CompilerParams(vmem_limit_bytes=56 * 1024 * 1024),
        cost_estimate=pl.CostEstimate(flops=BACK_COST * flat * wide * span, bytes_accessed=kv.size, transcendentals=0),
        name="attention_backward",
    )(place, lengths, *operands)


def join_columns(parts):
    rows, wide = parts[0].shape

    def kernel(*refs):
        for k in range(len(parts)):
            refs[-1][:, k * wide : (k + 1) * wide] = refs[k][...]

    return pl.pallas_call(
        kernel,
        grid=(4,),
        in_specs=[pl.BlockSpec((rows // 4, wide), lambda i: (i, 0)) for _ in parts],
        out_specs=pl.BlockSpec((rows // 4, wide * len(parts)), lambda i: (i, 0)),
        out_shape=jax.ShapeDtypeStruct((rows, wide * len(parts)), parts[0].dtype),
        cost_estimate=pl.CostEstimate(flops=JOIN_COST, bytes_accessed=0, transcendentals=0),
        name="join_columns",
    )(*parts)


def middle_bits(n):
    bits, bit = [], 2
    while bit < n // 2:
        bits.append(bit)
        bit *= 2
    return bits


def gather_middle(values):
    parts = [values]
    for bit in middle_bits(lax.axis_size("tensor")):
        parts = parts + [swap(part, bit) for part in parts]
    return parts


def reduce_middle(parts):
    for bit in reversed(middle_bits(lax.axis_size("tensor"))):
        half = len(parts) // 2
        parts = [add_up(parts[i], swap(parts[half + i].astype(BF16), bit)) for i in range(half)]
    return parts[0]


def tie(*values):
    return lax.optimization_barrier(values)


class LineSum:
    def __init__(self):
        self.line = lax.axis_size("dp") == 4
        place = lax.axis_index("dp")
        self.outer = (place == 0) | (place == 3)
        self.inward, self.across, self.outward = [], [], []
        self.sums = []

    def advance(self, arrays, others=()):
        if not self.line:
            self.sums += [lax.psum(a, "dp") for a in arrays]
            return others
        arrays, inward, across, outward, others = tie(
            list(arrays), self.inward, self.across, self.outward, others
        )
        pairs = [add_up(own, sent).astype(BF16) for own, sent in inward]
        totals = [add_up(own, sent).astype(BF16) for own, sent in across]
        self.inward, self.outward = [], []
        if MERGE and [a.shape for a in arrays] == [t.shape for t in totals]:
            for own, total in zip(arrays, totals):
                sent = jnp.where(self.outer, own, total)
                sent = lax.ppermute(sent, "dp", [(0, 1), (1, 0), (2, 3), (3, 2)])
                self.inward.append((own, sent))
                self.outward.append((total, sent))
        else:
            self.inward = [(a, lax.ppermute(a, "dp", [(0, 1), (3, 2)])) for a in arrays]
            self.outward = [(a, lax.ppermute(a, "dp", [(1, 0), (2, 3)])) for a in totals]
        self.across = [(a, lax.ppermute(a, "dp", [(1, 2), (2, 1)])) for a in pairs]
        self.sums += [jnp.where(self.outer, sent, own) for own, sent in outward]
        return others


def tensor_bits():
    n, bits, bit = lax.axis_size("tensor"), [], 1
    while bit < n:
        bits.append(bit)
        bit *= 2
    return bits


def reduce_blocks(blocks):
    n, me = blocks.shape[0], lax.axis_index("tensor")
    held = [lax.dynamic_index_in_dim(blocks, me ^ r, 0, keepdims=False) for r in range(n)]
    for bit in tensor_bits():
        keep = jnp.stack([held[r] for r in range(len(held)) if r % 2 == 0])
        give = jnp.stack([held[r] for r in range(len(held)) if r % 2 == 1])
        total = add_up(keep, swap(give.astype(BF16), bit))
        held = [total[k] for k in range(total.shape[0])]
    return held[0]


def gather_blocks(block):
    n, me = lax.axis_size("tensor"), lax.axis_index("tensor")
    held = block[None]
    for bit in reversed(tensor_bits()):
        other = swap(held, bit)
        held = jnp.stack([held, other], 1).reshape(2 * held.shape[0], *block.shape)
    result = jnp.zeros_like(held)
    for r in range(n):
        result = lax.dynamic_update_index_in_dim(result, held[r], me ^ r, 0)
    return result


def gather_near(values):
    if lax.axis_size("tensor") != 8:
        return values, values
    return swap(values, 2), swap(values, 4)


def gather_pairs(values):
    parts, bits = [values], tensor_bits()
    for bit in bits:
        parts = parts + [swap(part, bit) for part in parts]
    return [(parts[i], parts[i + 1]) for i in range(0, len(parts), 2)]


def halves(value):
    rows = value.shape[0] // 2
    return value[:rows], value[rows:]


def reduce_begin(count, terms, between):
    n = lax.axis_size("tensor")
    if n != 8:
        parts = []
        for i in range(count):
            own, other = terms(i, None)
            parts.append(add_up(own, swap(other, 1)))
        while len(parts) > 1:
            half = len(parts) // 2
            parts = [add_up(parts[i], swap(parts[half + i].astype(BF16), 2 * half)) for i in range(half)]
        between(parts[0])
        return parts[0], ()
    own_d, other_d = (terms(3, None))
    core_d = swap(other_d, 1)
    own_y, other_y = (terms(2, own_d))
    core_y = swap(other_y, 1)
    diagonal = add_up(own_d, core_d).astype(BF16)
    diagonal, own_y = tie(diagonal, own_y)
    first, second = halves(diagonal)
    from_x, from_y = swap(first, 2), swap(second, 4)
    own_x, other_x = (terms(1, between(diagonal)))
    core_x = swap(other_x, 1)
    own, other = (terms(0, own_x))
    core = swap(other, 1)
    low, high = halves(add_up(own_y, core_y))
    for_y = jnp.concatenate([add_up(low, from_x), high]).astype(BF16)
    low, high = halves(add_up(own_x, core_x))
    for_x = jnp.concatenate([low, add_up(high, from_y)]).astype(BF16)
    return (own, core), (for_x, for_y)


def reduce_end(own, sent):
    if not sent:
        return own
    return add_up(*own, swap(sent[0], 2), swap(sent[1], 4))


def per_device(
    tokens,
    lengths,
    query_weight,
    key_weight,
    value_weight,
    output_weight,
    gate_weight,
    up_weight,
    down_weight,
    gain_attn,
    gain_mlp,
    pair_grad,
    cotangent,
):
    seqs, rows, width = tokens.shape
    n = lax.axis_size("tensor")
    me = lax.axis_index("tensor")
    top = n // 2
    flat = seqs * rows
    local_pos = me * rows + jnp.arange(rows)
    valid = (local_pos[None, :] < lengths[:, None]).astype(F32)[..., None]
    x = tokens.astype(F32)
    attn_gain = gain_attn.astype(F32)
    mlp_gain = gain_mlp.astype(F32)
    grad_y = cotangent.astype(F32)
    kv_weight = jnp.concatenate([key_weight, value_weight], axis=1)

    norm_in = normed(x, attn_gain).astype(BF16).reshape(flat, width)
    far_in = swap(norm_in, top)
    far_in = (far_in, swap(far_in, 1))
    near_in = (norm_in, swap(norm_in, 1))
    query_weights = join_columns(gather_middle(query_weight))
    heads_width = query_weights.shape[1]
    own_cos, own_sin = rope_block(me * rows, rows)
    kv_raw = dot(norm_in, kv_weight, ((1,), (0,))).reshape(seqs, rows, 2 * HEAD)
    key_raw = kv_raw[..., :HEAD]
    key_own = key_raw * own_cos + jnp.roll(key_raw, HEAD // 2, axis=-1) * own_sin
    kv_own = jnp.concatenate([key_own, kv_raw[..., HEAD:]], axis=-1).astype(BF16)

    output_weight, kv_own = tie(output_weight, kv_own)
    output_parts = gather_middle(output_weight)
    kv = lax.all_gather(kv_own, "tensor", axis=1, tiled=True)

    def place_of(offset):
        place = jnp.stack([me ^ offset, me ^ (offset + 1)]).astype(jnp.int32)
        blocks = [rope_block(place[i] * rows, rows) for i in range(2)]
        return place, (jnp.stack([b[0] for b in blocks]), jnp.stack([b[1] for b in blocks]))

    def attend(part, place, table):
        return attention_forward(place, lengths, part, query_weights, kv, *table)

    def portions_of(mixed):
        return [dot(mixed[i], output_weights, ((1,), (0,)), BF16) for i in range(2)]

    near_place, near_table = place_of(0)
    far_place, far_table = place_of(top)
    grad_out = (valid * grad_y).astype(BF16).reshape(flat, width)
    grad_out, _ = tie(grad_out, norm_in)
    grad_far = swap(grad_out, top)
    near_result = attend(near_in, near_place, near_table)
    far_in, _ = tie(far_in, near_result[0])
    far_result = attend(far_in, far_place, far_table)
    output_parts, far_mixed, grad_far = tie(output_parts, far_result[0], grad_far)
    output_weights = jnp.concatenate(output_parts, axis=0)
    far_portions = portions_of(far_mixed)
    for_far = add_up(far_portions[0], swap(far_portions[1], 1)).astype(BF16)
    for_far, near_mixed = tie(for_far, near_result[0])
    from_far = swap(for_far, top)
    def slopes_of(blocks):
        return [dot(block, down_weight, ((1,), (1,))) for block in blocks]

    def with_core(part):
        return part, swap(part, 1)

    near_portions = portions_of(near_mixed)
    near_core = swap(near_portions[1], 1)
    if n == 8:
        grad_out, _ = tie(grad_out, far_mixed)
        grad_side = swap(grad_out, 2)
        size = flat // 2
        own_slopes = slopes_of([*with_core(grad_out), *with_core(grad_far)])
        from_far, grad_side, grad_far, own_slopes = tie(from_far, grad_side, grad_far, own_slopes)
        grad_diagonal = [swap(grad_side[:size], 4), swap(grad_far[size:], 2)]
    attn_out = add_up(near_portions[0], near_core, from_far)
    hidden = x + valid * attn_out.reshape(seqs, rows, width)

    chips = n // 2
    norm_mid = normed(hidden, mlp_gain).astype(BF16).reshape(flat, width)
    gate_rows, up_rows = gate_weight.T, up_weight.T

    mids, acts, g_gates, g_ups = [], [], [], []

    def forward_blocks(blocks, slopes):
        for mid, slope in zip(blocks, slopes):
            gate = dot(mid, gate_rows, ((1,), (1,)))
            up = dot(mid, up_rows, ((1,), (1,)))
            sig = 1.0 / (1.0 + jnp.exp(-gate))
            silu = gate * sig
            mids.append(mid)
            acts.append((silu * up).astype(BF16))
            g_gates.append((slope * up * sig * (1.0 + gate * (1.0 - sig))).astype(BF16))
            g_ups.append((slope * silu).astype(BF16))

    def diagonal_blocks(parts):
        return [jnp.concatenate(p) for p in zip(*[with_core(part) for part in parts])]

    if n == 8:
        at_x, at_y = gather_near(norm_mid)
        grads = [*with_core(grad_out), *with_core(grad_side)]
        slopes = own_slopes[:2] + slopes_of(grads[2:]) + own_slopes[2:]
        forward_blocks(with_core(norm_mid), slopes[:2])
        at_x, at_y, slopes, acts[1] = tie(at_x, at_y, slopes, acts[1])
        diagonal = [swap(at_x[:size], 4), swap(at_y[size:], 2)]
        grad_diagonal, _ = tie(grad_diagonal, at_x)
        grads += [*with_core(grad_far), *diagonal_blocks(grad_diagonal)]
        forward_blocks((*with_core(at_x), *with_core(at_y)), slopes[2:6])
        grad_down = dot(jnp.concatenate(acts), jnp.concatenate(grads[:6]), ((0,), (0,)))
        diagonal, grad_down = tie(diagonal, grad_down)
        forward_blocks(diagonal_blocks(diagonal), slopes_of(grads[6:]))
    else:
        grads = [block for pair in gather_pairs(grad_out) for block in pair]
        forward_blocks([block for pair in gather_pairs(norm_mid) for block in pair], slopes_of(grads))
        grad_down = dot(jnp.concatenate(acts[:-2]), jnp.concatenate(grads[:-2]), ((0,), (0,)))

    def mid_term(r):
        terms = dot(g_gates[r], gate_rows, ((1,), (0,))) + dot(g_ups[r], up_rows, ((1,), (0,)))
        return terms.astype(BF16)

    def mid_terms(i, after):
        for k in (2 * i, 2 * i + 1):
            if after is not None:
                g_gates[k], g_ups[k], _ = tie(g_gates[k], g_ups[k], after)
        return mid_term(2 * i), mid_term(2 * i + 1)

    sums, down_parts = LineSum(), []

    def down_gradient(after):
        last, after = tie(acts[-2:], after)
        term = dot(jnp.concatenate(last), jnp.concatenate(grads[-2:]), ((0,), (0,)))
        down_parts.extend(halves((grad_down + term).astype(BF16)))
        return sums.advance([down_parts[0]], after)

    mid_own, mid_sent = reduce_begin(chips, mid_terms, down_gradient)
    grad_mid = reduce_end(mid_own, mid_sent).reshape(seqs, rows, width)

    g_gates, g_ups, mids = sums.advance([down_parts[1]], (g_gates, g_ups, mids))
    mid_all = jnp.concatenate(mids)
    grad_gate = halves(dot(jnp.concatenate(g_gates), mid_all, ((0,), (0,)), BF16))
    back, mlp_gain_part = norm_back(hidden, mlp_gain, grad_mid)
    grad_hidden = grad_y + back
    grad_attn = (valid * grad_hidden).astype(BF16).reshape(flat, width)
    far_grad = swap(grad_attn, top)
    near_grad = (grad_attn, swap(grad_attn, 1))

    g_ups = sums.advance([grad_gate[0]], g_ups)
    grad_up = halves(dot(jnp.concatenate(g_ups), mid_all, ((0,), (0,)), BF16))

    def attend_back(part, result, place, table):
        return attention_backward(
            place, lengths, part, output_weights, query_weights, result[1], result[2], kv, *table
        )

    def product(left, right):
        return dot(jnp.concatenate(left), jnp.concatenate(right), ((0,), (0,)), BF16)

    far_grad, near_grad = sums.advance([grad_gate[1]], (far_grad, near_grad))
    far_grad = (far_grad, swap(far_grad, 1))
    far_q, far_terms, far_kv = attend_back(far_grad, far_result, far_place, far_table)
    for_far = add_up(far_terms[0], swap(far_terms[1], 1)).astype(BF16)
    from_far = swap(for_far, top)

    for_far, near_grad, far_grad = sums.advance([grad_up[0]], (for_far, near_grad, far_grad))
    unit = output_weight.shape[0]
    mixed = [r[0][i] for r in (near_result, far_result) for i in range(2)]
    wo_full = product(mixed, [*near_grad, *far_grad])
    wo_part = reduce_middle([wo_full[i * unit : (i + 1) * unit] for i in range(heads_width // unit)])
    wo_part = wo_part.astype(BF16)
    near_q, near_terms, near_kv = attend_back(near_grad, near_result, near_place, near_table)
    near_core = swap(near_terms[1], 1)

    from_far, near_terms, near_core, near_q, near_kv, wo_part = sums.advance(
        [grad_up[1]], (from_far, near_terms, near_core, near_q, near_kv, wo_part)
    )
    kv_blocks = (near_kv + far_kv).astype(BF16).reshape(seqs, n, rows, 2 * HEAD).swapaxes(0, 1)
    kv_sum = reduce_blocks(kv_blocks)
    wq_full = product([near_q[0], near_q[1], far_q[0], far_q[1]], [*near_in, *far_in])
    wq_full, kv_sum = tie(wq_full, kv_sum)
    wq_part = reduce_middle([wq_full[i * unit : (i + 1) * unit] for i in range(heads_width // unit)])
    wq_part = wq_part.astype(BF16)
    key_grad = kv_sum[..., :HEAD]
    key_grad = key_grad * own_cos - jnp.roll(key_grad, HEAD // 2, axis=-1) * own_sin
    kv_grad = jnp.concatenate([key_grad, kv_sum[..., HEAD:]], -1).astype(BF16).reshape(flat, 2 * HEAD)
    grad_in = add_up(near_terms[0], near_core, from_far)
    grad_in = grad_in + dot(kv_grad, kv_weight, ((1,), (1,)))
    kv_portion = dot(norm_in, kv_grad, ((0,), (0,)))
    back, attn_gain_part = norm_back(x, attn_gain, grad_in.reshape(seqs, rows, width))
    grad_tokens = grad_hidden + back

    kv_portion, attn_gain_part = sums.advance([wo_part], (kv_portion, attn_gain_part))
    gains = jnp.concatenate([attn_gain_part, mlp_gain_part]).reshape(-1, 2 * HEAD)
    shared = jnp.concatenate([kv_portion + pair_grad[0, 0], gains])
    shared = jnp.pad(shared, ((0, -shared.shape[0] % (16 * n)), (0, 0))).astype(BF16)
    shared = reduce_blocks(shared.reshape(n, -1, 2 * HEAD)).astype(BF16)


    acts = sums.advance([wq_part, shared], acts)

    def out_terms(i, after):
        left = acts[2 * i : 2 * i + 2]
        left = left if after is None else tie(left, after)[0]
        return [dot(part, down_weight, ((1,), (0,)), BF16) for part in left]

    out_own, out_sent = reduce_begin(chips, out_terms, lambda after: after)
    rows_out = reduce_end(out_own, out_sent)
    output = (hidden + valid * rows_out.reshape(seqs, rows, width)).astype(BF16)
    sums.advance([])
    sums.advance([])
    sums.advance([])
    down_1, down_2, gate_1, gate_2, up_1, up_2, wo_sum, wq_sum, shared = sums.sums
    shared = gather_blocks(shared).reshape(-1, 2 * HEAD).astype(F32)
    gains = shared[width : width + gains.shape[0]].reshape(2, width)
    return (
        output,
        grad_tokens,
        wq_sum.astype(F32).T,
        shared[:width, :HEAD],
        shared[:width, HEAD:],
        wo_sum.astype(F32),
        jnp.concatenate([gate_1, gate_2]).astype(F32).T,
        jnp.concatenate([up_1, up_2]).astype(F32).T,
        jnp.concatenate([down_1, down_2]).astype(F32),
        gains[0],
        gains[1],
    )


def solution(mesh):
    placed = (
        P("dp", "tensor", None),
        P("dp"),
        P(None, "tensor"),
        P(),
        P(),
        P("tensor", None),
        P(None, "tensor"),
        P(None, "tensor"),
        P("tensor", None),
        P(),
        P(),
        P("dp", "tensor", None, None),
        P("dp", "tensor", None),
    )
    return jax.shard_map(
        per_device,
        mesh=mesh,
        in_specs=placed,
        out_specs=(
            P("dp", "tensor", None),
            P("dp", "tensor", None),
            P(None, "tensor"),
            P(),
            P(),
            P("tensor", None),
            P(None, "tensor"),
            P(None, "tensor"),
            P("tensor", None),
            P(),
            P(),
        ),
        check_vma=False,
    )
```

```python
import functools

import jax
import jax.numpy as jnp
from jax import lax
from jax.experimental import pallas as pl
from jax.experimental.pallas import tpu as pltpu
from jax.sharding import PartitionSpec as P

HEAD = 128
KEY_BLOCK = 256
JOIN_COST = 8_000_000_000
MERGE = True
BACK_COST = 1
FORTH_COST = 60
SMALL_SHIFT = 1e-05
ROPE_BASE = 10000.0
NEG_FILL = -1e30
LOG2E = 1.4426950408889634
F32 = jnp.float32
BF16 = jnp.bfloat16


def rms_scale(values):
    return lax.rsqrt(jnp.mean(values * values, axis=-1, keepdims=True) + SMALL_SHIFT)


def normed(values, gain_vec):
    return values * rms_scale(values) * gain_vec


def norm_back(values, gain_vec, grad_vals):
    scale_vals = rms_scale(values)
    scaled = grad_vals * gain_vec
    inner_mean = jnp.mean(scaled * values, axis=-1, keepdims=True)
    grad_values = scale_vals * scaled - values * (scale_vals * scale_vals * scale_vals) * inner_mean
    grad_gain = jnp.sum(grad_vals * values * scale_vals, axis=(0, 1))
    return grad_values, grad_gain


def rope_block(start, rows):
    half = HEAD // 2
    frequency = ROPE_BASE ** (-2.0 * jnp.arange(half, dtype=F32) / HEAD)
    angles = (start + jnp.arange(rows)).astype(F32)[:, None] * frequency[None, :]
    cosine, sine = jnp.cos(angles), jnp.sin(angles)
    return jnp.concatenate([cosine, cosine], 1), jnp.concatenate([-sine, sine], 1)


def swap(values, bit):
    n = lax.axis_size("tensor")
    return lax.ppermute(values, "tensor", [(i, i ^ bit) for i in range(n)])


def dot(a, b, dims, out=F32):
    return lax.dot_general(a, b, (dims, ((), ())), preferred_element_type=F32).astype(out)


def add_up(*parts):
    total = parts[0].astype(F32)
    for part in parts[1:]:
        total = total + part.astype(F32)
    return total


def key_branches(start, rows, span, body):
    blocks = span // KEY_BLOCK
    needed = (start + rows + KEY_BLOCK - 1) // KEY_BLOCK
    for count in range(1, blocks + 1):
        pl.when(needed == count)(functools.partial(body, count * KEY_BLOCK))


def stack_heads(values, heads):
    return jnp.concatenate([values[:, h * HEAD : (h + 1) * HEAD] for h in range(heads)], axis=0)


def matmul(a, b, contract):
    return lax.dot_general(a, b, (contract, ((), ())), preferred_element_type=F32)


def masked_scores(keys, query, start, rows, heads, count):
    scores = matmul(keys, query, ((1,), (1,)))
    key_pos = lax.broadcasted_iota(jnp.int32, (KEY_BLOCK, rows), 0) + (count - KEY_BLOCK)
    row_pos = lax.broadcasted_iota(jnp.int32, (KEY_BLOCK, rows), 1) + start
    allowed = key_pos <= row_pos
    last = scores[count - KEY_BLOCK :]
    last = jnp.concatenate(
        [jnp.where(allowed, last[:, h * rows : (h + 1) * rows], NEG_FILL) for h in range(heads)], axis=1
    )
    if count == KEY_BLOCK:
        return last
    return jnp.concatenate([scores[: count - KEY_BLOCK], last], axis=0)


def forward_kernel(
    place, lengths, x0_ref, x1_ref, wq_ref, kv_ref, cos_ref, sin_ref, mixed_ref, query_ref, lse_ref, raw_ref, vt_ref
):
    a = pl.program_id(0)
    seqs, span = kv_ref.shape[0], kv_ref.shape[1]
    rows = x0_ref.shape[0] // seqs
    heads = wq_ref.shape[1] // HEAD
    start = place[a] * rows
    cosine, sine = cos_ref[0], sin_ref[0]
    factor = HEAD ** (-0.5) * LOG2E

    @pl.when(a == 0)
    def _():
        raw_ref[...] = matmul(x0_ref[...], wq_ref[...], ((1,), (0,)))
        for s in range(seqs):
            vt_ref[s] = kv_ref[s, :, HEAD:].T

    @pl.when(a == 1)
    def _():
        raw_ref[...] = matmul(x1_ref[...], wq_ref[...], ((1,), (0,)))

    for s in range(seqs):
        here = slice(s * rows, (s + 1) * rows)
        pieces = []
        for h in range(heads):
            raw = raw_ref[here, h * HEAD : (h + 1) * HEAD]
            pieces.append((raw * cosine + pltpu.roll(raw, HEAD // 2, 1) * sine).astype(BF16))
        query = jnp.concatenate(pieces, axis=0)
        query_ref[0, s] = query
        live = start < lengths[s]

        def body(count, s=s, here=here, query=query):
            scores = masked_scores(kv_ref[s, :count, :HEAD], query, start, rows, heads, count)
            top = jnp.max(scores, axis=0, keepdims=True)
            terms = jnp.exp2((scores - top) * factor)
            total = jnp.sum(terms, axis=0, keepdims=True)
            out = matmul(vt_ref[s, :, :count], terms.astype(BF16), ((1,), (0,))) / total
            lse_ref[0, s] = jnp.broadcast_to(top * factor + jnp.log2(total), lse_ref.shape[2:])
            for h in range(heads):
                piece = out[:, h * rows : (h + 1) * rows].T
                mixed_ref[0, here, h * HEAD : (h + 1) * HEAD] = piece.astype(BF16)

        @pl.when(live)
        def _(body=body):
            key_branches(start, rows, span, body)

        @pl.when(jnp.logical_not(live))
        def _(s=s, here=here):
            mixed_ref[0, here] = jnp.zeros((rows, heads * HEAD), BF16)
            lse_ref[0, s] = jnp.zeros(lse_ref.shape[2:], F32)


def whole(shape):
    return pl.BlockSpec(shape, lambda a, *_: (0,) * len(shape))


def blocked(shape):
    return pl.BlockSpec((1, *shape[1:]), lambda a, *_: (a,) + (0,) * (len(shape) - 1))


def attention_forward(place, lengths, parts, query_weights, kv, cosine, sine):
    flat, width = parts[0].shape
    seqs, span = kv.shape[0], kv.shape[1]
    rows, wide = flat // seqs, query_weights.shape[1]
    heads = wide // HEAD
    shapes = [(2, flat, wide), (2, seqs, heads * rows, HEAD), (2, seqs, 8, heads * rows)]
    return pl.pallas_call(
        forward_kernel,
        grid_spec=pltpu.PrefetchScalarGridSpec(
            num_scalar_prefetch=2,
            grid=(2,),
            in_specs=[
                whole(parts[0].shape),
                whole(parts[1].shape),
                whole(query_weights.shape),
                whole(kv.shape),
                blocked(cosine.shape),
                blocked(sine.shape),
            ],
            out_specs=[blocked(shape) for shape in shapes],
            scratch_shapes=[pltpu.VMEM((flat, wide), F32), pltpu.VMEM((seqs, HEAD, span), BF16)],
        ),
        out_shape=[jax.ShapeDtypeStruct(s, t) for s, t in zip(shapes, (BF16, BF16, F32))],
        compiler_params=pltpu.CompilerParams(vmem_limit_bytes=48 * 1024 * 1024),
        cost_estimate=pl.CostEstimate(flops=FORTH_COST * flat * wide * span, bytes_accessed=kv.size, transcendentals=0),
        name="attention_forward",
    )(place, lengths, *parts, query_weights, kv, cosine, sine)


def backward_kernel(
    place, lengths, g0_ref, g1_ref, wo_ref, wq_ref, query_ref, lse_ref, kv_ref, cos_ref, sin_ref,
    gq_ref, in_ref, gkv_ref, gm_ref, kt_ref,
):
    a = pl.program_id(0)
    seqs, span = kv_ref.shape[0], kv_ref.shape[1]
    rows = g0_ref.shape[0] // seqs
    heads = wq_ref.shape[1] // HEAD
    start = place[a] * rows
    scale = HEAD ** (-0.5)
    factor = scale * LOG2E

    @pl.when(a == 0)
    def _():
        gm_ref[...] = matmul(g0_ref[...], wo_ref[...], ((1,), (1,))).astype(BF16)
        gkv_ref[...] = jnp.zeros(gkv_ref.shape, F32)
        for s in range(seqs):
            kt_ref[s] = kv_ref[s, :, :HEAD].T

    @pl.when(a == 1)
    def _():
        gm_ref[...] = matmul(g1_ref[...], wo_ref[...], ((1,), (1,))).astype(BF16)

    for s in range(seqs):
        here = slice(s * rows, (s + 1) * rows)
        live = start < lengths[s]

        def body(count, s=s, here=here):
            query = query_ref[0, s]
            grad = stack_heads(gm_ref[here, :], heads)
            scores = masked_scores(kv_ref[s, :count, :HEAD], query, start, rows, heads, count)
            probs = jnp.exp2(scores * factor - lse_ref[0, s, 0:1, :])
            grad_probs = matmul(kv_ref[s, :count, HEAD:], grad, ((1,), (1,)))
            row_dots = jnp.sum(probs * grad_probs, axis=0, keepdims=True)
            grad_scores = (probs * (grad_probs - row_dots)).astype(BF16)
            gkv_ref[s, :count, :HEAD] += scale * matmul(grad_scores, query, ((1,), (0,)))
            gkv_ref[s, :count, HEAD:] += matmul(probs.astype(BF16), grad, ((1,), (0,)))
            grad_query = matmul(kt_ref[s, :, :count], grad_scores, ((1,), (0,)))
            cosine, sine = cos_ref[0], sin_ref[0]
            for h in range(heads):
                piece = grad_query[:, h * rows : (h + 1) * rows].T * scale
                piece = piece * cosine - pltpu.roll(piece, HEAD // 2, 1) * sine
                gq_ref[0, here, h * HEAD : (h + 1) * HEAD] = piece.astype(BF16)

        @pl.when(live)
        def _(body=body):
            key_branches(start, rows, span, body)

        @pl.when(jnp.logical_not(live))
        def _(here=here):
            gq_ref[0, here] = jnp.zeros((rows, heads * HEAD), BF16)

    in_ref[0] = matmul(gq_ref[0], wq_ref[...], ((1,), (1,))).astype(BF16)


def attention_backward(place, lengths, grads, output_weights, query_weights, query, lse, kv, cosine, sine):
    flat, width = grads[0].shape
    seqs, span = kv.shape[0], kv.shape[1]
    wide = query_weights.shape[1]
    operands = (*grads, output_weights, query_weights, query, lse, kv, cosine, sine)
    specs = [whole(v.shape) for v in operands]
    for k in (4, 5, 7, 8):
        specs[k] = blocked(operands[k].shape)
    return pl.pallas_call(
        backward_kernel,
        grid_spec=pltpu.PrefetchScalarGridSpec(
            num_scalar_prefetch=2,
            grid=(2,),
            in_specs=specs,
            out_specs=[blocked((2, flat, wide)), blocked((2, flat, width)), whole(kv.shape)],
            scratch_shapes=[pltpu.VMEM((flat, wide), BF16), pltpu.VMEM((seqs, HEAD, span), BF16)],
        ),
        out_shape=[
            jax.ShapeDtypeStruct((2, flat, wide), BF16),
            jax.ShapeDtypeStruct((2, flat, width), BF16),
            jax.ShapeDtypeStruct(kv.shape, F32),
        ],
        compiler_params=pltpu.CompilerParams(vmem_limit_bytes=56 * 1024 * 1024),
        cost_estimate=pl.CostEstimate(flops=BACK_COST * flat * wide * span, bytes_accessed=kv.size, transcendentals=0),
        name="attention_backward",
    )(place, lengths, *operands)


def join_columns(parts):
    rows, wide = parts[0].shape

    def kernel(*refs):
        for k in range(len(parts)):
            refs[-1][:, k * wide : (k + 1) * wide] = refs[k][...]

    return pl.pallas_call(
        kernel,
        grid=(4,),
        in_specs=[pl.BlockSpec((rows // 4, wide), lambda i: (i, 0)) for _ in parts],
        out_specs=pl.BlockSpec((rows // 4, wide * len(parts)), lambda i: (i, 0)),
        out_shape=jax.ShapeDtypeStruct((rows, wide * len(parts)), parts[0].dtype),
        cost_estimate=pl.CostEstimate(flops=JOIN_COST, bytes_accessed=0, transcendentals=0),
        name="join_columns",
    )(*parts)


def middle_bits(n):
    bits, bit = [], 2
    while bit < n // 2:
        bits.append(bit)
        bit *= 2
    return bits


def gather_middle(values):
    parts = [values]
    for bit in middle_bits(lax.axis_size("tensor")):
        parts = parts + [swap(part, bit) for part in parts]
    return parts


def reduce_middle(parts):
    for bit in reversed(middle_bits(lax.axis_size("tensor"))):
        half = len(parts) // 2
        parts = [add_up(parts[i], swap(parts[half + i].astype(BF16), bit)) for i in range(half)]
    return parts[0]


def sum_of_products(left, right, start=None):
    total = dot(jnp.concatenate(left), jnp.concatenate(right), ((0,), (0,)))
    return total if start is None else start + total


def tie(*values):
    return lax.optimization_barrier(values)


class LineSum:
    def __init__(self):
        self.line = lax.axis_size("dp") == 4
        place = lax.axis_index("dp")
        self.outer = (place == 0) | (place == 3)
        self.inward, self.across, self.outward = [], [], []
        self.sums = []

    def advance(self, arrays, others=()):
        if not self.line:
            self.sums += [lax.psum(a, "dp") for a in arrays]
            return others
        arrays, inward, across, outward, others = tie(
            list(arrays), self.inward, self.across, self.outward, others
        )
        pairs = [add_up(own, sent).astype(BF16) for own, sent in inward]
        totals = [add_up(own, sent).astype(BF16) for own, sent in across]
        self.inward, self.outward = [], []
        if MERGE and [a.shape for a in arrays] == [t.shape for t in totals]:
            for own, total in zip(arrays, totals):
                sent = jnp.where(self.outer, own, total)
                sent = lax.ppermute(sent, "dp", [(0, 1), (1, 0), (2, 3), (3, 2)])
                self.inward.append((own, sent))
                self.outward.append((total, sent))
        else:
            self.inward = [(a, lax.ppermute(a, "dp", [(0, 1), (3, 2)])) for a in arrays]
            self.outward = [(a, lax.ppermute(a, "dp", [(1, 0), (2, 3)])) for a in totals]
        self.across = [(a, lax.ppermute(a, "dp", [(1, 2), (2, 1)])) for a in pairs]
        self.sums += [jnp.where(self.outer, sent, own) for own, sent in outward]
        return others


def tensor_bits():
    n, bits, bit = lax.axis_size("tensor"), [], 1
    while bit < n:
        bits.append(bit)
        bit *= 2
    return bits


def reduce_blocks(blocks):
    n, me = blocks.shape[0], lax.axis_index("tensor")
    held = [lax.dynamic_index_in_dim(blocks, me ^ r, 0, keepdims=False) for r in range(n)]
    for bit in tensor_bits():
        keep = jnp.stack([held[r] for r in range(len(held)) if r % 2 == 0])
        give = jnp.stack([held[r] for r in range(len(held)) if r % 2 == 1])
        total = add_up(keep, swap(give.astype(BF16), bit))
        held = [total[k] for k in range(total.shape[0])]
    return held[0]


def gather_blocks(block):
    n, me = lax.axis_size("tensor"), lax.axis_index("tensor")
    held = block[None]
    for bit in reversed(tensor_bits()):
        other = swap(held, bit)
        held = jnp.stack([held, other], 1).reshape(2 * held.shape[0], *block.shape)
    result = jnp.zeros_like(held)
    for r in range(n):
        result = lax.dynamic_update_index_in_dim(result, held[r], me ^ r, 0)
    return result


def gather_near(values):
    if lax.axis_size("tensor") != 8:
        return values, values
    return swap(values, 2), swap(values, 4)


def gather_pairs(values):
    parts, bits = [values], tensor_bits()
    for bit in bits:
        parts = parts + [swap(part, bit) for part in parts]
    return [(parts[i], parts[i + 1]) for i in range(0, len(parts), 2)]


def halves(value):
    rows = value.shape[0] // 2
    return value[:rows], value[rows:]


def reduce_begin(count, terms, between):
    n = lax.axis_size("tensor")
    if n != 8:
        parts = []
        for i in range(count):
            own, other = terms(i, None)
            parts.append(add_up(own, swap(other, 1)))
        while len(parts) > 1:
            half = len(parts) // 2
            parts = [add_up(parts[i], swap(parts[half + i].astype(BF16), 2 * half)) for i in range(half)]
        between(parts[0])
        return parts[0], ()
    own_d, other_d = (terms(3, None))
    core_d = swap(other_d, 1)
    own_y, other_y = (terms(2, own_d))
    core_y = swap(other_y, 1)
    diagonal = add_up(own_d, core_d).astype(BF16)
    diagonal, own_y = tie(diagonal, own_y)
    first, second = halves(diagonal)
    from_x, from_y = swap(first, 2), swap(second, 4)
    own_x, other_x = (terms(1, between(diagonal)))
    core_x = swap(other_x, 1)
    own, other = (terms(0, own_x))
    core = swap(other, 1)
    low, high = halves(add_up(own_y, core_y))
    for_y = jnp.concatenate([add_up(low, from_x), high]).astype(BF16)
    low, high = halves(add_up(own_x, core_x))
    for_x = jnp.concatenate([low, add_up(high, from_y)]).astype(BF16)
    return (own, core), (for_x, for_y)


def reduce_end(own, sent):
    if not sent:
        return own
    return add_up(*own, swap(sent[0], 2), swap(sent[1], 4))


def per_device(
    tokens,
    lengths,
    query_weight,
    key_weight,
    value_weight,
    output_weight,
    gate_weight,
    up_weight,
    down_weight,
    gain_attn,
    gain_mlp,
    pair_grad,
    cotangent,
):
    seqs, rows, width = tokens.shape
    n = lax.axis_size("tensor")
    me = lax.axis_index("tensor")
    top = n // 2
    flat = seqs * rows
    local_pos = me * rows + jnp.arange(rows)
    valid = (local_pos[None, :] < lengths[:, None]).astype(F32)[..., None]
    x = tokens.astype(F32)
    attn_gain = gain_attn.astype(F32)
    mlp_gain = gain_mlp.astype(F32)
    grad_y = cotangent.astype(F32)
    kv_weight = jnp.concatenate([key_weight, value_weight], axis=1)

    norm_in = normed(x, attn_gain).astype(BF16).reshape(flat, width)
    far_in = swap(norm_in, top)
    far_in = (far_in, swap(far_in, 1))
    near_in = (norm_in, swap(norm_in, 1))
    def slopes_of(blocks):
        return [dot(block, down_weight, ((1,), (1,))) for block in blocks]

    def with_core(part):
        return part, swap(part, 1)

    grad_out = (valid * grad_y).astype(BF16).reshape(flat, width)
    own_grads = with_core(grad_out)
    own_slopes, query_parts = tie(slopes_of(own_grads), gather_middle(query_weight))
    query_weights = join_columns(query_parts)
    heads_width = query_weights.shape[1]
    own_cos, own_sin = rope_block(me * rows, rows)
    kv_raw = dot(norm_in, kv_weight, ((1,), (0,))).reshape(seqs, rows, 2 * HEAD)
    key_raw = kv_raw[..., :HEAD]
    key_own = key_raw * own_cos + jnp.roll(key_raw, HEAD // 2, axis=-1) * own_sin
    kv_own = jnp.concatenate([key_own, kv_raw[..., HEAD:]], axis=-1).astype(BF16)

    output_weight, kv_own = tie(output_weight, kv_own)
    output_parts = gather_middle(output_weight)
    kv = lax.all_gather(kv_own, "tensor", axis=1, tiled=True)

    def place_of(offset):
        place = jnp.stack([me ^ offset, me ^ (offset + 1)]).astype(jnp.int32)
        blocks = [rope_block(place[i] * rows, rows) for i in range(2)]
        return place, (jnp.stack([b[0] for b in blocks]), jnp.stack([b[1] for b in blocks]))

    def attend(part, place, table):
        return attention_forward(place, lengths, part, query_weights, kv, *table)

    def portions_of(mixed):
        return [dot(mixed[i], output_weights, ((1,), (0,)), BF16) for i in range(2)]

    near_place, near_table = place_of(0)
    far_place, far_table = place_of(top)
    grad_out, _ = tie(grad_out, norm_in)
    grad_far = swap(grad_out, top)
    near_result = attend(near_in, near_place, near_table)
    far_in, _ = tie(far_in, near_result[0])
    far_result = attend(far_in, far_place, far_table)
    output_parts, far_mixed, grad_far = tie(output_parts, far_result[0], grad_far)
    output_weights = jnp.concatenate(output_parts, axis=0)
    far_portions = portions_of(far_mixed)
    for_far = add_up(far_portions[0], swap(far_portions[1], 1)).astype(BF16)
    for_far, near_mixed = tie(for_far, near_result[0])
    from_far = swap(for_far, top)
    near_portions = portions_of(near_mixed)
    near_core = swap(near_portions[1], 1)
    if n == 8:
        grad_out, _ = tie(grad_out, far_mixed)
        grad_side = swap(grad_out, 2)
        size = flat // 2
        from_far, grad_side, grad_far = tie(from_far, grad_side, grad_far)
        grad_diagonal = [swap(grad_side[:size], 4), swap(grad_far[size:], 2)]
    attn_out = add_up(near_portions[0], near_core, from_far)
    hidden = x + valid * attn_out.reshape(seqs, rows, width)

    chips = n // 2
    norm_mid = normed(hidden, mlp_gain).astype(BF16).reshape(flat, width)
    gate_rows, up_rows = gate_weight.T, up_weight.T

    mids, acts, g_gates, g_ups = [], [], [], []

    def forward_blocks(blocks, slopes):
        for mid, slope in zip(blocks, slopes):
            gate = dot(mid, gate_rows, ((1,), (1,)))
            up = dot(mid, up_rows, ((1,), (1,)))
            sig = 1.0 / (1.0 + jnp.exp(-gate))
            silu = gate * sig
            mids.append(mid)
            acts.append((silu * up).astype(BF16))
            g_gates.append((slope * up * sig * (1.0 + gate * (1.0 - sig))).astype(BF16))
            g_ups.append((slope * silu).astype(BF16))

    def diagonal_blocks(parts):
        return [jnp.concatenate(p) for p in zip(*[with_core(part) for part in parts])]

    if n == 8:
        at_x, at_y = gather_near(norm_mid)
        grads = [*own_grads, *with_core(grad_side), *with_core(grad_far)]
        slopes = own_slopes + slopes_of(grads[2:])
        forward_blocks(with_core(norm_mid), slopes[:2])
        at_x, at_y, slopes, acts[1] = tie(at_x, at_y, slopes, acts[1])
        diagonal = [swap(at_x[:size], 4), swap(at_y[size:], 2)]
        forward_blocks((*with_core(at_x), *with_core(at_y)), slopes[2:6])
        grad_down = sum_of_products(acts[:6], grads[:6])
        diagonal, grad_diagonal, grad_down = tie(diagonal, grad_diagonal, grad_down)
        grads += diagonal_blocks(grad_diagonal)
        forward_blocks(diagonal_blocks(diagonal), slopes_of(grads[6:]))
    else:
        grads = [block for pair in gather_pairs(grad_out) for block in pair]
        forward_blocks([block for pair in gather_pairs(norm_mid) for block in pair], slopes_of(grads))
        grad_down = sum_of_products(acts[:-2], grads[:-2])

    def mid_term(r):
        terms = dot(g_gates[r], gate_rows, ((1,), (0,))) + dot(g_ups[r], up_rows, ((1,), (0,)))
        return terms.astype(BF16)

    def mid_terms(i, after):
        for k in (2 * i, 2 * i + 1):
            if after is not None:
                g_gates[k], g_ups[k], _ = tie(g_gates[k], g_ups[k], after)
        return mid_term(2 * i), mid_term(2 * i + 1)

    sums, down_parts = LineSum(), []

    def down_gradient(after):
        last, after = tie(acts[-2:], after)
        down_parts.extend(halves(sum_of_products(last, grads[-2:], grad_down).astype(BF16)))
        return sums.advance([down_parts[0]], after)

    mid_own, mid_sent = reduce_begin(chips, mid_terms, down_gradient)
    grad_mid = reduce_end(mid_own, mid_sent).reshape(seqs, rows, width)

    g_gates, g_ups, mids = sums.advance([down_parts[1]], (g_gates, g_ups, mids))
    mid_all = [jnp.concatenate(mids)]
    grad_gate = halves(sum_of_products(g_gates, mid_all).astype(BF16))
    back, mlp_gain_part = norm_back(hidden, mlp_gain, grad_mid)
    grad_hidden = grad_y + back
    grad_attn = (valid * grad_hidden).astype(BF16).reshape(flat, width)
    far_grad = swap(grad_attn, top)
    near_grad = (grad_attn, swap(grad_attn, 1))

    def attend_back(part, result, place, table):
        return attention_backward(
            place, lengths, part, output_weights, query_weights, result[1], result[2], kv, *table
        )

    def product(left, right):
        return dot(jnp.concatenate(left), jnp.concatenate(right), ((0,), (0,)), BF16)

    g_ups, near_grad = sums.advance([grad_gate[0]], (g_ups, near_grad))
    grad_up = halves(sum_of_products(g_ups, mid_all).astype(BF16))
    near_q, near_terms, near_kv = attend_back(near_grad, near_result, near_place, near_table)
    near_core = swap(near_terms[1], 1)

    far_grad, near_q, near_kv = sums.advance([grad_gate[1]], (far_grad, near_q, near_kv))
    far_grad = (far_grad, swap(far_grad, 1))
    far_q, far_terms, far_kv = attend_back(far_grad, far_result, far_place, far_table)
    for_far = add_up(far_terms[0], swap(far_terms[1], 1)).astype(BF16)
    from_far = swap(for_far, top)

    far_grad, far_q, far_kv = sums.advance([grad_up[0]], (far_grad, far_q, far_kv))
    unit = output_weight.shape[0]
    kv_blocks = (near_kv + far_kv).astype(BF16).reshape(seqs, n, rows, 2 * HEAD).swapaxes(0, 1)
    kv_sum = reduce_blocks(kv_blocks)
    mixed = [r[0][i] for r in (near_result, far_result) for i in range(2)]
    wo_full = product(mixed, [*near_grad, *far_grad])
    wo_full, kv_sum = tie(wo_full, kv_sum)
    wo_part = reduce_middle([wo_full[i * unit : (i + 1) * unit] for i in range(heads_width // unit)])
    wo_part = wo_part.astype(BF16)
    key_grad = kv_sum[..., :HEAD]
    key_grad = key_grad * own_cos - jnp.roll(key_grad, HEAD // 2, axis=-1) * own_sin
    kv_grad = jnp.concatenate([key_grad, kv_sum[..., HEAD:]], -1).astype(BF16).reshape(flat, 2 * HEAD)

    from_far, far_q, kv_grad = sums.advance([grad_up[1]], (from_far, far_q, kv_grad))
    grad_in = add_up(near_terms[0], near_core, from_far)
    grad_in = grad_in + dot(kv_grad, kv_weight, ((1,), (1,)))
    kv_portion = dot(norm_in, kv_grad, ((0,), (0,)))
    back, attn_gain_part = norm_back(x, attn_gain, grad_in.reshape(seqs, rows, width))
    grad_tokens = grad_hidden + back
    gains = jnp.concatenate([attn_gain_part, mlp_gain_part]).reshape(-1, 2 * HEAD)
    shared = jnp.concatenate([kv_portion + pair_grad[0, 0], gains])
    shared = jnp.pad(shared, ((0, -shared.shape[0] % (16 * n)), (0, 0))).astype(BF16)
    shared = reduce_blocks(shared.reshape(n, -1, 2 * HEAD)).astype(BF16)


    wq_full = product([near_q[0], near_q[1], far_q[0], far_q[1]], [*near_in, *far_in])
    wq_full, shared = tie(wq_full, shared)
    wq_part = reduce_middle([wq_full[i * unit : (i + 1) * unit] for i in range(heads_width // unit)])
    wq_part = wq_part.astype(BF16)

    acts = sums.advance([wo_part, shared], acts)

    def out_terms(i, after):
        left = acts[2 * i : 2 * i + 2]
        left = left if after is None else tie(left, after)[0]
        return [dot(part, down_weight, ((1,), (0,)), BF16) for part in left]

    out_own, out_sent = reduce_begin(chips, out_terms, lambda after: after)
    rows_out = reduce_end(out_own, out_sent)
    output = (hidden + valid * rows_out.reshape(seqs, rows, width)).astype(BF16)
    sums.advance([wq_part])
    sums.advance([])
    sums.advance([])
    sums.advance([])
    down_1, down_2, gate_1, gate_2, up_1, up_2, wo_sum, shared, wq_sum = sums.sums
    shared = gather_blocks(shared).reshape(-1, 2 * HEAD).astype(F32)
    gains = shared[width : width + gains.shape[0]].reshape(2, width)
    return (
        output,
        grad_tokens,
        wq_sum.astype(F32).T,
        shared[:width, :HEAD],
        shared[:width, HEAD:],
        wo_sum.astype(F32),
        jnp.concatenate([gate_1, gate_2]).astype(F32).T,
        jnp.concatenate([up_1, up_2]).astype(F32).T,
        jnp.concatenate([down_1, down_2]).astype(F32),
        gains[0],
        gains[1],
    )


def solution(mesh):
    placed = (
        P("dp", "tensor", None),
        P("dp"),
        P(None, "tensor"),
        P(),
        P(),
        P("tensor", None),
        P(None, "tensor"),
        P(None, "tensor"),
        P("tensor", None),
        P(),
        P(),
        P("dp", "tensor", None, None),
        P("dp", "tensor", None),
    )
    return jax.shard_map(
        per_device,
        mesh=mesh,
        in_specs=placed,
        out_specs=(
            P("dp", "tensor", None),
            P("dp", "tensor", None),
            P(None, "tensor"),
            P(),
            P(),
            P("tensor", None),
            P(None, "tensor"),
            P(None, "tensor"),
            P("tensor", None),
            P(),
            P(),
        ),
        check_vma=False,
    )
```

```python
import functools

import jax
import jax.numpy as jnp
from jax import lax
from jax.experimental import pallas as pl
from jax.experimental.pallas import tpu as pltpu
from jax.sharding import PartitionSpec as P

HEAD = 128
KEY_BLOCK = 256
JOIN_COST = 8_000_000_000
BACK_COST = 1
FORTH_COST = 60
SMALL_SHIFT = 1e-05
ROPE_BASE = 10000.0
NEG_FILL = -1e30
LOG2E = 1.4426950408889634
F32 = jnp.float32
BF16 = jnp.bfloat16


def rms_scale(values):
    return lax.rsqrt(jnp.mean(values * values, axis=-1, keepdims=True) + SMALL_SHIFT)


def normed(values, gain_vec):
    return values * rms_scale(values) * gain_vec


def norm_back(values, gain_vec, grad_vals):
    scale_vals = rms_scale(values)
    scaled = grad_vals * gain_vec
    inner_mean = jnp.mean(scaled * values, axis=-1, keepdims=True)
    grad_values = scale_vals * scaled - values * (scale_vals * scale_vals * scale_vals) * inner_mean
    grad_gain = jnp.sum(grad_vals * values * scale_vals, axis=(0, 1))
    return grad_values, grad_gain


def rope_block(start, rows):
    half = HEAD // 2
    frequency = ROPE_BASE ** (-2.0 * jnp.arange(half, dtype=F32) / HEAD)
    angles = (start + jnp.arange(rows)).astype(F32)[:, None] * frequency[None, :]
    cosine, sine = jnp.cos(angles), jnp.sin(angles)
    return jnp.concatenate([cosine, cosine], 1), jnp.concatenate([-sine, sine], 1)


def swap(values, bit):
    n = lax.axis_size("tensor")
    return lax.ppermute(values, "tensor", [(i, i ^ bit) for i in range(n)])


def dot(a, b, dims, out=F32):
    return lax.dot_general(a, b, (dims, ((), ())), preferred_element_type=F32).astype(out)


def add_up(*parts):
    total = parts[0].astype(F32)
    for part in parts[1:]:
        total = total + part.astype(F32)
    return total


def key_branches(start, rows, span, body):
    blocks = span // KEY_BLOCK
    needed = (start + rows + KEY_BLOCK - 1) // KEY_BLOCK
    for count in range(1, blocks + 1):
        pl.when(needed == count)(functools.partial(body, count * KEY_BLOCK))


def stack_heads(values, heads):
    return jnp.concatenate([values[:, h * HEAD : (h + 1) * HEAD] for h in range(heads)], axis=0)


def matmul(a, b, contract):
    return lax.dot_general(a, b, (contract, ((), ())), preferred_element_type=F32)


def masked_scores(keys, query, start, rows, heads, count):
    scores = matmul(keys, query, ((1,), (1,)))
    key_pos = lax.broadcasted_iota(jnp.int32, (KEY_BLOCK, rows), 0) + (count - KEY_BLOCK)
    row_pos = lax.broadcasted_iota(jnp.int32, (KEY_BLOCK, rows), 1) + start
    allowed = key_pos <= row_pos
    last = scores[count - KEY_BLOCK :]
    last = jnp.concatenate(
        [jnp.where(allowed, last[:, h * rows : (h + 1) * rows], NEG_FILL) for h in range(heads)], axis=1
    )
    if count == KEY_BLOCK:
        return last
    return jnp.concatenate([scores[: count - KEY_BLOCK], last], axis=0)


def forward_kernel(
    place, lengths, x0_ref, x1_ref, wq_ref, kv_ref, cos_ref, sin_ref, mixed_ref, query_ref, lse_ref, raw_ref, vt_ref
):
    a = pl.program_id(0)
    seqs, span = kv_ref.shape[0], kv_ref.shape[1]
    rows = x0_ref.shape[0] // seqs
    heads = wq_ref.shape[1] // HEAD
    start = place[a] * rows
    cosine, sine = cos_ref[0], sin_ref[0]
    factor = HEAD ** (-0.5) * LOG2E

    @pl.when(a == 0)
    def _():
        raw_ref[...] = matmul(x0_ref[...], wq_ref[...], ((1,), (0,)))
        for s in range(seqs):
            vt_ref[s] = kv_ref[s, :, HEAD:].T

    @pl.when(a == 1)
    def _():
        raw_ref[...] = matmul(x1_ref[...], wq_ref[...], ((1,), (0,)))

    for s in range(seqs):
        here = slice(s * rows, (s + 1) * rows)
        pieces = []
        for h in range(heads):
            raw = raw_ref[here, h * HEAD : (h + 1) * HEAD]
            pieces.append((raw * cosine + pltpu.roll(raw, HEAD // 2, 1) * sine).astype(BF16))
        query = jnp.concatenate(pieces, axis=0)
        query_ref[0, s] = query
        live = start < lengths[s]

        def body(count, s=s, here=here, query=query):
            scores = masked_scores(kv_ref[s, :count, :HEAD], query, start, rows, heads, count)
            top = jnp.max(scores, axis=0, keepdims=True)
            terms = jnp.exp2((scores - top) * factor)
            total = jnp.sum(terms, axis=0, keepdims=True)
            out = matmul(vt_ref[s, :, :count], terms.astype(BF16), ((1,), (0,))) / total
            lse_ref[0, s] = jnp.broadcast_to(top * factor + jnp.log2(total), lse_ref.shape[2:])
            for h in range(heads):
                piece = out[:, h * rows : (h + 1) * rows].T
                mixed_ref[0, here, h * HEAD : (h + 1) * HEAD] = piece.astype(BF16)

        @pl.when(live)
        def _(body=body):
            key_branches(start, rows, span, body)

        @pl.when(jnp.logical_not(live))
        def _(s=s, here=here):
            mixed_ref[0, here] = jnp.zeros((rows, heads * HEAD), BF16)
            lse_ref[0, s] = jnp.zeros(lse_ref.shape[2:], F32)


def whole(shape):
    return pl.BlockSpec(shape, lambda a, *_: (0,) * len(shape))


def blocked(shape):
    return pl.BlockSpec((1, *shape[1:]), lambda a, *_: (a,) + (0,) * (len(shape) - 1))


def attention_forward(place, lengths, parts, query_weights, kv, cosine, sine):
    flat, width = parts[0].shape
    seqs, span = kv.shape[0], kv.shape[1]
    rows, wide = flat // seqs, query_weights.shape[1]
    heads = wide // HEAD
    shapes = [(2, flat, wide), (2, seqs, heads * rows, HEAD), (2, seqs, 8, heads * rows)]
    return pl.pallas_call(
        forward_kernel,
        grid_spec=pltpu.PrefetchScalarGridSpec(
            num_scalar_prefetch=2,
            grid=(2,),
            in_specs=[
                whole(parts[0].shape),
                whole(parts[1].shape),
                whole(query_weights.shape),
                whole(kv.shape),
                blocked(cosine.shape),
                blocked(sine.shape),
            ],
            out_specs=[blocked(shape) for shape in shapes],
            scratch_shapes=[pltpu.VMEM((flat, wide), F32), pltpu.VMEM((seqs, HEAD, span), BF16)],
        ),
        out_shape=[jax.ShapeDtypeStruct(s, t) for s, t in zip(shapes, (BF16, BF16, F32))],
        compiler_params=pltpu.CompilerParams(vmem_limit_bytes=48 * 1024 * 1024),
        cost_estimate=pl.CostEstimate(flops=FORTH_COST * flat * wide * span, bytes_accessed=kv.size, transcendentals=0),
        name="attention_forward",
    )(place, lengths, *parts, query_weights, kv, cosine, sine)


def backward_kernel(
    place, lengths, g0_ref, g1_ref, wo_ref, wq_ref, query_ref, lse_ref, kv_ref, cos_ref, sin_ref,
    gq_ref, in_ref, gkv_ref, gm_ref, kt_ref,
):
    a = pl.program_id(0)
    seqs, span = kv_ref.shape[0], kv_ref.shape[1]
    rows = g0_ref.shape[0] // seqs
    heads = wq_ref.shape[1] // HEAD
    start = place[a] * rows
    scale = HEAD ** (-0.5)
    factor = scale * LOG2E

    @pl.when(a == 0)
    def _():
        gm_ref[...] = matmul(g0_ref[...], wo_ref[...], ((1,), (1,))).astype(BF16)
        gkv_ref[...] = jnp.zeros(gkv_ref.shape, F32)
        for s in range(seqs):
            kt_ref[s] = kv_ref[s, :, :HEAD].T

    @pl.when(a == 1)
    def _():
        gm_ref[...] = matmul(g1_ref[...], wo_ref[...], ((1,), (1,))).astype(BF16)

    for s in range(seqs):
        here = slice(s * rows, (s + 1) * rows)
        live = start < lengths[s]

        def body(count, s=s, here=here):
            query = query_ref[0, s]
            grad = stack_heads(gm_ref[here, :], heads)
            scores = masked_scores(kv_ref[s, :count, :HEAD], query, start, rows, heads, count)
            probs = jnp.exp2(scores * factor - lse_ref[0, s, 0:1, :])
            grad_probs = matmul(kv_ref[s, :count, HEAD:], grad, ((1,), (1,)))
            row_dots = jnp.sum(probs * grad_probs, axis=0, keepdims=True)
            grad_scores = (probs * (grad_probs - row_dots)).astype(BF16)
            gkv_ref[s, :count, :HEAD] += scale * matmul(grad_scores, query, ((1,), (0,)))
            gkv_ref[s, :count, HEAD:] += matmul(probs.astype(BF16), grad, ((1,), (0,)))
            grad_query = matmul(kt_ref[s, :, :count], grad_scores, ((1,), (0,)))
            cosine, sine = cos_ref[0], sin_ref[0]
            for h in range(heads):
                piece = grad_query[:, h * rows : (h + 1) * rows].T * scale
                piece = piece * cosine - pltpu.roll(piece, HEAD // 2, 1) * sine
                gq_ref[0, here, h * HEAD : (h + 1) * HEAD] = piece.astype(BF16)

        @pl.when(live)
        def _(body=body):
            key_branches(start, rows, span, body)

        @pl.when(jnp.logical_not(live))
        def _(here=here):
            gq_ref[0, here] = jnp.zeros((rows, heads * HEAD), BF16)

    in_ref[0] = matmul(gq_ref[0], wq_ref[...], ((1,), (1,))).astype(BF16)


def attention_backward(place, lengths, grads, output_weights, query_weights, query, lse, kv, cosine, sine):
    flat, width = grads[0].shape
    seqs, span = kv.shape[0], kv.shape[1]
    wide = query_weights.shape[1]
    operands = (*grads, output_weights, query_weights, query, lse, kv, cosine, sine)
    specs = [whole(v.shape) for v in operands]
    for k in (4, 5, 7, 8):
        specs[k] = blocked(operands[k].shape)
    return pl.pallas_call(
        backward_kernel,
        grid_spec=pltpu.PrefetchScalarGridSpec(
            num_scalar_prefetch=2,
            grid=(2,),
            in_specs=specs,
            out_specs=[blocked((2, flat, wide)), blocked((2, flat, width)), whole(kv.shape)],
            scratch_shapes=[pltpu.VMEM((flat, wide), BF16), pltpu.VMEM((seqs, HEAD, span), BF16)],
        ),
        out_shape=[
            jax.ShapeDtypeStruct((2, flat, wide), BF16),
            jax.ShapeDtypeStruct((2, flat, width), BF16),
            jax.ShapeDtypeStruct(kv.shape, F32),
        ],
        compiler_params=pltpu.CompilerParams(vmem_limit_bytes=56 * 1024 * 1024),
        cost_estimate=pl.CostEstimate(flops=BACK_COST * flat * wide * span, bytes_accessed=kv.size, transcendentals=0),
        name="attention_backward",
    )(place, lengths, *operands)


def join_columns(parts):
    rows, wide = parts[0].shape

    def kernel(*refs):
        for k in range(len(parts)):
            refs[-1][:, k * wide : (k + 1) * wide] = refs[k][...]

    return pl.pallas_call(
        kernel,
        grid=(4,),
        in_specs=[pl.BlockSpec((rows // 4, wide), lambda i: (i, 0)) for _ in parts],
        out_specs=pl.BlockSpec((rows // 4, wide * len(parts)), lambda i: (i, 0)),
        out_shape=jax.ShapeDtypeStruct((rows, wide * len(parts)), parts[0].dtype),
        cost_estimate=pl.CostEstimate(flops=JOIN_COST, bytes_accessed=0, transcendentals=0),
        name="join_columns",
    )(*parts)


def middle_bits(n):
    bits, bit = [], 2
    while bit < n // 2:
        bits.append(bit)
        bit *= 2
    return bits


def gather_middle(values):
    parts = [values]
    for bit in middle_bits(lax.axis_size("tensor")):
        parts = parts + [swap(part, bit) for part in parts]
    return parts


def reduce_middle(parts):
    for bit in reversed(middle_bits(lax.axis_size("tensor"))):
        half = len(parts) // 2
        parts = [add_up(parts[i], swap(parts[half + i].astype(BF16), bit)) for i in range(half)]
    return parts[0]


def sum_of_products(left, right, start=None):
    total = dot(jnp.concatenate(left), jnp.concatenate(right), ((0,), (0,)))
    return total if start is None else start + total


def tie(*values):
    return lax.optimization_barrier(values)


def line_step(outer, own_in, sent_in, fresh, own_across, sent_across):
    rows, width = fresh.shape

    def kernel(outer_ref, a_ref, b_ref, c_ref, d_ref, e_ref, pair_ref, leaving_ref):
        @pl.when(outer_ref[0] == 1)
        def _():
            pair_ref[...] = c_ref[...]
            leaving_ref[...] = c_ref[...]

        @pl.when(outer_ref[0] == 0)
        def _():
            pair_ref[...] = (a_ref[...].astype(F32) + b_ref[...].astype(F32)).astype(BF16)
            leaving_ref[...] = (d_ref[...].astype(F32) + e_ref[...].astype(F32)).astype(BF16)

    steps = 4
    inner_block = pl.BlockSpec((rows, width // steps), lambda i, o: (0, i * (1 - o[0])))
    outer_block = pl.BlockSpec((rows, width // steps), lambda i, o: (0, i * o[0]))
    block = pl.BlockSpec((rows, width // steps), lambda i, o: (0, i))
    return pl.pallas_call(
        kernel,
        grid_spec=pltpu.PrefetchScalarGridSpec(
            num_scalar_prefetch=1,
            grid=(steps,),
            in_specs=[inner_block, inner_block, outer_block, inner_block, inner_block],
            out_specs=[block, block],
        ),
        out_shape=[jax.ShapeDtypeStruct((rows, width), BF16)] * 2,
        name="line_step",
    )(outer.astype(jnp.int32).reshape(1), own_in, sent_in, fresh, own_across, sent_across)


class LineSum:
    def __init__(self):
        self.line = lax.axis_size("dp") == 4
        place = lax.axis_index("dp")
        self.outer = (place == 0) | (place == 3)
        self.inward, self.across, self.outward = [], [], []
        self.sums = []

    def advance(self, arrays, others=()):
        if not self.line:
            self.sums += [lax.psum(a, "dp") for a in arrays]
            return others
        arrays, inward, across, outward, others = tie(
            list(arrays), self.inward, self.across, self.outward, others
        )
        self.inward, self.outward = [], []
        if len(arrays) == 1 and [a.shape for a, _ in inward + across] == [arrays[0].shape] * 2:
            pairs, leaving = line_step(self.outer, *inward[0], arrays[0], *across[0])
            sent = lax.ppermute(leaving, "dp", [(0, 1), (1, 0), (2, 3), (3, 2)])
            self.inward.append((arrays[0], sent))
            self.outward.append((leaving, sent))
            pairs = [pairs]
        else:
            pairs = [add_up(own, sent).astype(BF16) for own, sent in inward]
            totals = [add_up(own, sent).astype(BF16) for own, sent in across]
            self.inward = [(a, lax.ppermute(a, "dp", [(0, 1), (3, 2)])) for a in arrays]
            self.outward = [(a, lax.ppermute(a, "dp", [(1, 0), (2, 3)])) for a in totals]
        self.across = [(a, lax.ppermute(a, "dp", [(1, 2), (2, 1)])) for a in pairs]
        self.sums += [jnp.where(self.outer, sent, own) for own, sent in outward]
        return others


    def advance_and_peek(self):
        self.advance([])
        if not self.line:
            return self.sums[-2]
        own, sent = self.outward[-1]
        return jnp.where(self.outer, sent, own)


def tensor_bits():
    n, bits, bit = lax.axis_size("tensor"), [], 1
    while bit < n:
        bits.append(bit)
        bit *= 2
    return bits


def reduce_blocks(blocks):
    n, me = blocks.shape[0], lax.axis_index("tensor")
    held = [lax.dynamic_index_in_dim(blocks, me ^ r, 0, keepdims=False) for r in range(n)]
    for bit in tensor_bits():
        keep = jnp.stack([held[r] for r in range(len(held)) if r % 2 == 0])
        give = jnp.stack([held[r] for r in range(len(held)) if r % 2 == 1])
        total = add_up(keep, swap(give.astype(BF16), bit))
        held = [total[k] for k in range(total.shape[0])]
    return held[0]


def gather_blocks(block):
    n, me = lax.axis_size("tensor"), lax.axis_index("tensor")
    held = block[None]
    for bit in reversed(tensor_bits()):
        other = swap(held, bit)
        held = jnp.stack([held, other], 1).reshape(2 * held.shape[0], *block.shape)
    result = jnp.zeros_like(held)
    for r in range(n):
        result = lax.dynamic_update_index_in_dim(result, held[r], me ^ r, 0)
    return result


def gather_near(values):
    if lax.axis_size("tensor") != 8:
        return values, values
    return swap(values, 2), swap(values, 4)


def gather_pairs(values):
    parts, bits = [values], tensor_bits()
    for bit in bits:
        parts = parts + [swap(part, bit) for part in parts]
    return [(parts[i], parts[i + 1]) for i in range(0, len(parts), 2)]


def halves(value):
    rows = value.shape[0] // 2
    return value[:rows], value[rows:]


def reduce_begin(count, terms, between):
    n = lax.axis_size("tensor")
    if n != 8:
        parts = []
        for i in range(count):
            own, other = terms(i, None)
            parts.append(add_up(own, swap(other, 1)))
        while len(parts) > 1:
            half = len(parts) // 2
            parts = [add_up(parts[i], swap(parts[half + i].astype(BF16), 2 * half)) for i in range(half)]
        between(parts[0])
        return parts[0], ()
    own_d, other_d = (terms(3, None))
    core_d = swap(other_d, 1)
    own_y, other_y = (terms(2, own_d))
    core_y = swap(other_y, 1)
    diagonal = add_up(own_d, core_d).astype(BF16)
    diagonal, own_y = tie(diagonal, own_y)
    first, second = halves(diagonal)
    from_x, from_y = swap(first, 2), swap(second, 4)
    own_x, other_x = (terms(1, between(diagonal)))
    core_x = swap(other_x, 1)
    own, other = (terms(0, own_x))
    core = swap(other, 1)
    low, high = halves(add_up(own_y, core_y))
    for_y = jnp.concatenate([add_up(low, from_x), high]).astype(BF16)
    low, high = halves(add_up(own_x, core_x))
    for_x = jnp.concatenate([low, add_up(high, from_y)]).astype(BF16)
    return (own, core), (for_x, for_y)


def reduce_end(own, sent):
    if not sent:
        return own
    return add_up(*own, swap(sent[0], 2), swap(sent[1], 4))


def per_device(
    tokens,
    lengths,
    query_weight,
    key_weight,
    value_weight,
    output_weight,
    gate_weight,
    up_weight,
    down_weight,
    gain_attn,
    gain_mlp,
    pair_grad,
    cotangent,
):
    seqs, rows, width = tokens.shape
    n = lax.axis_size("tensor")
    me = lax.axis_index("tensor")
    top = n // 2
    flat = seqs * rows
    local_pos = me * rows + jnp.arange(rows)
    valid = (local_pos[None, :] < lengths[:, None]).astype(F32)[..., None]
    x = tokens.astype(F32)
    attn_gain = gain_attn.astype(F32)
    mlp_gain = gain_mlp.astype(F32)
    grad_y = cotangent.astype(F32)
    kv_weight = jnp.concatenate([key_weight, value_weight], axis=1)

    norm_in = normed(x, attn_gain).astype(BF16).reshape(flat, width)
    far_in = swap(norm_in, top)
    far_in = (far_in, swap(far_in, 1))
    near_in = (norm_in, swap(norm_in, 1))
    def slopes_of(blocks):
        return [dot(block, down_weight, ((1,), (1,))) for block in blocks]

    def with_core(part):
        return part, swap(part, 1)

    grad_out = (valid * grad_y).astype(BF16).reshape(flat, width)
    own_grads = with_core(grad_out)
    own_slopes, query_parts = tie(slopes_of(own_grads), gather_middle(query_weight))
    query_weights = join_columns(query_parts)
    heads_width = query_weights.shape[1]
    own_cos, own_sin = rope_block(me * rows, rows)
    kv_raw = dot(norm_in, kv_weight, ((1,), (0,))).reshape(seqs, rows, 2 * HEAD)
    key_raw = kv_raw[..., :HEAD]
    key_own = key_raw * own_cos + jnp.roll(key_raw, HEAD // 2, axis=-1) * own_sin
    kv_own = jnp.concatenate([key_own, kv_raw[..., HEAD:]], axis=-1).astype(BF16)

    output_weight, kv_own = tie(output_weight, kv_own)
    output_parts = gather_middle(output_weight)
    kv = lax.all_gather(kv_own, "tensor", axis=1, tiled=True)

    def place_of(offset):
        place = jnp.stack([me ^ offset, me ^ (offset + 1)]).astype(jnp.int32)
        blocks = [rope_block(place[i] * rows, rows) for i in range(2)]
        return place, (jnp.stack([b[0] for b in blocks]), jnp.stack([b[1] for b in blocks]))

    def attend(part, place, table):
        return attention_forward(place, lengths, part, query_weights, kv, *table)

    def portions_of(mixed):
        return [dot(mixed[i], output_weights, ((1,), (0,)), BF16) for i in range(2)]

    near_place, near_table = place_of(0)
    far_place, far_table = place_of(top)
    grad_out, _ = tie(grad_out, norm_in)
    grad_far = swap(grad_out, top)
    near_result = attend(near_in, near_place, near_table)
    far_in, _ = tie(far_in, near_result[0])
    far_result = attend(far_in, far_place, far_table)
    output_parts, far_mixed, grad_far = tie(output_parts, far_result[0], grad_far)
    output_weights = jnp.concatenate(output_parts, axis=0)
    far_portions = portions_of(far_mixed)
    for_far = add_up(far_portions[0], swap(far_portions[1], 1)).astype(BF16)
    for_far, near_mixed = tie(for_far, near_result[0])
    from_far = swap(for_far, top)
    near_portions = portions_of(near_mixed)
    near_core = swap(near_portions[1], 1)
    if n == 8:
        grad_out, _ = tie(grad_out, far_mixed)
        grad_side = swap(grad_out, 2)
        size = flat // 2
        from_far, grad_side, grad_far = tie(from_far, grad_side, grad_far)
        grad_diagonal = [swap(grad_side[:size], 4), swap(grad_far[size:], 2)]
    attn_out = add_up(near_portions[0], near_core, from_far)
    hidden = x + valid * attn_out.reshape(seqs, rows, width)

    chips = n // 2
    norm_mid = normed(hidden, mlp_gain).astype(BF16).reshape(flat, width)
    gate_rows, up_rows = gate_weight.T, up_weight.T

    mids, acts, g_gates, g_ups = [], [], [], []

    def forward_blocks(blocks, slopes):
        for mid, slope in zip(blocks, slopes):
            gate = dot(mid, gate_rows, ((1,), (1,)))
            up = dot(mid, up_rows, ((1,), (1,)))
            sig = 1.0 / (1.0 + jnp.exp(-gate))
            silu = gate * sig
            mids.append(mid)
            acts.append((silu * up).astype(BF16))
            g_gates.append((slope * up * sig * (1.0 + gate * (1.0 - sig))).astype(BF16))
            g_ups.append((slope * silu).astype(BF16))

    def diagonal_blocks(parts):
        return [jnp.concatenate(p) for p in zip(*[with_core(part) for part in parts])]

    if n == 8:
        at_x, at_y = gather_near(norm_mid)
        grads = [*own_grads, *with_core(grad_side), *with_core(grad_far)]
        slopes = own_slopes + slopes_of(grads[2:])
        forward_blocks(with_core(norm_mid), slopes[:2])
        at_x, at_y, slopes, acts[1] = tie(at_x, at_y, slopes, acts[1])
        diagonal = [swap(at_x[:size], 4), swap(at_y[size:], 2)]
        forward_blocks((*with_core(at_x), *with_core(at_y)), slopes[2:6])
        grad_down = sum_of_products(acts[:6], grads[:6])
        diagonal, grad_diagonal, grad_down = tie(diagonal, grad_diagonal, grad_down)
        grads += diagonal_blocks(grad_diagonal)
        forward_blocks(diagonal_blocks(diagonal), slopes_of(grads[6:]))
    else:
        grads = [block for pair in gather_pairs(grad_out) for block in pair]
        forward_blocks([block for pair in gather_pairs(norm_mid) for block in pair], slopes_of(grads))
        grad_down = sum_of_products(acts[:-2], grads[:-2])

    def mid_term(r):
        terms = dot(g_gates[r], gate_rows, ((1,), (0,))) + dot(g_ups[r], up_rows, ((1,), (0,)))
        return terms.astype(BF16)

    def mid_terms(i, after):
        for k in (2 * i, 2 * i + 1):
            if after is not None:
                g_gates[k], g_ups[k], _ = tie(g_gates[k], g_ups[k], after)
        return mid_term(2 * i), mid_term(2 * i + 1)

    sums, down_parts = LineSum(), []

    def down_gradient(after):
        last, after = tie(acts[-2:], after)
        down_parts.extend(halves(sum_of_products(last, grads[-2:], grad_down).astype(BF16)))
        return sums.advance([down_parts[0]], after)

    mid_own, mid_sent = reduce_begin(chips, mid_terms, down_gradient)
    grad_mid = reduce_end(mid_own, mid_sent).reshape(seqs, rows, width)

    g_gates, g_ups, mids = sums.advance([down_parts[1]], (g_gates, g_ups, mids))
    mid_all = [jnp.concatenate(mids)]
    grad_gate = halves(sum_of_products(g_gates, mid_all).astype(BF16))
    back, mlp_gain_part = norm_back(hidden, mlp_gain, grad_mid)
    grad_hidden = grad_y + back
    grad_attn = (valid * grad_hidden).astype(BF16).reshape(flat, width)
    far_grad = swap(grad_attn, top)
    near_grad = (grad_attn, swap(grad_attn, 1))

    def attend_back(part, result, place, table):
        return attention_backward(
            place, lengths, part, output_weights, query_weights, result[1], result[2], kv, *table
        )

    def product(left, right):
        return dot(jnp.concatenate(left), jnp.concatenate(right), ((0,), (0,)), BF16)

    g_ups, near_grad = sums.advance([grad_gate[0]], (g_ups, near_grad))
    grad_up = halves(sum_of_products(g_ups, mid_all).astype(BF16))
    near_q, near_terms, near_kv = attend_back(near_grad, near_result, near_place, near_table)
    near_core = swap(near_terms[1], 1)

    far_grad, near_q, near_kv = sums.advance([grad_gate[1]], (far_grad, near_q, near_kv))
    far_grad = (far_grad, swap(far_grad, 1))
    far_q, far_terms, far_kv = attend_back(far_grad, far_result, far_place, far_table)
    for_far = add_up(far_terms[0], swap(far_terms[1], 1)).astype(BF16)
    from_far = swap(for_far, top)

    far_grad, far_q, far_kv = sums.advance([grad_up[0]], (far_grad, far_q, far_kv))
    unit = output_weight.shape[0]
    kv_blocks = (near_kv + far_kv).astype(BF16).reshape(seqs, n, rows, 2 * HEAD).swapaxes(0, 1)
    kv_sum = reduce_blocks(kv_blocks)
    mixed = [r[0][i] for r in (near_result, far_result) for i in range(2)]
    wo_full = product(mixed, [*near_grad, *far_grad])
    wo_full, kv_sum = tie(wo_full, kv_sum)
    wo_part = reduce_middle([wo_full[i * unit : (i + 1) * unit] for i in range(heads_width // unit)])
    wo_part = wo_part.astype(BF16)
    key_grad = kv_sum[..., :HEAD]
    key_grad = key_grad * own_cos - jnp.roll(key_grad, HEAD // 2, axis=-1) * own_sin
    kv_grad = jnp.concatenate([key_grad, kv_sum[..., HEAD:]], -1).astype(BF16).reshape(flat, 2 * HEAD)

    from_far, far_q, kv_grad = sums.advance([grad_up[1]], (from_far, far_q, kv_grad))
    grad_in = add_up(near_terms[0], near_core, from_far)
    grad_in = grad_in + dot(kv_grad, kv_weight, ((1,), (1,)))
    kv_portion = dot(norm_in, kv_grad, ((0,), (0,)))
    back, attn_gain_part = norm_back(x, attn_gain, grad_in.reshape(seqs, rows, width))
    grad_tokens = grad_hidden + back
    gains = jnp.concatenate([attn_gain_part, mlp_gain_part]).reshape(-1, 2 * HEAD)
    shared = jnp.concatenate([kv_portion + pair_grad[0, 0], gains])
    shared = jnp.pad(shared, ((0, -shared.shape[0] % (16 * n)), (0, 0))).astype(BF16)
    shared = reduce_blocks(shared.reshape(n, -1, 2 * HEAD)).astype(BF16)


    wq_full = product([near_q[0], near_q[1], far_q[0], far_q[1]], [*near_in, *far_in])
    wq_full, shared = tie(wq_full, shared)
    wq_part = reduce_middle([wq_full[i * unit : (i + 1) * unit] for i in range(heads_width // unit)])
    wq_part = wq_part.astype(BF16)

    acts = sums.advance([wo_part, shared], acts)

    def out_terms(i, after):
        left = acts[2 * i : 2 * i + 2]
        left = left if after is None else tie(left, after)[0]
        return [dot(part, down_weight, ((1,), (0,)), BF16) for part in left]

    out_own, out_sent = reduce_begin(chips, out_terms, lambda after: after)
    rows_out = reduce_end(out_own, out_sent)
    output = (hidden + valid * rows_out.reshape(seqs, rows, width)).astype(BF16)
    sums.advance([wq_part])
    shared = sums.advance_and_peek()
    shared = sums.advance([], gather_blocks(shared))
    sums.advance([])
    down_1, down_2, gate_1, gate_2, up_1, up_2, wo_sum, _, wq_sum = sums.sums
    shared = shared.reshape(-1, 2 * HEAD).astype(F32)
    gains = shared[width : width + gains.shape[0]].reshape(2, width)
    return (
        output,
        grad_tokens,
        wq_sum.astype(F32).T,
        shared[:width, :HEAD],
        shared[:width, HEAD:],
        wo_sum.astype(F32),
        jnp.concatenate([gate_1, gate_2]).astype(F32).T,
        jnp.concatenate([up_1, up_2]).astype(F32).T,
        jnp.concatenate([down_1, down_2]).astype(F32),
        gains[0],
        gains[1],
    )


def solution(mesh):
    placed = (
        P("dp", "tensor", None),
        P("dp"),
        P(None, "tensor"),
        P(),
        P(),
        P("tensor", None),
        P(None, "tensor"),
        P(None, "tensor"),
        P("tensor", None),
        P(),
        P(),
        P("dp", "tensor", None, None),
        P("dp", "tensor", None),
    )
    return jax.shard_map(
        per_device,
        mesh=mesh,
        in_specs=placed,
        out_specs=(
            P("dp", "tensor", None),
            P("dp", "tensor", None),
            P(None, "tensor"),
            P(),
            P(),
            P("tensor", None),
            P(None, "tensor"),
            P(None, "tensor"),
            P("tensor", None),
            P(),
            P(),
        ),
        check_vma=False,
    )
```

```python
import functools

import jax
import jax.numpy as jnp
from jax import lax
from jax.experimental import pallas as pl
from jax.experimental.pallas import tpu as pltpu
from jax.sharding import PartitionSpec as P

HEAD = 128
KEY_BLOCK = 256
JOIN_COST = 8_000_000_000
BACK_COST = 1
FORTH_COST = 60
SMALL_SHIFT = 1e-05
ROPE_BASE = 10000.0
NEG_FILL = -1e30
LOG2E = 1.4426950408889634
F32 = jnp.float32
BF16 = jnp.bfloat16


def rms_scale(values):
    return lax.rsqrt(jnp.mean(values * values, axis=-1, keepdims=True) + SMALL_SHIFT)


def normed(values, gain_vec):
    return values * rms_scale(values) * gain_vec


def norm_back(values, gain_vec, grad_vals):
    scale_vals = rms_scale(values)
    scaled = grad_vals * gain_vec
    inner_mean = jnp.mean(scaled * values, axis=-1, keepdims=True)
    grad_values = scale_vals * scaled - values * (scale_vals * scale_vals * scale_vals) * inner_mean
    grad_gain = jnp.sum(grad_vals * values * scale_vals, axis=(0, 1))
    return grad_values, grad_gain


def rope_block(start, rows):
    half = HEAD // 2
    frequency = ROPE_BASE ** (-2.0 * jnp.arange(half, dtype=F32) / HEAD)
    angles = (start + jnp.arange(rows)).astype(F32)[:, None] * frequency[None, :]
    cosine, sine = jnp.cos(angles), jnp.sin(angles)
    return jnp.concatenate([cosine, cosine], 1), jnp.concatenate([-sine, sine], 1)


def swap(values, bit):
    n = lax.axis_size("tensor")
    return lax.ppermute(values, "tensor", [(i, i ^ bit) for i in range(n)])


def dot(a, b, dims, out=F32):
    return lax.dot_general(a, b, (dims, ((), ())), preferred_element_type=F32).astype(out)


def add_up(*parts):
    total = parts[0].astype(F32)
    for part in parts[1:]:
        total = total + part.astype(F32)
    return total


def key_branches(start, rows, span, body):
    blocks = span // KEY_BLOCK
    needed = (start + rows + KEY_BLOCK - 1) // KEY_BLOCK
    for count in range(1, blocks + 1):
        pl.when(needed == count)(functools.partial(body, count * KEY_BLOCK))


def stack_heads(values, heads):
    return jnp.concatenate([values[:, h * HEAD : (h + 1) * HEAD] for h in range(heads)], axis=0)


def matmul(a, b, contract):
    return lax.dot_general(a, b, (contract, ((), ())), preferred_element_type=F32)


def masked_scores(keys, query, start, rows, heads, count):
    scores = matmul(keys, query, ((1,), (1,)))
    key_pos = lax.broadcasted_iota(jnp.int32, (KEY_BLOCK, rows), 0) + (count - KEY_BLOCK)
    row_pos = lax.broadcasted_iota(jnp.int32, (KEY_BLOCK, rows), 1) + start
    allowed = key_pos <= row_pos
    last = scores[count - KEY_BLOCK :]
    last = jnp.concatenate(
        [jnp.where(allowed, last[:, h * rows : (h + 1) * rows], NEG_FILL) for h in range(heads)], axis=1
    )
    if count == KEY_BLOCK:
        return last
    return jnp.concatenate([scores[: count - KEY_BLOCK], last], axis=0)


def forward_kernel(
    place, lengths, x0_ref, x1_ref, wq_ref, kv_ref, cos_ref, sin_ref, mixed_ref, query_ref, lse_ref, raw_ref, vt_ref
):
    a, s = pl.program_id(0), pl.program_id(1)
    seqs, span = kv_ref.shape[0], kv_ref.shape[1]
    rows = x0_ref.shape[0] // seqs
    heads = wq_ref.shape[1] // HEAD
    start = place[a] * rows
    here = pl.ds(pl.multiple_of(s * rows, rows), rows)
    live = start < lengths[s]
    factor = HEAD ** (-0.5) * LOG2E

    for k, x_ref in enumerate((x0_ref, x1_ref)):

        @pl.when((a == k) & (s == 0))
        def _(x_ref=x_ref):
            raw_ref[...] = matmul(x_ref[...], wq_ref[...], ((1,), (0,)))

    @pl.when(a == 0)
    def _():
        vt_ref[s] = kv_ref[s, :, HEAD:].T

    pieces = []
    for h in range(heads):
        raw = raw_ref[here, h * HEAD : (h + 1) * HEAD]
        pieces.append((raw * cos_ref[0] + pltpu.roll(raw, HEAD // 2, 1) * sin_ref[0]).astype(BF16))
    query_ref[0, s] = jnp.concatenate(pieces, axis=0)

    def body(count):
        scores = masked_scores(kv_ref[s, :count, :HEAD], query_ref[0, s], start, rows, heads, count)
        top = jnp.max(scores, axis=0, keepdims=True)
        terms = jnp.exp2((scores - top) * factor)
        total = jnp.sum(terms, axis=0, keepdims=True)
        out = matmul(vt_ref[s, :, :count], terms.astype(BF16), ((1,), (0,))) / total
        lse_ref[0, s] = jnp.broadcast_to(top * factor + jnp.log2(total), lse_ref.shape[2:])
        for h in range(heads):
            piece = out[:, h * rows : (h + 1) * rows].T
            mixed_ref[0, here, h * HEAD : (h + 1) * HEAD] = piece.astype(BF16)

    @pl.when(live)
    def _():
        key_branches(start, rows, span, body)

    @pl.when(jnp.logical_not(live))
    def _():
        mixed_ref[0, here] = jnp.zeros((rows, heads * HEAD), BF16)
        lse_ref[0, s] = jnp.zeros(lse_ref.shape[2:], F32)


def whole(shape):
    return pl.BlockSpec(shape, lambda a, *_: (0,) * len(shape))


def blocked(shape):
    return pl.BlockSpec((1, *shape[1:]), lambda a, *_: (a,) + (0,) * (len(shape) - 1))


def attention_forward(place, lengths, parts, query_weights, kv, cosine, sine):
    flat, width = parts[0].shape
    seqs, span = kv.shape[0], kv.shape[1]
    rows, wide = flat // seqs, query_weights.shape[1]
    heads = wide // HEAD
    shapes = [(2, flat, wide), (2, seqs, heads * rows, HEAD), (2, seqs, 8, heads * rows)]
    return pl.pallas_call(
        forward_kernel,
        grid_spec=pltpu.PrefetchScalarGridSpec(
            num_scalar_prefetch=2,
            grid=(2, seqs),
            in_specs=[
                whole(parts[0].shape),
                whole(parts[1].shape),
                whole(query_weights.shape),
                whole(kv.shape),
                blocked(cosine.shape),
                blocked(sine.shape),
            ],
            out_specs=[blocked(shape) for shape in shapes],
            scratch_shapes=[pltpu.VMEM((flat, wide), F32), pltpu.VMEM((seqs, HEAD, span), BF16)],
        ),
        out_shape=[jax.ShapeDtypeStruct(s, t) for s, t in zip(shapes, (BF16, BF16, F32))],
        compiler_params=pltpu.CompilerParams(vmem_limit_bytes=48 * 1024 * 1024),
        cost_estimate=pl.CostEstimate(flops=FORTH_COST * flat * wide * span, bytes_accessed=kv.size, transcendentals=0),
        name="attention_forward",
    )(place, lengths, *parts, query_weights, kv, cosine, sine)


def backward_kernel(
    place, lengths, g0_ref, g1_ref, wo_ref, wq_ref, query_ref, lse_ref, kv_ref, cos_ref, sin_ref,
    gq_ref, in_ref, gkv_ref, gm_ref, kt_ref,
):
    a, s = pl.program_id(0), pl.program_id(1)
    seqs, span = kv_ref.shape[0], kv_ref.shape[1]
    rows = g0_ref.shape[0] // seqs
    heads = wq_ref.shape[1] // HEAD
    start = place[a] * rows
    here = pl.ds(pl.multiple_of(s * rows, rows), rows)
    live = start < lengths[s]
    scale = HEAD ** (-0.5)
    factor = scale * LOG2E

    for k, g_ref in enumerate((g0_ref, g1_ref)):

        @pl.when((a == k) & (s == 0))
        def _(g_ref=g_ref):
            gm_ref[...] = matmul(g_ref[...], wo_ref[...], ((1,), (1,))).astype(BF16)

    @pl.when(a == 0)
    def _():
        gkv_ref[s] = jnp.zeros(gkv_ref.shape[1:], F32)
        kt_ref[s] = kv_ref[s, :, :HEAD].T

    def body(count):
        query = query_ref[0, s]
        grad = stack_heads(gm_ref[here, :], heads)
        scores = masked_scores(kv_ref[s, :count, :HEAD], query, start, rows, heads, count)
        probs = jnp.exp2(scores * factor - lse_ref[0, s, 0:1, :])
        grad_probs = matmul(kv_ref[s, :count, HEAD:], grad, ((1,), (1,)))
        row_dots = jnp.sum(probs * grad_probs, axis=0, keepdims=True)
        grad_scores = (probs * (grad_probs - row_dots)).astype(BF16)
        gkv_ref[s, :count, :HEAD] += scale * matmul(grad_scores, query, ((1,), (0,)))
        gkv_ref[s, :count, HEAD:] += matmul(probs.astype(BF16), grad, ((1,), (0,)))
        grad_query = matmul(kt_ref[s, :, :count], grad_scores, ((1,), (0,)))
        for h in range(heads):
            piece = grad_query[:, h * rows : (h + 1) * rows].T * scale
            piece = piece * cos_ref[0] - pltpu.roll(piece, HEAD // 2, 1) * sin_ref[0]
            gq_ref[0, here, h * HEAD : (h + 1) * HEAD] = piece.astype(BF16)

    @pl.when(live)
    def _():
        key_branches(start, rows, span, body)

    @pl.when(jnp.logical_not(live))
    def _():
        gq_ref[0, here] = jnp.zeros((rows, heads * HEAD), BF16)

    @pl.when(s == seqs - 1)
    def _():
        in_ref[0] = matmul(gq_ref[0], wq_ref[...], ((1,), (1,))).astype(BF16)


def attention_backward(place, lengths, grads, output_weights, query_weights, query, lse, kv, cosine, sine):
    flat, width = grads[0].shape
    seqs, span = kv.shape[0], kv.shape[1]
    wide = query_weights.shape[1]
    operands = (*grads, output_weights, query_weights, query, lse, kv, cosine, sine)
    specs = [whole(v.shape) for v in operands]
    for k in (4, 5, 7, 8):
        specs[k] = blocked(operands[k].shape)
    return pl.pallas_call(
        backward_kernel,
        grid_spec=pltpu.PrefetchScalarGridSpec(
            num_scalar_prefetch=2,
            grid=(2, seqs),
            in_specs=specs,
            out_specs=[blocked((2, flat, wide)), blocked((2, flat, width)), whole(kv.shape)],
            scratch_shapes=[pltpu.VMEM((flat, wide), BF16), pltpu.VMEM((seqs, HEAD, span), BF16)],
        ),
        out_shape=[
            jax.ShapeDtypeStruct((2, flat, wide), BF16),
            jax.ShapeDtypeStruct((2, flat, width), BF16),
            jax.ShapeDtypeStruct(kv.shape, F32),
        ],
        compiler_params=pltpu.CompilerParams(vmem_limit_bytes=56 * 1024 * 1024),
        cost_estimate=pl.CostEstimate(flops=BACK_COST * flat * wide * span, bytes_accessed=kv.size, transcendentals=0),
        name="attention_backward",
    )(place, lengths, *operands)


def join_columns(parts):
    rows, wide = parts[0].shape

    def kernel(*refs):
        for k in range(len(parts)):
            refs[-1][:, k * wide : (k + 1) * wide] = refs[k][...]

    return pl.pallas_call(
        kernel,
        grid=(4,),
        in_specs=[pl.BlockSpec((rows // 4, wide), lambda i: (i, 0)) for _ in parts],
        out_specs=pl.BlockSpec((rows // 4, wide * len(parts)), lambda i: (i, 0)),
        out_shape=jax.ShapeDtypeStruct((rows, wide * len(parts)), parts[0].dtype),
        cost_estimate=pl.CostEstimate(flops=JOIN_COST, bytes_accessed=0, transcendentals=0),
        name="join_columns",
    )(*parts)


def middle_bits(n):
    bits, bit = [], 2
    while bit < n // 2:
        bits.append(bit)
        bit *= 2
    return bits


def gather_middle(values):
    parts = [values]
    for bit in middle_bits(lax.axis_size("tensor")):
        parts = parts + [swap(part, bit) for part in parts]
    return parts


def reduce_middle(parts):
    for bit in reversed(middle_bits(lax.axis_size("tensor"))):
        half = len(parts) // 2
        parts = [add_up(parts[i], swap(parts[half + i].astype(BF16), bit)) for i in range(half)]
    return parts[0]


def sum_of_products(left, right, start=None):
    total = dot(jnp.concatenate(left), jnp.concatenate(right), ((0,), (0,)))
    return total if start is None else start + total


def tie(*values):
    return lax.optimization_barrier(values)


def line_step(outer, own_in, sent_in, fresh, own_across, sent_across):
    rows, width = fresh.shape

    def kernel(outer_ref, a_ref, b_ref, c_ref, d_ref, e_ref, pair_ref, leaving_ref):
        @pl.when(outer_ref[0] == 1)
        def _():
            pair_ref[...] = c_ref[...]
            leaving_ref[...] = c_ref[...]

        @pl.when(outer_ref[0] == 0)
        def _():
            pair_ref[...] = (a_ref[...].astype(F32) + b_ref[...].astype(F32)).astype(BF16)
            leaving_ref[...] = (d_ref[...].astype(F32) + e_ref[...].astype(F32)).astype(BF16)

    steps = 4
    inner_block = pl.BlockSpec((rows, width // steps), lambda i, o: (0, i * (1 - o[0])))
    outer_block = pl.BlockSpec((rows, width // steps), lambda i, o: (0, i * o[0]))
    block = pl.BlockSpec((rows, width // steps), lambda i, o: (0, i))
    return pl.pallas_call(
        kernel,
        grid_spec=pltpu.PrefetchScalarGridSpec(
            num_scalar_prefetch=1,
            grid=(steps,),
            in_specs=[inner_block, inner_block, outer_block, inner_block, inner_block],
            out_specs=[block, block],
        ),
        out_shape=[jax.ShapeDtypeStruct((rows, width), BF16)] * 2,
        name="line_step",
    )(outer.astype(jnp.int32).reshape(1), own_in, sent_in, fresh, own_across, sent_across)


class LineSum:
    def __init__(self):
        self.line = lax.axis_size("dp") == 4
        place = lax.axis_index("dp")
        self.outer = (place == 0) | (place == 3)
        self.inward, self.across, self.outward = [], [], []
        self.sums = []

    def advance(self, arrays, others=()):
        if not self.line:
            self.sums += [lax.psum(a, "dp") for a in arrays]
            return others
        arrays, inward, across, outward, others = tie(
            list(arrays), self.inward, self.across, self.outward, others
        )
        self.inward, self.outward = [], []
        if len(arrays) == 1 and [a.shape for a, _ in inward + across] == [arrays[0].shape] * 2:
            pairs, leaving = line_step(self.outer, *inward[0], arrays[0], *across[0])
            sent = lax.ppermute(leaving, "dp", [(0, 1), (1, 0), (2, 3), (3, 2)])
            self.inward.append((arrays[0], sent))
            self.outward.append((leaving, sent))
            pairs = [pairs]
        else:
            pairs = [add_up(own, sent).astype(BF16) for own, sent in inward]
            totals = [add_up(own, sent).astype(BF16) for own, sent in across]
            self.inward = [(a, lax.ppermute(a, "dp", [(0, 1), (3, 2)])) for a in arrays]
            self.outward = [(a, lax.ppermute(a, "dp", [(1, 0), (2, 3)])) for a in totals]
        self.across = [(a, lax.ppermute(a, "dp", [(1, 2), (2, 1)])) for a in pairs]
        self.sums += [jnp.where(self.outer, sent, own) for own, sent in outward]
        return others


    def advance_and_peek(self):
        self.advance([])
        if not self.line:
            return self.sums[-2]
        own, sent = self.outward[-1]
        return jnp.where(self.outer, sent, own)


def tensor_bits():
    n, bits, bit = lax.axis_size("tensor"), [], 1
    while bit < n:
        bits.append(bit)
        bit *= 2
    return bits


def reduce_blocks(blocks):
    n, me = blocks.shape[0], lax.axis_index("tensor")
    held = [lax.dynamic_index_in_dim(blocks, me ^ r, 0, keepdims=False) for r in range(n)]
    for bit in tensor_bits():
        keep = jnp.stack([held[r] for r in range(len(held)) if r % 2 == 0])
        give = jnp.stack([held[r] for r in range(len(held)) if r % 2 == 1])
        total = add_up(keep, swap(give.astype(BF16), bit))
        held = [total[k] for k in range(total.shape[0])]
    return held[0]


def gather_blocks(block):
    n, me = lax.axis_size("tensor"), lax.axis_index("tensor")
    held = block[None]
    for bit in reversed(tensor_bits()):
        other = swap(held, bit)
        held = jnp.stack([held, other], 1).reshape(2 * held.shape[0], *block.shape)
    result = jnp.zeros_like(held)
    for r in range(n):
        result = lax.dynamic_update_index_in_dim(result, held[r], me ^ r, 0)
    return result


def gather_near(values):
    if lax.axis_size("tensor") != 8:
        return values, values
    return swap(values, 2), swap(values, 4)


def gather_pairs(values):
    parts, bits = [values], tensor_bits()
    for bit in bits:
        parts = parts + [swap(part, bit) for part in parts]
    return [(parts[i], parts[i + 1]) for i in range(0, len(parts), 2)]


def halves(value):
    rows = value.shape[0] // 2
    return value[:rows], value[rows:]


def reduce_begin(count, terms, between):
    n = lax.axis_size("tensor")
    if n != 8:
        parts = []
        for i in range(count):
            own, other = terms(i, None)
            parts.append(add_up(own, swap(other, 1)))
        while len(parts) > 1:
            half = len(parts) // 2
            parts = [add_up(parts[i], swap(parts[half + i].astype(BF16), 2 * half)) for i in range(half)]
        between(parts[0])
        return parts[0], ()
    own_d, other_d = (terms(3, None))
    core_d = swap(other_d, 1)
    own_y, other_y = (terms(2, own_d))
    core_y = swap(other_y, 1)
    diagonal = add_up(own_d, core_d).astype(BF16)
    diagonal, own_y = tie(diagonal, own_y)
    first, second = halves(diagonal)
    from_x, from_y = swap(first, 2), swap(second, 4)
    own_x, other_x = (terms(1, between(diagonal)))
    core_x = swap(other_x, 1)
    own, other = (terms(0, own_x))
    core = swap(other, 1)
    low, high = halves(add_up(own_y, core_y))
    for_y = jnp.concatenate([add_up(low, from_x), high]).astype(BF16)
    low, high = halves(add_up(own_x, core_x))
    for_x = jnp.concatenate([low, add_up(high, from_y)]).astype(BF16)
    return (own, core), (for_x, for_y)


def reduce_end(own, sent):
    if not sent:
        return own
    return add_up(*own, swap(sent[0], 2), swap(sent[1], 4))


def per_device(
    tokens,
    lengths,
    query_weight,
    key_weight,
    value_weight,
    output_weight,
    gate_weight,
    up_weight,
    down_weight,
    gain_attn,
    gain_mlp,
    pair_grad,
    cotangent,
):
    seqs, rows, width = tokens.shape
    n = lax.axis_size("tensor")
    me = lax.axis_index("tensor")
    top = n // 2
    flat = seqs * rows
    local_pos = me * rows + jnp.arange(rows)
    valid = (local_pos[None, :] < lengths[:, None]).astype(F32)[..., None]
    x = tokens.astype(F32)
    attn_gain = gain_attn.astype(F32)
    mlp_gain = gain_mlp.astype(F32)
    grad_y = cotangent.astype(F32)
    kv_weight = jnp.concatenate([key_weight, value_weight], axis=1)

    norm_in = normed(x, attn_gain).astype(BF16).reshape(flat, width)
    far_in = swap(norm_in, top)
    far_in = (far_in, swap(far_in, 1))
    near_in = (norm_in, swap(norm_in, 1))
    def slopes_of(blocks):
        return [dot(block, down_weight, ((1,), (1,))) for block in blocks]

    def with_core(part):
        return part, swap(part, 1)

    grad_out = (valid * grad_y).astype(BF16).reshape(flat, width)
    own_grads = with_core(grad_out)
    own_slopes, query_parts = tie(slopes_of(own_grads), gather_middle(query_weight))
    query_weights = join_columns(query_parts)
    heads_width = query_weights.shape[1]
    own_cos, own_sin = rope_block(me * rows, rows)
    kv_raw = dot(norm_in, kv_weight, ((1,), (0,))).reshape(seqs, rows, 2 * HEAD)
    key_raw = kv_raw[..., :HEAD]
    key_own = key_raw * own_cos + jnp.roll(key_raw, HEAD // 2, axis=-1) * own_sin
    kv_own = jnp.concatenate([key_own, kv_raw[..., HEAD:]], axis=-1).astype(BF16)

    output_weight, kv_own = tie(output_weight, kv_own)
    output_parts = gather_middle(output_weight)
    kv = lax.all_gather(kv_own, "tensor", axis=1, tiled=True)

    def place_of(offset):
        place = jnp.stack([me ^ offset, me ^ (offset + 1)]).astype(jnp.int32)
        blocks = [rope_block(place[i] * rows, rows) for i in range(2)]
        return place, (jnp.stack([b[0] for b in blocks]), jnp.stack([b[1] for b in blocks]))

    def attend(part, place, table):
        return attention_forward(place, lengths, part, query_weights, kv, *table)

    def portions_of(mixed):
        return [dot(mixed[i], output_weights, ((1,), (0,)), BF16) for i in range(2)]

    near_place, near_table = place_of(0)
    far_place, far_table = place_of(top)
    grad_out, _ = tie(grad_out, norm_in)
    grad_far = swap(grad_out, top)
    near_result = attend(near_in, near_place, near_table)
    far_in, _ = tie(far_in, near_result[0])
    far_result = attend(far_in, far_place, far_table)
    output_parts, far_mixed, grad_far = tie(output_parts, far_result[0], grad_far)
    output_weights = jnp.concatenate(output_parts, axis=0)
    far_portions = portions_of(far_mixed)
    for_far = add_up(far_portions[0], swap(far_portions[1], 1)).astype(BF16)
    for_far, near_mixed = tie(for_far, near_result[0])
    from_far = swap(for_far, top)
    near_portions = portions_of(near_mixed)
    near_core = swap(near_portions[1], 1)
    if n == 8:
        grad_out, _ = tie(grad_out, far_mixed)
        grad_side = swap(grad_out, 2)
        size = flat // 2
        from_far, grad_side, grad_far = tie(from_far, grad_side, grad_far)
        grad_diagonal = [swap(grad_side[:size], 4), swap(grad_far[size:], 2)]
    attn_out = add_up(near_portions[0], near_core, from_far)
    hidden = x + valid * attn_out.reshape(seqs, rows, width)

    chips = n // 2
    norm_mid = normed(hidden, mlp_gain).astype(BF16).reshape(flat, width)
    gate_rows, up_rows = gate_weight.T, up_weight.T

    mids, acts, g_gates, g_ups = [], [], [], []

    def forward_blocks(blocks, slopes):
        for mid, slope in zip(blocks, slopes):
            gate = dot(mid, gate_rows, ((1,), (1,)))
            up = dot(mid, up_rows, ((1,), (1,)))
            sig = 1.0 / (1.0 + jnp.exp(-gate))
            silu = gate * sig
            mids.append(mid)
            acts.append((silu * up).astype(BF16))
            g_gates.append((slope * up * sig * (1.0 + gate * (1.0 - sig))).astype(BF16))
            g_ups.append((slope * silu).astype(BF16))

    def diagonal_blocks(parts):
        return [jnp.concatenate(p) for p in zip(*[with_core(part) for part in parts])]

    if n == 8:
        at_x, at_y = gather_near(norm_mid)
        grads = [*own_grads, *with_core(grad_side), *with_core(grad_far)]
        slopes = own_slopes + slopes_of(grads[2:])
        forward_blocks(with_core(norm_mid), slopes[:2])
        at_x, at_y, slopes, acts[1] = tie(at_x, at_y, slopes, acts[1])
        diagonal = [swap(at_x[:size], 4), swap(at_y[size:], 2)]
        forward_blocks((*with_core(at_x), *with_core(at_y)), slopes[2:6])
        grad_down = sum_of_products(acts[:6], grads[:6])
        diagonal, grad_diagonal, grad_down = tie(diagonal, grad_diagonal, grad_down)
        grads += diagonal_blocks(grad_diagonal)
        forward_blocks(diagonal_blocks(diagonal), slopes_of(grads[6:]))
    else:
        grads = [block for pair in gather_pairs(grad_out) for block in pair]
        forward_blocks([block for pair in gather_pairs(norm_mid) for block in pair], slopes_of(grads))
        grad_down = sum_of_products(acts[:-2], grads[:-2])

    def mid_term(r):
        terms = dot(g_gates[r], gate_rows, ((1,), (0,))) + dot(g_ups[r], up_rows, ((1,), (0,)))
        return terms.astype(BF16)

    def mid_terms(i, after):
        for k in (2 * i, 2 * i + 1):
            if after is not None:
                g_gates[k], g_ups[k], _ = tie(g_gates[k], g_ups[k], after)
        return mid_term(2 * i), mid_term(2 * i + 1)

    sums, down_parts = LineSum(), []

    def down_gradient(after):
        last, after = tie(acts[-2:], after)
        down_parts.extend(halves(sum_of_products(last, grads[-2:], grad_down).astype(BF16)))
        return sums.advance([down_parts[0]], after)

    mid_own, mid_sent = reduce_begin(chips, mid_terms, down_gradient)
    grad_mid = reduce_end(mid_own, mid_sent).reshape(seqs, rows, width)

    g_gates, g_ups, mids = sums.advance([down_parts[1]], (g_gates, g_ups, mids))
    mid_all = [jnp.concatenate(mids)]
    grad_gate = halves(sum_of_products(g_gates, mid_all).astype(BF16))
    back, mlp_gain_part = norm_back(hidden, mlp_gain, grad_mid)
    grad_hidden = grad_y + back
    grad_attn = (valid * grad_hidden).astype(BF16).reshape(flat, width)
    far_grad = swap(grad_attn, top)
    near_grad = (grad_attn, swap(grad_attn, 1))

    def attend_back(part, result, place, table):
        return attention_backward(
            place, lengths, part, output_weights, query_weights, result[1], result[2], kv, *table
        )

    def product(left, right):
        return dot(jnp.concatenate(left), jnp.concatenate(right), ((0,), (0,)), BF16)

    g_ups, near_grad = sums.advance([grad_gate[0]], (g_ups, near_grad))
    grad_up = halves(sum_of_products(g_ups, mid_all).astype(BF16))
    near_q, near_terms, near_kv = attend_back(near_grad, near_result, near_place, near_table)
    near_core = swap(near_terms[1], 1)

    far_grad, near_q, near_kv = sums.advance([grad_gate[1]], (far_grad, near_q, near_kv))
    far_grad = (far_grad, swap(far_grad, 1))
    far_q, far_terms, far_kv = attend_back(far_grad, far_result, far_place, far_table)
    for_far = add_up(far_terms[0], swap(far_terms[1], 1)).astype(BF16)
    from_far = swap(for_far, top)

    far_grad, far_q, far_kv = sums.advance([grad_up[0]], (far_grad, far_q, far_kv))
    unit = output_weight.shape[0]
    kv_blocks = (near_kv + far_kv).astype(BF16).reshape(seqs, n, rows, 2 * HEAD).swapaxes(0, 1)
    kv_sum = reduce_blocks(kv_blocks)
    mixed = [r[0][i] for r in (near_result, far_result) for i in range(2)]
    wo_full = product(mixed, [*near_grad, *far_grad])
    wo_full, kv_sum = tie(wo_full, kv_sum)
    wo_part = reduce_middle([wo_full[i * unit : (i + 1) * unit] for i in range(heads_width // unit)])
    wo_part = wo_part.astype(BF16)
    key_grad = kv_sum[..., :HEAD]
    key_grad = key_grad * own_cos - jnp.roll(key_grad, HEAD // 2, axis=-1) * own_sin
    kv_grad = jnp.concatenate([key_grad, kv_sum[..., HEAD:]], -1).astype(BF16).reshape(flat, 2 * HEAD)

    from_far, far_q, kv_grad = sums.advance([grad_up[1]], (from_far, far_q, kv_grad))
    grad_in = add_up(near_terms[0], near_core, from_far)
    grad_in = grad_in + dot(kv_grad, kv_weight, ((1,), (1,)))
    kv_portion = dot(norm_in, kv_grad, ((0,), (0,)))
    back, attn_gain_part = norm_back(x, attn_gain, grad_in.reshape(seqs, rows, width))
    grad_tokens = grad_hidden + back
    gains = jnp.concatenate([attn_gain_part, mlp_gain_part]).reshape(-1, 2 * HEAD)
    shared = jnp.concatenate([kv_portion + pair_grad[0, 0], gains])
    shared = jnp.pad(shared, ((0, -shared.shape[0] % (16 * n)), (0, 0))).astype(BF16)
    shared = reduce_blocks(shared.reshape(n, -1, 2 * HEAD)).astype(BF16)


    wq_full = product([near_q[0], near_q[1], far_q[0], far_q[1]], [*near_in, *far_in])
    wq_full, shared = tie(wq_full, shared)
    wq_part = reduce_middle([wq_full[i * unit : (i + 1) * unit] for i in range(heads_width // unit)])
    wq_part = wq_part.astype(BF16)

    acts = sums.advance([wo_part, shared], acts)

    def out_terms(i, after):
        left = acts[2 * i : 2 * i + 2]
        left = left if after is None else tie(left, after)[0]
        return [dot(part, down_weight, ((1,), (0,)), BF16) for part in left]

    out_own, out_sent = reduce_begin(chips, out_terms, lambda after: after)
    rows_out = reduce_end(out_own, out_sent)
    output = (hidden + valid * rows_out.reshape(seqs, rows, width)).astype(BF16)
    sums.advance([wq_part])
    shared = sums.advance_and_peek()
    shared = sums.advance([], gather_blocks(shared))
    sums.advance([])
    down_1, down_2, gate_1, gate_2, up_1, up_2, wo_sum, _, wq_sum = sums.sums
    shared = shared.reshape(-1, 2 * HEAD).astype(F32)
    gains = shared[width : width + gains.shape[0]].reshape(2, width)
    return (
        output,
        grad_tokens,
        wq_sum.astype(F32).T,
        shared[:width, :HEAD],
        shared[:width, HEAD:],
        wo_sum.astype(F32),
        jnp.concatenate([gate_1, gate_2]).astype(F32).T,
        jnp.concatenate([up_1, up_2]).astype(F32).T,
        jnp.concatenate([down_1, down_2]).astype(F32),
        gains[0],
        gains[1],
    )


def solution(mesh):
    placed = (
        P("dp", "tensor", None),
        P("dp"),
        P(None, "tensor"),
        P(),
        P(),
        P("tensor", None),
        P(None, "tensor"),
        P(None, "tensor"),
        P("tensor", None),
        P(),
        P(),
        P("dp", "tensor", None, None),
        P("dp", "tensor", None),
    )
    return jax.shard_map(
        per_device,
        mesh=mesh,
        in_specs=placed,
        out_specs=(
            P("dp", "tensor", None),
            P("dp", "tensor", None),
            P(None, "tensor"),
            P(),
            P(),
            P("tensor", None),
            P(None, "tensor"),
            P(None, "tensor"),
            P("tensor", None),
            P(),
            P(),
        ),
        check_vma=False,
    )
```

```python
import functools

import jax
import jax.numpy as jnp
from jax import lax
from jax.experimental import pallas as pl
from jax.experimental.pallas import tpu as pltpu
from jax.sharding import PartitionSpec as P

HEAD = 128
KEY_BLOCK = 256
JOIN_COST = 8_000_000_000
BACK_COST = 1
FORTH_COST = 60
SMALL_SHIFT = 1e-05
ROPE_BASE = 10000.0
NEG_FILL = -1e30
LOG2E = 1.4426950408889634
F32 = jnp.float32
BF16 = jnp.bfloat16


def rms_scale(values):
    return lax.rsqrt(jnp.mean(values * values, axis=-1, keepdims=True) + SMALL_SHIFT)


def normed(values, gain_vec):
    return values * rms_scale(values) * gain_vec


def norm_back(values, gain_vec, grad_vals):
    scale_vals = rms_scale(values)
    scaled = grad_vals * gain_vec
    inner_mean = jnp.mean(scaled * values, axis=-1, keepdims=True)
    grad_values = scale_vals * scaled - values * (scale_vals * scale_vals * scale_vals) * inner_mean
    grad_gain = jnp.sum(grad_vals * values * scale_vals, axis=(0, 1))
    return grad_values, grad_gain


def rope_block(start, rows):
    half = HEAD // 2
    frequency = ROPE_BASE ** (-2.0 * jnp.arange(half, dtype=F32) / HEAD)
    angles = (start + jnp.arange(rows)).astype(F32)[:, None] * frequency[None, :]
    cosine, sine = jnp.cos(angles), jnp.sin(angles)
    return jnp.concatenate([cosine, cosine], 1), jnp.concatenate([-sine, sine], 1)


def swap(values, bit):
    n = lax.axis_size("tensor")
    return lax.ppermute(values, "tensor", [(i, i ^ bit) for i in range(n)])


def dot(a, b, dims, out=F32):
    return lax.dot_general(a, b, (dims, ((), ())), preferred_element_type=F32).astype(out)


def add_up(*parts):
    total = parts[0].astype(F32)
    for part in parts[1:]:
        total = total + part.astype(F32)
    return total


def key_branches(start, rows, span, body):
    blocks = span // KEY_BLOCK
    needed = (start + rows + KEY_BLOCK - 1) // KEY_BLOCK
    for count in range(1, blocks + 1):
        pl.when(needed == count)(functools.partial(body, count * KEY_BLOCK))


def stack_heads(values, heads):
    return jnp.concatenate([values[:, h * HEAD : (h + 1) * HEAD] for h in range(heads)], axis=0)


def matmul(a, b, contract):
    return lax.dot_general(a, b, (contract, ((), ())), preferred_element_type=F32)


def masked_scores(keys, query, start, rows, heads, count):
    scores = matmul(keys, query, ((1,), (1,)))
    key_pos = lax.broadcasted_iota(jnp.int32, (KEY_BLOCK, rows), 0) + (count - KEY_BLOCK)
    row_pos = lax.broadcasted_iota(jnp.int32, (KEY_BLOCK, rows), 1) + start
    allowed = key_pos <= row_pos
    last = scores[count - KEY_BLOCK :]
    last = jnp.concatenate(
        [jnp.where(allowed, last[:, h * rows : (h + 1) * rows], NEG_FILL) for h in range(heads)], axis=1
    )
    if count == KEY_BLOCK:
        return last
    return jnp.concatenate([scores[: count - KEY_BLOCK], last], axis=0)


def forward_kernel(
    place, lengths, x0_ref, x1_ref, wq_ref, kv_ref, cos_ref, sin_ref, mixed_ref, query_ref, lse_ref, raw_ref, vt_ref
):
    a, s = pl.program_id(0), pl.program_id(1)
    seqs, span = kv_ref.shape[0], kv_ref.shape[1]
    rows = x0_ref.shape[0] // seqs
    heads = wq_ref.shape[1] // HEAD
    start = place[a] * rows
    here = pl.ds(pl.multiple_of(s * rows, rows), rows)
    live = start < lengths[s]
    factor = HEAD ** (-0.5) * LOG2E

    for k, x_ref in enumerate((x0_ref, x1_ref)):

        @pl.when((a == k) & (s == 0))
        def _(x_ref=x_ref):
            raw_ref[...] = matmul(x_ref[...], wq_ref[...], ((1,), (0,)))

    @pl.when(a == 0)
    def _():
        vt_ref[s] = kv_ref[s, :, HEAD:].T

    pieces = []
    for h in range(heads):
        raw = raw_ref[here, h * HEAD : (h + 1) * HEAD]
        pieces.append((raw * cos_ref[0] + pltpu.roll(raw, HEAD // 2, 1) * sin_ref[0]).astype(BF16))
    query_ref[0, s] = jnp.concatenate(pieces, axis=0)

    def body(count):
        scores = masked_scores(kv_ref[s, :count, :HEAD], query_ref[0, s], start, rows, heads, count)
        top = jnp.max(scores, axis=0, keepdims=True)
        terms = jnp.exp2((scores - top) * factor)
        total = jnp.sum(terms, axis=0, keepdims=True)
        out = matmul(vt_ref[s, :, :count], terms.astype(BF16), ((1,), (0,))) / total
        lse_ref[0, s] = jnp.broadcast_to(top * factor + jnp.log2(total), lse_ref.shape[2:])
        for h in range(heads):
            piece = out[:, h * rows : (h + 1) * rows].T
            mixed_ref[0, here, h * HEAD : (h + 1) * HEAD] = piece.astype(BF16)

    @pl.when(live)
    def _():
        key_branches(start, rows, span, body)

    @pl.when(jnp.logical_not(live))
    def _():
        mixed_ref[0, here] = jnp.zeros((rows, heads * HEAD), BF16)
        lse_ref[0, s] = jnp.zeros(lse_ref.shape[2:], F32)


def whole(shape):
    return pl.BlockSpec(shape, lambda a, *_: (0,) * len(shape))


def blocked(shape):
    return pl.BlockSpec((1, *shape[1:]), lambda a, *_: (a,) + (0,) * (len(shape) - 1))


def attention_forward(place, lengths, parts, query_weights, kv, cosine, sine):
    flat, width = parts[0].shape
    seqs, span = kv.shape[0], kv.shape[1]
    rows, wide = flat // seqs, query_weights.shape[1]
    heads = wide // HEAD
    shapes = [(2, flat, wide), (2, seqs, heads * rows, HEAD), (2, seqs, 8, heads * rows)]
    return pl.pallas_call(
        forward_kernel,
        grid_spec=pltpu.PrefetchScalarGridSpec(
            num_scalar_prefetch=2,
            grid=(2, seqs),
            in_specs=[
                whole(parts[0].shape),
                whole(parts[1].shape),
                whole(query_weights.shape),
                whole(kv.shape),
                blocked(cosine.shape),
                blocked(sine.shape),
            ],
            out_specs=[blocked(shape) for shape in shapes],
            scratch_shapes=[pltpu.VMEM((flat, wide), F32), pltpu.VMEM((seqs, HEAD, span), BF16)],
        ),
        out_shape=[jax.ShapeDtypeStruct(s, t) for s, t in zip(shapes, (BF16, BF16, F32))],
        compiler_params=pltpu.CompilerParams(vmem_limit_bytes=48 * 1024 * 1024),
        cost_estimate=pl.CostEstimate(flops=FORTH_COST * flat * wide * span, bytes_accessed=kv.size, transcendentals=0),
        name="attention_forward",
    )(place, lengths, *parts, query_weights, kv, cosine, sine)


def backward_kernel(
    place, lengths, g0_ref, g1_ref, wo_ref, wq_ref, query_ref, lse_ref, kv_ref, cos_ref, sin_ref,
    gq_ref, in_ref, gkv_ref, gm_ref, kt_ref,
):
    a, s = pl.program_id(0), pl.program_id(1)
    seqs, span = kv_ref.shape[0], kv_ref.shape[1]
    rows = g0_ref.shape[0] // seqs
    heads = wq_ref.shape[1] // HEAD
    start = place[a] * rows
    here = pl.ds(pl.multiple_of(s * rows, rows), rows)
    live = start < lengths[s]
    scale = HEAD ** (-0.5)
    factor = scale * LOG2E

    for k, g_ref in enumerate((g0_ref, g1_ref)):

        @pl.when((a == k) & (s == 0))
        def _(g_ref=g_ref):
            gm_ref[...] = matmul(g_ref[...], wo_ref[...], ((1,), (1,))).astype(BF16)

    @pl.when(a == 0)
    def _():
        gkv_ref[s] = jnp.zeros(gkv_ref.shape[1:], F32)
        kt_ref[s] = kv_ref[s, :, :HEAD].T

    def body(count):
        query = query_ref[0, s]
        grad = stack_heads(gm_ref[here, :], heads)
        scores = masked_scores(kv_ref[s, :count, :HEAD], query, start, rows, heads, count)
        probs = jnp.exp2(scores * factor - lse_ref[0, s, 0:1, :])
        grad_probs = matmul(kv_ref[s, :count, HEAD:], grad, ((1,), (1,)))
        row_dots = jnp.sum(probs * grad_probs, axis=0, keepdims=True)
        grad_scores = (probs * (grad_probs - row_dots)).astype(BF16)
        gkv_ref[s, :count, :HEAD] += scale * matmul(grad_scores, query, ((1,), (0,)))
        gkv_ref[s, :count, HEAD:] += matmul(probs.astype(BF16), grad, ((1,), (0,)))
        grad_query = matmul(kt_ref[s, :, :count], grad_scores, ((1,), (0,)))
        for h in range(heads):
            piece = grad_query[:, h * rows : (h + 1) * rows].T * scale
            piece = piece * cos_ref[0] - pltpu.roll(piece, HEAD // 2, 1) * sin_ref[0]
            gq_ref[0, here, h * HEAD : (h + 1) * HEAD] = piece.astype(BF16)

    @pl.when(live)
    def _():
        key_branches(start, rows, span, body)

    @pl.when(jnp.logical_not(live))
    def _():
        gq_ref[0, here] = jnp.zeros((rows, heads * HEAD), BF16)

    @pl.when(s == seqs - 1)
    def _():
        in_ref[0] = matmul(gq_ref[0], wq_ref[...], ((1,), (1,))).astype(BF16)


def attention_backward(place, lengths, grads, output_weights, query_weights, query, lse, kv, cosine, sine):
    flat, width = grads[0].shape
    seqs, span = kv.shape[0], kv.shape[1]
    wide = query_weights.shape[1]
    operands = (*grads, output_weights, query_weights, query, lse, kv, cosine, sine)
    specs = [whole(v.shape) for v in operands]
    for k in (4, 5, 7, 8):
        specs[k] = blocked(operands[k].shape)
    return pl.pallas_call(
        backward_kernel,
        grid_spec=pltpu.PrefetchScalarGridSpec(
            num_scalar_prefetch=2,
            grid=(2, seqs),
            in_specs=specs,
            out_specs=[blocked((2, flat, wide)), blocked((2, flat, width)), whole(kv.shape)],
            scratch_shapes=[pltpu.VMEM((flat, wide), BF16), pltpu.VMEM((seqs, HEAD, span), BF16)],
        ),
        out_shape=[
            jax.ShapeDtypeStruct((2, flat, wide), BF16),
            jax.ShapeDtypeStruct((2, flat, width), BF16),
            jax.ShapeDtypeStruct(kv.shape, F32),
        ],
        compiler_params=pltpu.CompilerParams(vmem_limit_bytes=56 * 1024 * 1024),
        cost_estimate=pl.CostEstimate(flops=BACK_COST * flat * wide * span, bytes_accessed=kv.size, transcendentals=0),
        name="attention_backward",
    )(place, lengths, *operands)


def join_columns(parts):
    rows, wide = parts[0].shape

    def kernel(*refs):
        for k in range(len(parts)):
            refs[-1][:, k * wide : (k + 1) * wide] = refs[k][...]

    return pl.pallas_call(
        kernel,
        grid=(4,),
        in_specs=[pl.BlockSpec((rows // 4, wide), lambda i: (i, 0)) for _ in parts],
        out_specs=pl.BlockSpec((rows // 4, wide * len(parts)), lambda i: (i, 0)),
        out_shape=jax.ShapeDtypeStruct((rows, wide * len(parts)), parts[0].dtype),
        cost_estimate=pl.CostEstimate(flops=JOIN_COST, bytes_accessed=0, transcendentals=0),
        name="join_columns",
    )(*parts)


def middle_bits(n):
    bits, bit = [], 2
    while bit < n // 2:
        bits.append(bit)
        bit *= 2
    return bits


def gather_middle(values):
    parts = [values]
    for bit in middle_bits(lax.axis_size("tensor")):
        parts = parts + [swap(part, bit) for part in parts]
    return parts


def reduce_middle(parts):
    for bit in reversed(middle_bits(lax.axis_size("tensor"))):
        half = len(parts) // 2
        parts = [add_up(parts[i], swap(parts[half + i].astype(BF16), bit)) for i in range(half)]
    return parts[0]


def sum_of_products(left, right, start=None):
    total = dot(jnp.concatenate(left), jnp.concatenate(right), ((0,), (0,)))
    return total if start is None else start + total


def tie(*values):
    return lax.optimization_barrier(values)


def line_step(outer, own_in, sent_in, fresh, own_across, sent_across):
    rows, width = fresh.shape

    def kernel(outer_ref, a_ref, b_ref, c_ref, d_ref, e_ref, pair_ref, leaving_ref):
        @pl.when(outer_ref[0] == 1)
        def _():
            pair_ref[...] = c_ref[...]
            leaving_ref[...] = c_ref[...]

        @pl.when(outer_ref[0] == 0)
        def _():
            pair_ref[...] = (a_ref[...].astype(F32) + b_ref[...].astype(F32)).astype(BF16)
            leaving_ref[...] = (d_ref[...].astype(F32) + e_ref[...].astype(F32)).astype(BF16)

    steps = 4
    inner_block = pl.BlockSpec((rows, width // steps), lambda i, o: (0, i * (1 - o[0])))
    outer_block = pl.BlockSpec((rows, width // steps), lambda i, o: (0, i * o[0]))
    block = pl.BlockSpec((rows, width // steps), lambda i, o: (0, i))
    return pl.pallas_call(
        kernel,
        grid_spec=pltpu.PrefetchScalarGridSpec(
            num_scalar_prefetch=1,
            grid=(steps,),
            in_specs=[inner_block, inner_block, outer_block, inner_block, inner_block],
            out_specs=[block, block],
        ),
        out_shape=[jax.ShapeDtypeStruct((rows, width), BF16)] * 2,
        name="line_step",
    )(outer.astype(jnp.int32).reshape(1), own_in, sent_in, fresh, own_across, sent_across)


class LineSum:
    def __init__(self):
        self.line = lax.axis_size("dp") == 4
        place = lax.axis_index("dp")
        self.outer = (place == 0) | (place == 3)
        self.inward, self.across, self.outward = [], [], []
        self.sums = []

    def advance(self, arrays, others=()):
        if not self.line:
            self.sums += [lax.psum(a, "dp") for a in arrays]
            return others
        arrays, inward, across, outward, others = tie(
            list(arrays), self.inward, self.across, self.outward, others
        )
        self.inward, self.outward = [], []
        if len(arrays) == 1 and [a.shape for a, _ in inward + across] == [arrays[0].shape] * 2:
            pairs, leaving = line_step(self.outer, *inward[0], arrays[0], *across[0])
            sent = lax.ppermute(leaving, "dp", [(0, 1), (1, 0), (2, 3), (3, 2)])
            self.inward.append((arrays[0], sent))
            self.outward.append((leaving, sent))
            pairs = [pairs]
        else:
            pairs = [add_up(own, sent).astype(BF16) for own, sent in inward]
            totals = [add_up(own, sent).astype(BF16) for own, sent in across]
            self.inward = [(a, lax.ppermute(a, "dp", [(0, 1), (3, 2)])) for a in arrays]
            self.outward = [(a, lax.ppermute(a, "dp", [(1, 0), (2, 3)])) for a in totals]
        self.across = [(a, lax.ppermute(a, "dp", [(1, 2), (2, 1)])) for a in pairs]
        self.sums += [jnp.where(self.outer, sent, own) for own, sent in outward]
        return others


    def advance_and_peek(self):
        self.advance([])
        if not self.line:
            return self.sums[-2]
        own, sent = self.outward[-1]
        return jnp.where(self.outer, sent, own)


def tensor_bits():
    n, bits, bit = lax.axis_size("tensor"), [], 1
    while bit < n:
        bits.append(bit)
        bit *= 2
    return bits


def reduce_blocks(blocks):
    n, me = blocks.shape[0], lax.axis_index("tensor")
    held = [lax.dynamic_index_in_dim(blocks, me ^ r, 0, keepdims=False) for r in range(n)]
    for bit in tensor_bits():
        keep = jnp.stack([held[r] for r in range(len(held)) if r % 2 == 0])
        give = jnp.stack([held[r] for r in range(len(held)) if r % 2 == 1])
        total = add_up(keep, swap(give.astype(BF16), bit))
        held = [total[k] for k in range(total.shape[0])]
    return held[0]


def gather_blocks(block):
    n, me = lax.axis_size("tensor"), lax.axis_index("tensor")
    held = block[None]
    for bit in reversed(tensor_bits()):
        other = swap(held, bit)
        held = jnp.stack([held, other], 1).reshape(2 * held.shape[0], *block.shape)
    result = jnp.zeros_like(held)
    for r in range(n):
        result = lax.dynamic_update_index_in_dim(result, held[r], me ^ r, 0)
    return result


def gather_near(values):
    if lax.axis_size("tensor") != 8:
        return values, values
    return swap(values, 2), swap(values, 4)


def gather_pairs(values):
    parts, bits = [values], tensor_bits()
    for bit in bits:
        parts = parts + [swap(part, bit) for part in parts]
    return [(parts[i], parts[i + 1]) for i in range(0, len(parts), 2)]


def halves(value):
    rows = value.shape[0] // 2
    return value[:rows], value[rows:]


def reduce_begin(count, terms, between):
    n = lax.axis_size("tensor")
    if n != 8:
        parts = []
        for i in range(count):
            own, other = terms(i, None)
            parts.append(add_up(own, swap(other, 1)))
        while len(parts) > 1:
            half = len(parts) // 2
            parts = [add_up(parts[i], swap(parts[half + i].astype(BF16), 2 * half)) for i in range(half)]
        between(parts[0])
        return parts[0], ()
    own_d, other_d = (terms(3, None))
    core_d = swap(other_d, 1)
    own_y, other_y = (terms(2, own_d))
    core_y = swap(other_y, 1)
    diagonal = add_up(own_d, core_d).astype(BF16)
    diagonal, own_y = tie(diagonal, own_y)
    first, second = halves(diagonal)
    from_x, from_y = swap(first, 2), swap(second, 4)
    own_x, other_x = (terms(1, between(diagonal)))
    core_x = swap(other_x, 1)
    own, other = (terms(0, own_x))
    core = swap(other, 1)
    low, high = halves(add_up(own_y, core_y))
    for_y = jnp.concatenate([add_up(low, from_x), high]).astype(BF16)
    low, high = halves(add_up(own_x, core_x))
    for_x = jnp.concatenate([low, add_up(high, from_y)]).astype(BF16)
    return (own, core), (for_x, for_y)


def reduce_end(own, sent):
    if not sent:
        return own
    return add_up(*own, swap(sent[0], 2), swap(sent[1], 4))


def per_device(
    tokens,
    lengths,
    query_weight,
    key_weight,
    value_weight,
    output_weight,
    gate_weight,
    up_weight,
    down_weight,
    gain_attn,
    gain_mlp,
    pair_grad,
    cotangent,
):
    seqs, rows, width = tokens.shape
    n = lax.axis_size("tensor")
    me = lax.axis_index("tensor")
    top = n // 2
    flat = seqs * rows
    local_pos = me * rows + jnp.arange(rows)
    valid = (local_pos[None, :] < lengths[:, None]).astype(F32)[..., None]
    x = tokens.astype(F32)
    attn_gain = gain_attn.astype(F32)
    mlp_gain = gain_mlp.astype(F32)
    grad_y = cotangent.astype(F32)
    kv_weight = jnp.concatenate([key_weight, value_weight], axis=1)

    norm_in = normed(x, attn_gain).astype(BF16).reshape(flat, width)
    far_in = swap(norm_in, top)
    far_in = (far_in, swap(far_in, 1))
    near_in = (norm_in, swap(norm_in, 1))
    def slopes_of(blocks):
        return [dot(block, down_weight, ((1,), (1,))) for block in blocks]

    def with_core(part):
        return part, swap(part, 1)

    grad_out = (valid * grad_y).astype(BF16).reshape(flat, width)
    own_grads = with_core(grad_out)
    own_slopes, query_parts = tie(slopes_of(own_grads), gather_middle(query_weight))
    query_weights = join_columns(query_parts)
    heads_width = query_weights.shape[1]
    own_cos, own_sin = rope_block(me * rows, rows)
    kv_raw = dot(norm_in, kv_weight, ((1,), (0,))).reshape(seqs, rows, 2 * HEAD)
    key_raw = kv_raw[..., :HEAD]
    key_own = key_raw * own_cos + jnp.roll(key_raw, HEAD // 2, axis=-1) * own_sin
    kv_own = jnp.concatenate([key_own, kv_raw[..., HEAD:]], axis=-1).astype(BF16)

    output_weight, kv_own = tie(output_weight, kv_own)
    output_parts = gather_middle(output_weight)
    kv = lax.all_gather(kv_own, "tensor", axis=1, tiled=True)

    def place_of(offset):
        place = jnp.stack([me ^ offset, me ^ (offset + 1)]).astype(jnp.int32)
        blocks = [rope_block(place[i] * rows, rows) for i in range(2)]
        return place, (jnp.stack([b[0] for b in blocks]), jnp.stack([b[1] for b in blocks]))

    def attend(part, place, table):
        return attention_forward(place, lengths, part, query_weights, kv, *table)

    def portions_of(mixed):
        return [dot(mixed[i], output_weights, ((1,), (0,)), BF16) for i in range(2)]

    near_place, near_table = place_of(0)
    far_place, far_table = place_of(top)
    grad_out, _ = tie(grad_out, norm_in)
    grad_far = swap(grad_out, top)
    near_result = attend(near_in, near_place, near_table)
    far_in, _ = tie(far_in, near_result[0])
    far_result = attend(far_in, far_place, far_table)
    output_parts, far_mixed, grad_far = tie(output_parts, far_result[0], grad_far)
    output_weights = jnp.concatenate(output_parts, axis=0)
    far_portions = portions_of(far_mixed)
    for_far = add_up(far_portions[0], swap(far_portions[1], 1)).astype(BF16)
    for_far, near_mixed = tie(for_far, near_result[0])
    from_far = swap(for_far, top)
    near_portions = portions_of(near_mixed)
    near_core = swap(near_portions[1], 1)
    if n == 8:
        grad_out, _ = tie(grad_out, far_mixed)
        grad_side = swap(grad_out, 2)
        size = flat // 2
        from_far, grad_side, grad_far = tie(from_far, grad_side, grad_far)
        grad_diagonal = [swap(grad_side[:size], 4), swap(grad_far[size:], 2)]
    attn_out = add_up(near_portions[0], near_core, from_far)
    hidden = x + valid * attn_out.reshape(seqs, rows, width)

    chips = n // 2
    norm_mid = normed(hidden, mlp_gain).astype(BF16).reshape(flat, width)
    gate_rows, up_rows = gate_weight.T, up_weight.T

    mids, acts, g_gates, g_ups = [], [], [], []

    def forward_blocks(blocks, slopes):
        for mid, slope in zip(blocks, slopes):
            gate = dot(mid, gate_rows, ((1,), (1,)))
            up = dot(mid, up_rows, ((1,), (1,)))
            sig = 1.0 / (1.0 + jnp.exp(-gate))
            silu = gate * sig
            mids.append(mid)
            acts.append((silu * up).astype(BF16))
            g_gates.append((slope * up * sig * (1.0 + gate * (1.0 - sig))).astype(BF16))
            g_ups.append((slope * silu).astype(BF16))

    def diagonal_blocks(parts):
        return [jnp.concatenate(p) for p in zip(*[with_core(part) for part in parts])]

    if n == 8:
        at_x, at_y = gather_near(norm_mid)
        grads = [*own_grads, *with_core(grad_side), *with_core(grad_far)]
        slopes = own_slopes + slopes_of(grads[2:])
        forward_blocks(with_core(norm_mid), slopes[:2])
        at_x, at_y, slopes, acts[1] = tie(at_x, at_y, slopes, acts[1])
        diagonal = [swap(at_x[:size], 4), swap(at_y[size:], 2)]
        forward_blocks((*with_core(at_x), *with_core(at_y)), slopes[2:6])
        grad_down = sum_of_products(acts[:6], grads[:6])
        diagonal, grad_diagonal, grad_down = tie(diagonal, grad_diagonal, grad_down)
        grads += diagonal_blocks(grad_diagonal)
        forward_blocks(diagonal_blocks(diagonal), slopes_of(grads[6:]))
    else:
        grads = [block for pair in gather_pairs(grad_out) for block in pair]
        forward_blocks([block for pair in gather_pairs(norm_mid) for block in pair], slopes_of(grads))
        grad_down = sum_of_products(acts[:-2], grads[:-2])

    def mid_term(r):
        terms = dot(g_gates[r], gate_rows, ((1,), (0,))) + dot(g_ups[r], up_rows, ((1,), (0,)))
        return terms.astype(BF16)

    def mid_terms(i, after):
        for k in (2 * i, 2 * i + 1):
            if after is not None:
                g_gates[k], g_ups[k], _ = tie(g_gates[k], g_ups[k], after)
        return mid_term(2 * i), mid_term(2 * i + 1)

    sums, down_parts = LineSum(), []

    def down_gradient(after):
        last, after = tie(acts[-2:], after)
        down_parts.extend(halves(sum_of_products(last, grads[-2:], grad_down).astype(BF16)))
        return sums.advance([down_parts[0]], after)

    mid_own, mid_sent = reduce_begin(chips, mid_terms, down_gradient)
    grad_mid = reduce_end(mid_own, mid_sent).reshape(seqs, rows, width)

    g_gates, g_ups, mids = sums.advance([down_parts[1]], (g_gates, g_ups, mids))
    mid_all = [jnp.concatenate(mids)]
    grad_gate = halves(sum_of_products(g_gates, mid_all).astype(BF16))
    back, mlp_gain_part = norm_back(hidden, mlp_gain, grad_mid)
    grad_hidden = grad_y + back
    grad_attn = (valid * grad_hidden).astype(BF16).reshape(flat, width)
    far_grad = swap(grad_attn, top)
    near_grad = (grad_attn, swap(grad_attn, 1))

    def attend_back(part, result, place, table):
        return attention_backward(
            place, lengths, part, output_weights, query_weights, result[1], result[2], kv, *table
        )

    def product(left, right):
        return dot(jnp.concatenate(left), jnp.concatenate(right), ((0,), (0,)), BF16)

    g_ups, near_grad = sums.advance([grad_gate[0]], (g_ups, near_grad))
    grad_up = halves(sum_of_products(g_ups, mid_all).astype(BF16))
    near_q, near_terms, near_kv = attend_back(near_grad, near_result, near_place, near_table)
    near_core = swap(near_terms[1], 1)

    far_grad, near_q, near_kv = sums.advance([grad_gate[1]], (far_grad, near_q, near_kv))
    far_grad = (far_grad, swap(far_grad, 1))
    far_q, far_terms, far_kv = attend_back(far_grad, far_result, far_place, far_table)
    for_far = add_up(far_terms[0], swap(far_terms[1], 1)).astype(BF16)
    from_far = swap(for_far, top)

    far_grad, far_q, far_kv = sums.advance([grad_up[0]], (far_grad, far_q, far_kv))
    unit = output_weight.shape[0]
    kv_blocks = (near_kv + far_kv).astype(BF16).reshape(seqs, n, rows, 2 * HEAD).swapaxes(0, 1)
    kv_sum = reduce_blocks(kv_blocks)
    mixed = [r[0][i] for r in (near_result, far_result) for i in range(2)]
    wo_full = product(mixed, [*near_grad, *far_grad])
    wo_full, kv_sum = tie(wo_full, kv_sum)
    wo_part = reduce_middle([wo_full[i * unit : (i + 1) * unit] for i in range(heads_width // unit)])
    wo_part = wo_part.astype(BF16)
    key_grad = kv_sum[..., :HEAD]
    key_grad = key_grad * own_cos - jnp.roll(key_grad, HEAD // 2, axis=-1) * own_sin
    kv_grad = jnp.concatenate([key_grad, kv_sum[..., HEAD:]], -1).astype(BF16).reshape(flat, 2 * HEAD)

    far_q = sums.advance([grad_up[1]], far_q)
    grad_in = add_up(near_terms[0], near_core, from_far)
    grad_in = grad_in + dot(kv_grad, kv_weight, ((1,), (1,)))
    kv_portion = dot(norm_in, kv_grad, ((0,), (0,)))
    back, attn_gain_part = norm_back(x, attn_gain, grad_in.reshape(seqs, rows, width))
    grad_tokens = grad_hidden + back
    gains = jnp.concatenate([attn_gain_part, mlp_gain_part]).reshape(-1, 2 * HEAD)
    shared = jnp.concatenate([kv_portion + pair_grad[0, 0], gains])
    shared = jnp.pad(shared, ((0, -shared.shape[0] % (16 * n)), (0, 0))).astype(BF16)
    shared = reduce_blocks(shared.reshape(n, -1, 2 * HEAD)).astype(BF16)


    wq_full = product([near_q[0], near_q[1], far_q[0], far_q[1]], [*near_in, *far_in])
    wq_full, shared = tie(wq_full, shared)
    wq_part = reduce_middle([wq_full[i * unit : (i + 1) * unit] for i in range(heads_width // unit)])
    wq_part = wq_part.astype(BF16)

    acts = sums.advance([wo_part, shared], acts)

    def out_terms(i, after):
        left = acts[2 * i : 2 * i + 2]
        left = left if after is None else tie(left, after)[0]
        return [dot(part, down_weight, ((1,), (0,)), BF16) for part in left]

    out_own, out_sent = reduce_begin(chips, out_terms, lambda after: after)
    rows_out = reduce_end(out_own, out_sent)
    output = (hidden + valid * rows_out.reshape(seqs, rows, width)).astype(BF16)
    sums.advance([wq_part])
    shared = sums.advance_and_peek()
    shared = sums.advance([], gather_blocks(shared))
    sums.advance([])
    down_1, down_2, gate_1, gate_2, up_1, up_2, wo_sum, _, wq_sum = sums.sums
    shared = shared.reshape(-1, 2 * HEAD).astype(F32)
    gains = shared[width : width + gains.shape[0]].reshape(2, width)
    return (
        output,
        grad_tokens,
        wq_sum.astype(F32).T,
        shared[:width, :HEAD],
        shared[:width, HEAD:],
        wo_sum.astype(F32),
        jnp.concatenate([gate_1, gate_2]).astype(F32).T,
        jnp.concatenate([up_1, up_2]).astype(F32).T,
        jnp.concatenate([down_1, down_2]).astype(F32),
        gains[0],
        gains[1],
    )


def solution(mesh):
    placed = (
        P("dp", "tensor", None),
        P("dp"),
        P(None, "tensor"),
        P(),
        P(),
        P("tensor", None),
        P(None, "tensor"),
        P(None, "tensor"),
        P("tensor", None),
        P(),
        P(),
        P("dp", "tensor", None, None),
        P("dp", "tensor", None),
    )
    return jax.shard_map(
        per_device,
        mesh=mesh,
        in_specs=placed,
        out_specs=(
            P("dp", "tensor", None),
            P("dp", "tensor", None),
            P(None, "tensor"),
            P(),
            P(),
            P("tensor", None),
            P(None, "tensor"),
            P(None, "tensor"),
            P("tensor", None),
            P(),
            P(),
        ),
        check_vma=False,
    )
```

```python
import functools

import jax
import jax.numpy as jnp
from jax import lax
from jax.experimental import pallas as pl
from jax.experimental.pallas import tpu as pltpu
from jax.sharding import PartitionSpec as P

HEAD = 128
KEY_BLOCK = 256
JOIN_COST = 8_000_000_000
BACK_COST = 1
FORTH_COST = 60
SMALL_SHIFT = 1e-05
ROPE_BASE = 10000.0
NEG_FILL = -1e30
LOG2E = 1.4426950408889634
F32 = jnp.float32
BF16 = jnp.bfloat16


def rms_scale(values):
    return lax.rsqrt(jnp.mean(values * values, axis=-1, keepdims=True) + SMALL_SHIFT)


def normed(values, gain_vec):
    return values * rms_scale(values) * gain_vec


def norm_back(values, gain_vec, grad_vals):
    scale_vals = rms_scale(values)
    scaled = grad_vals * gain_vec
    inner_mean = jnp.mean(scaled * values, axis=-1, keepdims=True)
    grad_values = scale_vals * scaled - values * (scale_vals * scale_vals * scale_vals) * inner_mean
    grad_gain = jnp.sum(grad_vals * values * scale_vals, axis=(0, 1))
    return grad_values, grad_gain


def rope_block(start, rows):
    half = HEAD // 2
    frequency = ROPE_BASE ** (-2.0 * jnp.arange(half, dtype=F32) / HEAD)
    angles = (start + jnp.arange(rows)).astype(F32)[:, None] * frequency[None, :]
    cosine, sine = jnp.cos(angles), jnp.sin(angles)
    return jnp.concatenate([cosine, cosine], 1), jnp.concatenate([-sine, sine], 1)


def swap(values, bit):
    n = lax.axis_size("tensor")
    return lax.ppermute(values, "tensor", [(i, i ^ bit) for i in range(n)])


def dot(a, b, dims, out=F32):
    return lax.dot_general(a, b, (dims, ((), ())), preferred_element_type=F32).astype(out)


def add_up(*parts):
    total = parts[0].astype(F32)
    for part in parts[1:]:
        total = total + part.astype(F32)
    return total


def key_branches(start, rows, span, body):
    blocks = span // KEY_BLOCK
    needed = (start + rows + KEY_BLOCK - 1) // KEY_BLOCK
    for count in range(1, blocks + 1):
        pl.when(needed == count)(functools.partial(body, count * KEY_BLOCK))


def stack_heads(values, heads):
    return jnp.concatenate([values[:, h * HEAD : (h + 1) * HEAD] for h in range(heads)], axis=0)


def matmul(a, b, contract):
    return lax.dot_general(a, b, (contract, ((), ())), preferred_element_type=F32)


def masked_scores(keys, query, start, rows, heads, count):
    scores = matmul(keys, query, ((1,), (1,)))
    key_pos = lax.broadcasted_iota(jnp.int32, (KEY_BLOCK, rows), 0) + (count - KEY_BLOCK)
    row_pos = lax.broadcasted_iota(jnp.int32, (KEY_BLOCK, rows), 1) + start
    allowed = key_pos <= row_pos
    last = scores[count - KEY_BLOCK :]
    last = jnp.concatenate(
        [jnp.where(allowed, last[:, h * rows : (h + 1) * rows], NEG_FILL) for h in range(heads)], axis=1
    )
    if count == KEY_BLOCK:
        return last
    return jnp.concatenate([scores[: count - KEY_BLOCK], last], axis=0)


def forward_kernel(
    place, lengths, x0_ref, x1_ref, wq_ref, kv_ref, cos_ref, sin_ref, mixed_ref, query_ref, lse_ref, raw_ref, vt_ref
):
    a, s = pl.program_id(0), pl.program_id(1)
    seqs, span = kv_ref.shape[0], kv_ref.shape[1]
    rows = x0_ref.shape[0] // seqs
    heads = wq_ref.shape[1] // HEAD
    start = place[a] * rows
    here = pl.ds(pl.multiple_of(s * rows, rows), rows)
    live = start < lengths[s]
    factor = HEAD ** (-0.5) * LOG2E

    for k, x_ref in enumerate((x0_ref, x1_ref)):

        @pl.when((a == k) & (s == 0))
        def _(x_ref=x_ref):
            raw_ref[...] = matmul(x_ref[...], wq_ref[...], ((1,), (0,)))

    @pl.when(a == 0)
    def _():
        vt_ref[s] = kv_ref[s, :, HEAD:].T

    pieces = []
    for h in range(heads):
        raw = raw_ref[here, h * HEAD : (h + 1) * HEAD]
        pieces.append((raw * cos_ref[0] + pltpu.roll(raw, HEAD // 2, 1) * sin_ref[0]).astype(BF16))
    query_ref[0, s] = jnp.concatenate(pieces, axis=0)

    def body(count):
        scores = masked_scores(kv_ref[s, :count, :HEAD], query_ref[0, s], start, rows, heads, count)
        top = jnp.max(scores, axis=0, keepdims=True)
        terms = jnp.exp2((scores - top) * factor)
        total = jnp.sum(terms, axis=0, keepdims=True)
        out = matmul(vt_ref[s, :, :count], terms.astype(BF16), ((1,), (0,))) / total
        lse_ref[0, s] = jnp.broadcast_to(top * factor + jnp.log2(total), lse_ref.shape[2:])
        for h in range(heads):
            piece = out[:, h * rows : (h + 1) * rows].T
            mixed_ref[0, here, h * HEAD : (h + 1) * HEAD] = piece.astype(BF16)

    @pl.when(live)
    def _():
        key_branches(start, rows, span, body)

    @pl.when(jnp.logical_not(live))
    def _():
        mixed_ref[0, here] = jnp.zeros((rows, heads * HEAD), BF16)
        lse_ref[0, s] = jnp.zeros(lse_ref.shape[2:], F32)


def whole(shape):
    return pl.BlockSpec(shape, lambda a, *_: (0,) * len(shape))


def blocked(shape):
    return pl.BlockSpec((1, *shape[1:]), lambda a, *_: (a,) + (0,) * (len(shape) - 1))


def attention_forward(place, lengths, parts, query_weights, kv, cosine, sine):
    flat, width = parts[0].shape
    seqs, span = kv.shape[0], kv.shape[1]
    rows, wide = flat // seqs, query_weights.shape[1]
    heads = wide // HEAD
    shapes = [(2, flat, wide), (2, seqs, heads * rows, HEAD), (2, seqs, 8, heads * rows)]
    return pl.pallas_call(
        forward_kernel,
        grid_spec=pltpu.PrefetchScalarGridSpec(
            num_scalar_prefetch=2,
            grid=(2, seqs),
            in_specs=[
                whole(parts[0].shape),
                whole(parts[1].shape),
                whole(query_weights.shape),
                whole(kv.shape),
                blocked(cosine.shape),
                blocked(sine.shape),
            ],
            out_specs=[blocked(shape) for shape in shapes],
            scratch_shapes=[pltpu.VMEM((flat, wide), F32), pltpu.VMEM((seqs, HEAD, span), BF16)],
        ),
        out_shape=[jax.ShapeDtypeStruct(s, t) for s, t in zip(shapes, (BF16, BF16, F32))],
        compiler_params=pltpu.CompilerParams(vmem_limit_bytes=48 * 1024 * 1024),
        cost_estimate=pl.CostEstimate(flops=FORTH_COST * flat * wide * span, bytes_accessed=kv.size, transcendentals=0),
        name="attention_forward",
    )(place, lengths, *parts, query_weights, kv, cosine, sine)


def backward_kernel(
    place, lengths, g0_ref, g1_ref, wo_ref, wq_ref, query_ref, lse_ref, kv_ref, cos_ref, sin_ref,
    gq_ref, in_ref, gkv_ref, gm_ref, kt_ref,
):
    a, s = pl.program_id(0), pl.program_id(1)
    seqs, span = kv_ref.shape[0], kv_ref.shape[1]
    rows = g0_ref.shape[0] // seqs
    heads = wq_ref.shape[1] // HEAD
    start = place[a] * rows
    here = pl.ds(pl.multiple_of(s * rows, rows), rows)
    live = start < lengths[s]
    scale = HEAD ** (-0.5)
    factor = scale * LOG2E

    for k, g_ref in enumerate((g0_ref, g1_ref)):

        @pl.when((a == k) & (s == 0))
        def _(g_ref=g_ref):
            gm_ref[...] = matmul(g_ref[...], wo_ref[...], ((1,), (1,))).astype(BF16)

    @pl.when(a == 0)
    def _():
        gkv_ref[s] = jnp.zeros(gkv_ref.shape[1:], F32)
        kt_ref[s] = kv_ref[s, :, :HEAD].T

    def body(count):
        query = query_ref[0, s]
        grad = stack_heads(gm_ref[here, :], heads)
        scores = masked_scores(kv_ref[s, :count, :HEAD], query, start, rows, heads, count)
        probs = jnp.exp2(scores * factor - lse_ref[0, s, 0:1, :])
        grad_probs = matmul(kv_ref[s, :count, HEAD:], grad, ((1,), (1,)))
        row_dots = jnp.sum(probs * grad_probs, axis=0, keepdims=True)
        grad_scores = (probs * (grad_probs - row_dots)).astype(BF16)
        gkv_ref[s, :count, :HEAD] += scale * matmul(grad_scores, query, ((1,), (0,)))
        gkv_ref[s, :count, HEAD:] += matmul(probs.astype(BF16), grad, ((1,), (0,)))
        grad_query = matmul(kt_ref[s, :, :count], grad_scores, ((1,), (0,)))
        for h in range(heads):
            piece = grad_query[:, h * rows : (h + 1) * rows].T * scale
            piece = piece * cos_ref[0] - pltpu.roll(piece, HEAD // 2, 1) * sin_ref[0]
            gq_ref[0, here, h * HEAD : (h + 1) * HEAD] = piece.astype(BF16)

    @pl.when(live)
    def _():
        key_branches(start, rows, span, body)

    @pl.when(jnp.logical_not(live))
    def _():
        gq_ref[0, here] = jnp.zeros((rows, heads * HEAD), BF16)

    @pl.when(s == seqs - 1)
    def _():
        in_ref[0] = matmul(gq_ref[0], wq_ref[...], ((1,), (1,))).astype(BF16)


def attention_backward(place, lengths, grads, output_weights, query_weights, query, lse, kv, cosine, sine):
    flat, width = grads[0].shape
    seqs, span = kv.shape[0], kv.shape[1]
    wide = query_weights.shape[1]
    operands = (*grads, output_weights, query_weights, query, lse, kv, cosine, sine)
    specs = [whole(v.shape) for v in operands]
    for k in (4, 5, 7, 8):
        specs[k] = blocked(operands[k].shape)
    return pl.pallas_call(
        backward_kernel,
        grid_spec=pltpu.PrefetchScalarGridSpec(
            num_scalar_prefetch=2,
            grid=(2, seqs),
            in_specs=specs,
            out_specs=[blocked((2, flat, wide)), blocked((2, flat, width)), whole(kv.shape)],
            scratch_shapes=[pltpu.VMEM((flat, wide), BF16), pltpu.VMEM((seqs, HEAD, span), BF16)],
        ),
        out_shape=[
            jax.ShapeDtypeStruct((2, flat, wide), BF16),
            jax.ShapeDtypeStruct((2, flat, width), BF16),
            jax.ShapeDtypeStruct(kv.shape, F32),
        ],
        compiler_params=pltpu.CompilerParams(vmem_limit_bytes=56 * 1024 * 1024),
        cost_estimate=pl.CostEstimate(flops=BACK_COST * flat * wide * span, bytes_accessed=kv.size, transcendentals=0),
        name="attention_backward",
    )(place, lengths, *operands)


def join_columns(parts):
    rows, wide = parts[0].shape

    def kernel(*refs):
        for k in range(len(parts)):
            refs[-1][:, k * wide : (k + 1) * wide] = refs[k][...]

    return pl.pallas_call(
        kernel,
        grid=(4,),
        in_specs=[pl.BlockSpec((rows // 4, wide), lambda i: (i, 0)) for _ in parts],
        out_specs=pl.BlockSpec((rows // 4, wide * len(parts)), lambda i: (i, 0)),
        out_shape=jax.ShapeDtypeStruct((rows, wide * len(parts)), parts[0].dtype),
        cost_estimate=pl.CostEstimate(flops=JOIN_COST, bytes_accessed=0, transcendentals=0),
        name="join_columns",
    )(*parts)


def middle_bits(n):
    bits, bit = [], 2
    while bit < n // 2:
        bits.append(bit)
        bit *= 2
    return bits


def gather_middle(values):
    parts = [values]
    for bit in middle_bits(lax.axis_size("tensor")):
        parts = parts + [swap(part, bit) for part in parts]
    return parts


def reduce_middle(parts):
    for bit in reversed(middle_bits(lax.axis_size("tensor"))):
        half = len(parts) // 2
        parts = [add_up(parts[i], swap(parts[half + i].astype(BF16), bit)) for i in range(half)]
    return parts[0]


def sum_of_products(left, right, start=None):
    total = dot(jnp.concatenate(left), jnp.concatenate(right), ((0,), (0,)))
    return total if start is None else start + total


def tie(*values):
    return lax.optimization_barrier(values)


def line_step(outer, own_in, sent_in, fresh, own_across, sent_across):
    rows, width = fresh.shape

    def kernel(outer_ref, a_ref, b_ref, c_ref, d_ref, e_ref, pair_ref, leaving_ref):
        @pl.when(outer_ref[0] == 1)
        def _():
            pair_ref[...] = c_ref[...]
            leaving_ref[...] = c_ref[...]

        @pl.when(outer_ref[0] == 0)
        def _():
            pair_ref[...] = (a_ref[...].astype(F32) + b_ref[...].astype(F32)).astype(BF16)
            leaving_ref[...] = (d_ref[...].astype(F32) + e_ref[...].astype(F32)).astype(BF16)

    steps = 4
    inner_block = pl.BlockSpec((rows, width // steps), lambda i, o: (0, i * (1 - o[0])))
    outer_block = pl.BlockSpec((rows, width // steps), lambda i, o: (0, i * o[0]))
    block = pl.BlockSpec((rows, width // steps), lambda i, o: (0, i))
    return pl.pallas_call(
        kernel,
        grid_spec=pltpu.PrefetchScalarGridSpec(
            num_scalar_prefetch=1,
            grid=(steps,),
            in_specs=[inner_block, inner_block, outer_block, inner_block, inner_block],
            out_specs=[block, block],
        ),
        out_shape=[jax.ShapeDtypeStruct((rows, width), BF16)] * 2,
        name="line_step",
    )(outer.astype(jnp.int32).reshape(1), own_in, sent_in, fresh, own_across, sent_across)


class LineSum:
    def __init__(self):
        self.line = lax.axis_size("dp") == 4
        place = lax.axis_index("dp")
        self.outer = (place == 0) | (place == 3)
        self.inward, self.across, self.outward = [], [], []
        self.sums = []

    def advance(self, arrays, others=()):
        if not self.line:
            self.sums += [lax.psum(a, "dp") for a in arrays]
            return others
        arrays, inward, across, outward, others = tie(
            list(arrays), self.inward, self.across, self.outward, others
        )
        self.inward, self.outward = [], []
        if len(arrays) == 1 and [a.shape for a, _ in inward + across] == [arrays[0].shape] * 2:
            pairs, leaving = line_step(self.outer, *inward[0], arrays[0], *across[0])
            sent = lax.ppermute(leaving, "dp", [(0, 1), (1, 0), (2, 3), (3, 2)])
            self.inward.append((arrays[0], sent))
            self.outward.append((leaving, sent))
            pairs = [pairs]
        else:
            pairs = [add_up(own, sent).astype(BF16) for own, sent in inward]
            totals = [add_up(own, sent).astype(BF16) for own, sent in across]
            self.inward = [(a, lax.ppermute(a, "dp", [(0, 1), (3, 2)])) for a in arrays]
            self.outward = [(a, lax.ppermute(a, "dp", [(1, 0), (2, 3)])) for a in totals]
        self.across = [(a, lax.ppermute(a, "dp", [(1, 2), (2, 1)])) for a in pairs]
        self.sums += [jnp.where(self.outer, sent, own) for own, sent in outward]
        return others


    def leave(self, array):
        return lax.ppermute(array, "dp", [(0, 1), (3, 2)]) if self.line else lax.psum(array, "dp")

    def add(self, array, sent):
        if self.line:
            self.inward.append((array, sent))
        else:
            self.sums.append(sent)

    def advance_and_peek(self):
        self.advance([])
        if not self.line:
            return self.sums[-2]
        own, sent = self.outward[-1]
        return jnp.where(self.outer, sent, own)


def tensor_bits():
    n, bits, bit = lax.axis_size("tensor"), [], 1
    while bit < n:
        bits.append(bit)
        bit *= 2
    return bits


def reduce_blocks(blocks):
    n, me = blocks.shape[0], lax.axis_index("tensor")
    held = [lax.dynamic_index_in_dim(blocks, me ^ r, 0, keepdims=False) for r in range(n)]
    for bit in tensor_bits():
        keep = jnp.stack([held[r] for r in range(len(held)) if r % 2 == 0])
        give = jnp.stack([held[r] for r in range(len(held)) if r % 2 == 1])
        total = add_up(keep, swap(give.astype(BF16), bit))
        held = [total[k] for k in range(total.shape[0])]
    return held[0]


def gather_blocks(block):
    n, me = lax.axis_size("tensor"), lax.axis_index("tensor")
    held = block[None]
    for bit in reversed(tensor_bits()):
        other = swap(held, bit)
        held = jnp.stack([held, other], 1).reshape(2 * held.shape[0], *block.shape)
    result = jnp.zeros_like(held)
    for r in range(n):
        result = lax.dynamic_update_index_in_dim(result, held[r], me ^ r, 0)
    return result


def gather_near(values):
    if lax.axis_size("tensor") != 8:
        return values, values
    return swap(values, 2), swap(values, 4)


def gather_pairs(values):
    parts, bits = [values], tensor_bits()
    for bit in bits:
        parts = parts + [swap(part, bit) for part in parts]
    return [(parts[i], parts[i + 1]) for i in range(0, len(parts), 2)]


def halves(value):
    rows = value.shape[0] // 2
    return value[:rows], value[rows:]


def reduce_begin(count, terms, between):
    n = lax.axis_size("tensor")
    if n != 8:
        parts = []
        for i in range(count):
            own, other = terms(i, None)
            parts.append(add_up(own, swap(other, 1)))
        while len(parts) > 1:
            half = len(parts) // 2
            parts = [add_up(parts[i], swap(parts[half + i].astype(BF16), 2 * half)) for i in range(half)]
        between(parts[0])
        return parts[0], ()
    own_d, other_d = (terms(3, None))
    core_d = swap(other_d, 1)
    own_y, other_y = (terms(2, own_d))
    core_y = swap(other_y, 1)
    diagonal = add_up(own_d, core_d).astype(BF16)
    diagonal, own_y = tie(diagonal, own_y)
    first, second = halves(diagonal)
    from_x, from_y = swap(first, 2), swap(second, 4)
    own_x, other_x = (terms(1, between(diagonal)))
    core_x = swap(other_x, 1)
    own, other = (terms(0, own_x))
    core = swap(other, 1)
    low, high = halves(add_up(own_y, core_y))
    for_y = jnp.concatenate([add_up(low, from_x), high]).astype(BF16)
    low, high = halves(add_up(own_x, core_x))
    for_x = jnp.concatenate([low, add_up(high, from_y)]).astype(BF16)
    return (own, core), (for_x, for_y)


def reduce_end(own, sent):
    if not sent:
        return own
    return add_up(*own, swap(sent[0], 2), swap(sent[1], 4))


def per_device(
    tokens,
    lengths,
    query_weight,
    key_weight,
    value_weight,
    output_weight,
    gate_weight,
    up_weight,
    down_weight,
    gain_attn,
    gain_mlp,
    pair_grad,
    cotangent,
):
    seqs, rows, width = tokens.shape
    n = lax.axis_size("tensor")
    me = lax.axis_index("tensor")
    top = n // 2
    flat = seqs * rows
    local_pos = me * rows + jnp.arange(rows)
    valid = (local_pos[None, :] < lengths[:, None]).astype(F32)[..., None]
    x = tokens.astype(F32)
    attn_gain = gain_attn.astype(F32)
    mlp_gain = gain_mlp.astype(F32)
    grad_y = cotangent.astype(F32)
    kv_weight = jnp.concatenate([key_weight, value_weight], axis=1)

    norm_in = normed(x, attn_gain).astype(BF16).reshape(flat, width)
    far_in = swap(norm_in, top)
    far_in = (far_in, swap(far_in, 1))
    near_in = (norm_in, swap(norm_in, 1))
    def slopes_of(blocks):
        return [dot(block, down_weight, ((1,), (1,))) for block in blocks]

    def with_core(part):
        return part, swap(part, 1)

    grad_out = (valid * grad_y).astype(BF16).reshape(flat, width)
    own_grads = with_core(grad_out)
    own_slopes, query_parts = tie(slopes_of(own_grads), gather_middle(query_weight))
    query_weights = join_columns(query_parts)
    heads_width = query_weights.shape[1]
    own_cos, own_sin = rope_block(me * rows, rows)
    kv_raw = dot(norm_in, kv_weight, ((1,), (0,))).reshape(seqs, rows, 2 * HEAD)
    key_raw = kv_raw[..., :HEAD]
    key_own = key_raw * own_cos + jnp.roll(key_raw, HEAD // 2, axis=-1) * own_sin
    kv_own = jnp.concatenate([key_own, kv_raw[..., HEAD:]], axis=-1).astype(BF16)

    output_weight, kv_own = tie(output_weight, kv_own)
    output_parts = gather_middle(output_weight)
    kv = lax.all_gather(kv_own, "tensor", axis=1, tiled=True)

    def place_of(offset):
        place = jnp.stack([me ^ offset, me ^ (offset + 1)]).astype(jnp.int32)
        blocks = [rope_block(place[i] * rows, rows) for i in range(2)]
        return place, (jnp.stack([b[0] for b in blocks]), jnp.stack([b[1] for b in blocks]))

    def attend(part, place, table):
        return attention_forward(place, lengths, part, query_weights, kv, *table)

    def portions_of(mixed):
        return [dot(mixed[i], output_weights, ((1,), (0,)), BF16) for i in range(2)]

    near_place, near_table = place_of(0)
    far_place, far_table = place_of(top)
    grad_out, _ = tie(grad_out, norm_in)
    grad_far = swap(grad_out, top)
    near_result = attend(near_in, near_place, near_table)
    far_in, _ = tie(far_in, near_result[0])
    far_result = attend(far_in, far_place, far_table)
    output_parts, far_mixed, grad_far = tie(output_parts, far_result[0], grad_far)
    output_weights = jnp.concatenate(output_parts, axis=0)
    far_portions = portions_of(far_mixed)
    for_far = add_up(far_portions[0], swap(far_portions[1], 1)).astype(BF16)
    for_far, near_mixed = tie(for_far, near_result[0])
    from_far = swap(for_far, top)
    near_portions = portions_of(near_mixed)
    near_core = swap(near_portions[1], 1)
    if n == 8:
        grad_out, _ = tie(grad_out, far_mixed)
        grad_side = swap(grad_out, 2)
        size = flat // 2
        from_far, grad_side, grad_far = tie(from_far, grad_side, grad_far)
        grad_diagonal = [swap(grad_side[:size], 4), swap(grad_far[size:], 2)]
    attn_out = add_up(near_portions[0], near_core, from_far)
    hidden = x + valid * attn_out.reshape(seqs, rows, width)

    chips = n // 2
    norm_mid = normed(hidden, mlp_gain).astype(BF16).reshape(flat, width)
    gate_rows, up_rows = gate_weight.T, up_weight.T

    mids, acts, g_gates, g_ups = [], [], [], []

    def forward_blocks(blocks, slopes):
        for mid, slope in zip(blocks, slopes):
            gate = dot(mid, gate_rows, ((1,), (1,)))
            up = dot(mid, up_rows, ((1,), (1,)))
            sig = 1.0 / (1.0 + jnp.exp(-gate))
            silu = gate * sig
            mids.append(mid)
            acts.append((silu * up).astype(BF16))
            g_gates.append((slope * up * sig * (1.0 + gate * (1.0 - sig))).astype(BF16))
            g_ups.append((slope * silu).astype(BF16))

    def diagonal_blocks(parts):
        return [jnp.concatenate(p) for p in zip(*[with_core(part) for part in parts])]

    if n == 8:
        at_x, at_y = gather_near(norm_mid)
        grads = [*own_grads, *with_core(grad_side), *with_core(grad_far)]
        slopes = own_slopes + slopes_of(grads[2:])
        forward_blocks(with_core(norm_mid), slopes[:2])
        at_x, at_y, slopes, acts[1] = tie(at_x, at_y, slopes, acts[1])
        diagonal = [swap(at_x[:size], 4), swap(at_y[size:], 2)]
        forward_blocks((*with_core(at_x), *with_core(at_y)), slopes[2:6])
        grad_down = sum_of_products(acts[:6], grads[:6])
        diagonal, grad_diagonal, grad_down = tie(diagonal, grad_diagonal, grad_down)
        grads += diagonal_blocks(grad_diagonal)
        forward_blocks(diagonal_blocks(diagonal), slopes_of(grads[6:]))
    else:
        grads = [block for pair in gather_pairs(grad_out) for block in pair]
        forward_blocks([block for pair in gather_pairs(norm_mid) for block in pair], slopes_of(grads))
        grad_down = sum_of_products(acts[:-2], grads[:-2])

    def mid_term(r):
        terms = dot(g_gates[r], gate_rows, ((1,), (0,))) + dot(g_ups[r], up_rows, ((1,), (0,)))
        return terms.astype(BF16)

    def mid_terms(i, after):
        for k in (2 * i, 2 * i + 1):
            if after is not None:
                g_gates[k], g_ups[k], _ = tie(g_gates[k], g_ups[k], after)
        return mid_term(2 * i), mid_term(2 * i + 1)

    sums, down_parts = LineSum(), []

    def down_gradient(after):
        last, after = tie(acts[-2:], after)
        down_parts.extend(halves(sum_of_products(last, grads[-2:], grad_down).astype(BF16)))
        after, down_parts[1] = sums.advance([down_parts[0]], (after, down_parts[1]))
        down_parts.append(sums.leave(down_parts[1]))
        return after

    mid_own, mid_sent = reduce_begin(chips, mid_terms, down_gradient)
    grad_mid = reduce_end(mid_own, mid_sent).reshape(seqs, rows, width)

    g_gates, g_ups, mids = sums.advance([], (g_gates, g_ups, mids))
    sums.add(down_parts[1], down_parts[2])
    mid_all = [jnp.concatenate(mids)]
    grad_gate = halves(sum_of_products(g_gates, mid_all).astype(BF16))
    back, mlp_gain_part = norm_back(hidden, mlp_gain, grad_mid)
    grad_hidden = grad_y + back
    grad_attn = (valid * grad_hidden).astype(BF16).reshape(flat, width)
    far_grad = swap(grad_attn, top)
    near_grad = (grad_attn, swap(grad_attn, 1))

    def attend_back(part, result, place, table):
        return attention_backward(
            place, lengths, part, output_weights, query_weights, result[1], result[2], kv, *table
        )

    def product(left, right):
        return dot(jnp.concatenate(left), jnp.concatenate(right), ((0,), (0,)), BF16)

    g_ups, near_grad = sums.advance([grad_gate[0]], (g_ups, near_grad))
    grad_up = halves(sum_of_products(g_ups, mid_all).astype(BF16))
    near_q, near_terms, near_kv = attend_back(near_grad, near_result, near_place, near_table)
    near_core = swap(near_terms[1], 1)

    far_grad, near_q, near_kv = sums.advance([grad_gate[1]], (far_grad, near_q, near_kv))
    far_grad = (far_grad, swap(far_grad, 1))
    far_q, far_terms, far_kv = attend_back(far_grad, far_result, far_place, far_table)
    for_far = add_up(far_terms[0], swap(far_terms[1], 1)).astype(BF16)
    from_far = swap(for_far, top)

    far_grad, far_q, far_kv = sums.advance([grad_up[0]], (far_grad, far_q, far_kv))
    unit = output_weight.shape[0]
    kv_blocks = (near_kv + far_kv).astype(BF16).reshape(seqs, n, rows, 2 * HEAD).swapaxes(0, 1)
    kv_sum = reduce_blocks(kv_blocks)
    wq_full = product([near_q[0], near_q[1], far_q[0], far_q[1]], [*near_in, *far_in])
    wq_full, kv_sum = tie(wq_full, kv_sum)
    wq_part = reduce_middle([wq_full[i * unit : (i + 1) * unit] for i in range(heads_width // unit)])
    wq_part = wq_part.astype(BF16)
    key_grad = kv_sum[..., :HEAD]
    key_grad = key_grad * own_cos - jnp.roll(key_grad, HEAD // 2, axis=-1) * own_sin
    kv_grad = jnp.concatenate([key_grad, kv_sum[..., HEAD:]], -1).astype(BF16).reshape(flat, 2 * HEAD)

    far_grad = sums.advance([grad_up[1]], far_grad)
    grad_in = add_up(near_terms[0], near_core, from_far)
    grad_in = grad_in + dot(kv_grad, kv_weight, ((1,), (1,)))
    kv_portion = dot(norm_in, kv_grad, ((0,), (0,)))
    back, attn_gain_part = norm_back(x, attn_gain, grad_in.reshape(seqs, rows, width))
    grad_tokens = grad_hidden + back
    gains = jnp.concatenate([attn_gain_part, mlp_gain_part]).reshape(-1, 2 * HEAD)
    shared = jnp.concatenate([kv_portion + pair_grad[0, 0], gains])
    shared = jnp.pad(shared, ((0, -shared.shape[0] % (16 * n)), (0, 0))).astype(BF16)
    shared = reduce_blocks(shared.reshape(n, -1, 2 * HEAD)).astype(BF16)


    mixed = [r[0][i] for r in (near_result, far_result) for i in range(2)]
    wo_full = product(mixed, [*near_grad, *far_grad])
    wo_full, shared = tie(wo_full, shared)
    wo_part = reduce_middle([wo_full[i * unit : (i + 1) * unit] for i in range(heads_width // unit)])
    wo_part = wo_part.astype(BF16)

    acts = sums.advance([wq_part, shared], acts)

    def out_terms(i, after):
        left = acts[2 * i : 2 * i + 2]
        left = left if after is None else tie(left, after)[0]
        return [dot(part, down_weight, ((1,), (0,)), BF16) for part in left]

    out_own, out_sent = reduce_begin(chips, out_terms, lambda after: after)
    rows_out = reduce_end(out_own, out_sent)
    output = (hidden + valid * rows_out.reshape(seqs, rows, width)).astype(BF16)
    sums.advance([wo_part])
    shared = sums.advance_and_peek()
    shared = sums.advance([], gather_blocks(shared))
    sums.advance([])
    down_1, down_2, gate_1, gate_2, up_1, up_2, wq_sum, _, wo_sum = sums.sums
    shared = shared.reshape(-1, 2 * HEAD).astype(F32)
    gains = shared[width : width + gains.shape[0]].reshape(2, width)
    return (
        output,
        grad_tokens,
        wq_sum.astype(F32).T,
        shared[:width, :HEAD],
        shared[:width, HEAD:],
        wo_sum.astype(F32),
        jnp.concatenate([gate_1, gate_2]).astype(F32).T,
        jnp.concatenate([up_1, up_2]).astype(F32).T,
        jnp.concatenate([down_1, down_2]).astype(F32),
        gains[0],
        gains[1],
    )


def solution(mesh):
    placed = (
        P("dp", "tensor", None),
        P("dp"),
        P(None, "tensor"),
        P(),
        P(),
        P("tensor", None),
        P(None, "tensor"),
        P(None, "tensor"),
        P("tensor", None),
        P(),
        P(),
        P("dp", "tensor", None, None),
        P("dp", "tensor", None),
    )
    return jax.shard_map(
        per_device,
        mesh=mesh,
        in_specs=placed,
        out_specs=(
            P("dp", "tensor", None),
            P("dp", "tensor", None),
            P(None, "tensor"),
            P(),
            P(),
            P("tensor", None),
            P(None, "tensor"),
            P(None, "tensor"),
            P("tensor", None),
            P(),
            P(),
        ),
        check_vma=False,
    )
```

```python
import functools

import jax
import jax.numpy as jnp
from jax import lax
from jax.experimental import pallas as pl
from jax.experimental.pallas import tpu as pltpu
from jax.sharding import PartitionSpec as P

HEAD = 128
KEY_BLOCK = 256
JOIN_COST = 8_000_000_000
BACK_COST = 1
FORTH_COST = 60
SMALL_SHIFT = 1e-05
ROPE_BASE = 10000.0
NEG_FILL = -1e30
LOG2E = 1.4426950408889634
F32 = jnp.float32
BF16 = jnp.bfloat16


def rms_scale(values):
    return lax.rsqrt(jnp.mean(values * values, axis=-1, keepdims=True) + SMALL_SHIFT)


def normed(values, gain_vec):
    return values * rms_scale(values) * gain_vec


def norm_back(values, gain_vec, grad_vals):
    scale_vals = rms_scale(values)
    scaled = grad_vals * gain_vec
    inner_mean = jnp.mean(scaled * values, axis=-1, keepdims=True)
    grad_values = scale_vals * scaled - values * (scale_vals * scale_vals * scale_vals) * inner_mean
    grad_gain = jnp.sum(grad_vals * values * scale_vals, axis=(0, 1))
    return grad_values, grad_gain


def rope_block(start, rows):
    half = HEAD // 2
    frequency = ROPE_BASE ** (-2.0 * jnp.arange(half, dtype=F32) / HEAD)
    angles = (start + jnp.arange(rows)).astype(F32)[:, None] * frequency[None, :]
    cosine, sine = jnp.cos(angles), jnp.sin(angles)
    return jnp.concatenate([cosine, cosine], 1), jnp.concatenate([-sine, sine], 1)


def swap(values, bit):
    n = lax.axis_size("tensor")
    return lax.ppermute(values, "tensor", [(i, i ^ bit) for i in range(n)])


def dot(a, b, dims, out=F32):
    return lax.dot_general(a, b, (dims, ((), ())), preferred_element_type=F32).astype(out)


def add_up(*parts):
    total = parts[0].astype(F32)
    for part in parts[1:]:
        total = total + part.astype(F32)
    return total


def key_branches(start, rows, span, body):
    blocks = span // KEY_BLOCK
    needed = (start + rows + KEY_BLOCK - 1) // KEY_BLOCK
    for count in range(1, blocks + 1):
        pl.when(needed == count)(functools.partial(body, count * KEY_BLOCK))


def stack_heads(values, heads):
    return jnp.concatenate([values[:, h * HEAD : (h + 1) * HEAD] for h in range(heads)], axis=0)


def matmul(a, b, contract):
    return lax.dot_general(a, b, (contract, ((), ())), preferred_element_type=F32)


def masked_scores(keys, query, start, rows, heads, count):
    scores = matmul(keys, query, ((1,), (1,)))
    key_pos = lax.broadcasted_iota(jnp.int32, (KEY_BLOCK, rows), 0) + (count - KEY_BLOCK)
    row_pos = lax.broadcasted_iota(jnp.int32, (KEY_BLOCK, rows), 1) + start
    allowed = key_pos <= row_pos
    last = scores[count - KEY_BLOCK :]
    last = jnp.concatenate(
        [jnp.where(allowed, last[:, h * rows : (h + 1) * rows], NEG_FILL) for h in range(heads)], axis=1
    )
    if count == KEY_BLOCK:
        return last
    return jnp.concatenate([scores[: count - KEY_BLOCK], last], axis=0)


def forward_kernel(
    place, lengths, x0_ref, x1_ref, wq_ref, kv_ref, cos_ref, sin_ref, mixed_ref, query_ref, lse_ref, raw_ref, vt_ref
):
    a, s = pl.program_id(0), pl.program_id(1)
    seqs, span = kv_ref.shape[0], kv_ref.shape[1]
    rows = x0_ref.shape[0] // seqs
    heads = wq_ref.shape[1] // HEAD
    start = place[a] * rows
    here = pl.ds(pl.multiple_of(s * rows, rows), rows)
    live = start < lengths[s]
    factor = HEAD ** (-0.5) * LOG2E

    for k, x_ref in enumerate((x0_ref, x1_ref)):

        @pl.when((a == k) & (s == 0))
        def _(x_ref=x_ref):
            raw_ref[...] = matmul(x_ref[...], wq_ref[...], ((1,), (0,)))

    @pl.when(a == 0)
    def _():
        vt_ref[s] = kv_ref[s, :, HEAD:].T

    pieces = []
    for h in range(heads):
        raw = raw_ref[here, h * HEAD : (h + 1) * HEAD]
        pieces.append((raw * cos_ref[0] + pltpu.roll(raw, HEAD // 2, 1) * sin_ref[0]).astype(BF16))
    query_ref[0, s] = jnp.concatenate(pieces, axis=0)

    def body(count):
        scores = masked_scores(kv_ref[s, :count, :HEAD], query_ref[0, s], start, rows, heads, count)
        top = jnp.max(scores, axis=0, keepdims=True)
        terms = jnp.exp2((scores - top) * factor)
        total = jnp.sum(terms, axis=0, keepdims=True)
        out = matmul(vt_ref[s, :, :count], terms.astype(BF16), ((1,), (0,))) / total
        lse_ref[0, s] = jnp.broadcast_to(top * factor + jnp.log2(total), lse_ref.shape[2:])
        for h in range(heads):
            piece = out[:, h * rows : (h + 1) * rows].T
            mixed_ref[0, here, h * HEAD : (h + 1) * HEAD] = piece.astype(BF16)

    @pl.when(live)
    def _():
        key_branches(start, rows, span, body)

    @pl.when(jnp.logical_not(live))
    def _():
        mixed_ref[0, here] = jnp.zeros((rows, heads * HEAD), BF16)
        lse_ref[0, s] = jnp.zeros(lse_ref.shape[2:], F32)


def whole(shape):
    return pl.BlockSpec(shape, lambda a, *_: (0,) * len(shape))


def blocked(shape):
    return pl.BlockSpec((1, *shape[1:]), lambda a, *_: (a,) + (0,) * (len(shape) - 1))


def attention_forward(place, lengths, parts, query_weights, kv, cosine, sine):
    flat, width = parts[0].shape
    seqs, span = kv.shape[0], kv.shape[1]
    rows, wide = flat // seqs, query_weights.shape[1]
    heads = wide // HEAD
    shapes = [(2, flat, wide), (2, seqs, heads * rows, HEAD), (2, seqs, 8, heads * rows)]
    return pl.pallas_call(
        forward_kernel,
        grid_spec=pltpu.PrefetchScalarGridSpec(
            num_scalar_prefetch=2,
            grid=(2, seqs),
            in_specs=[
                whole(parts[0].shape),
                whole(parts[1].shape),
                whole(query_weights.shape),
                whole(kv.shape),
                blocked(cosine.shape),
                blocked(sine.shape),
            ],
            out_specs=[blocked(shape) for shape in shapes],
            scratch_shapes=[pltpu.VMEM((flat, wide), F32), pltpu.VMEM((seqs, HEAD, span), BF16)],
        ),
        out_shape=[jax.ShapeDtypeStruct(s, t) for s, t in zip(shapes, (BF16, BF16, F32))],
        compiler_params=pltpu.CompilerParams(vmem_limit_bytes=48 * 1024 * 1024),
        cost_estimate=pl.CostEstimate(flops=FORTH_COST * flat * wide * span, bytes_accessed=kv.size, transcendentals=0),
        name="attention_forward",
    )(place, lengths, *parts, query_weights, kv, cosine, sine)


def backward_kernel(
    place, lengths, g0_ref, g1_ref, wo_ref, wq_ref, query_ref, lse_ref, kv_ref, cos_ref, sin_ref,
    gq_ref, in_ref, gkv_ref, gm_ref, kt_ref,
):
    a, s = pl.program_id(0), pl.program_id(1)
    seqs, span = kv_ref.shape[0], kv_ref.shape[1]
    rows = g0_ref.shape[0] // seqs
    heads = wq_ref.shape[1] // HEAD
    start = place[a] * rows
    here = pl.ds(pl.multiple_of(s * rows, rows), rows)
    live = start < lengths[s]
    scale = HEAD ** (-0.5)
    factor = scale * LOG2E

    for k, g_ref in enumerate((g0_ref, g1_ref)):

        @pl.when((a == k) & (s == 0))
        def _(g_ref=g_ref):
            gm_ref[...] = matmul(g_ref[...], wo_ref[...], ((1,), (1,))).astype(BF16)

    @pl.when(a == 0)
    def _():
        gkv_ref[s] = jnp.zeros(gkv_ref.shape[1:], F32)
        kt_ref[s] = kv_ref[s, :, :HEAD].T

    def body(count):
        query = query_ref[0, s]
        grad = stack_heads(gm_ref[here, :], heads)
        scores = masked_scores(kv_ref[s, :count, :HEAD], query, start, rows, heads, count)
        probs = jnp.exp2(scores * factor - lse_ref[0, s, 0:1, :])
        grad_probs = matmul(kv_ref[s, :count, HEAD:], grad, ((1,), (1,)))
        row_dots = jnp.sum(probs * grad_probs, axis=0, keepdims=True)
        grad_scores = (probs * (grad_probs - row_dots)).astype(BF16)
        gkv_ref[s, :count, :HEAD] += scale * matmul(grad_scores, query, ((1,), (0,)))
        gkv_ref[s, :count, HEAD:] += matmul(probs.astype(BF16), grad, ((1,), (0,)))
        grad_query = matmul(kt_ref[s, :, :count], grad_scores, ((1,), (0,)))
        for h in range(heads):
            piece = grad_query[:, h * rows : (h + 1) * rows].T * scale
            piece = piece * cos_ref[0] - pltpu.roll(piece, HEAD // 2, 1) * sin_ref[0]
            gq_ref[0, here, h * HEAD : (h + 1) * HEAD] = piece.astype(BF16)

    @pl.when(live)
    def _():
        key_branches(start, rows, span, body)

    @pl.when(jnp.logical_not(live))
    def _():
        gq_ref[0, here] = jnp.zeros((rows, heads * HEAD), BF16)

    @pl.when(s == seqs - 1)
    def _():
        in_ref[0] = matmul(gq_ref[0], wq_ref[...], ((1,), (1,))).astype(BF16)


def attention_backward(place, lengths, grads, output_weights, query_weights, query, lse, kv, cosine, sine):
    flat, width = grads[0].shape
    seqs, span = kv.shape[0], kv.shape[1]
    wide = query_weights.shape[1]
    operands = (*grads, output_weights, query_weights, query, lse, kv, cosine, sine)
    specs = [whole(v.shape) for v in operands]
    for k in (4, 5, 7, 8):
        specs[k] = blocked(operands[k].shape)
    return pl.pallas_call(
        backward_kernel,
        grid_spec=pltpu.PrefetchScalarGridSpec(
            num_scalar_prefetch=2,
            grid=(2, seqs),
            in_specs=specs,
            out_specs=[blocked((2, flat, wide)), blocked((2, flat, width)), whole(kv.shape)],
            scratch_shapes=[pltpu.VMEM((flat, wide), BF16), pltpu.VMEM((seqs, HEAD, span), BF16)],
        ),
        out_shape=[
            jax.ShapeDtypeStruct((2, flat, wide), BF16),
            jax.ShapeDtypeStruct((2, flat, width), BF16),
            jax.ShapeDtypeStruct(kv.shape, F32),
        ],
        compiler_params=pltpu.CompilerParams(vmem_limit_bytes=56 * 1024 * 1024),
        cost_estimate=pl.CostEstimate(flops=BACK_COST * flat * wide * span, bytes_accessed=kv.size, transcendentals=0),
        name="attention_backward",
    )(place, lengths, *operands)


def middle_bits(n):
    bits, bit = [], 2
    while bit < n // 2:
        bits.append(bit)
        bit *= 2
    return bits


def gather_middle(values):
    parts = [values]
    for bit in middle_bits(lax.axis_size("tensor")):
        parts = parts + [swap(part, bit) for part in parts]
    return parts


def reduce_middle(parts):
    for bit in reversed(middle_bits(lax.axis_size("tensor"))):
        half = len(parts) // 2
        parts = [add_up(parts[i], swap(parts[half + i].astype(BF16), bit)) for i in range(half)]
    return parts[0]


def sum_of_products(left, right, start=None):
    total = dot(jnp.concatenate(left), jnp.concatenate(right), ((0,), (0,)))
    return total if start is None else start + total


def tie(*values):
    return lax.optimization_barrier(values)


def line_step(outer, own_in, sent_in, fresh, own_across, sent_across):
    rows, width = fresh.shape

    def kernel(outer_ref, a_ref, b_ref, c_ref, d_ref, e_ref, pair_ref, leaving_ref):
        @pl.when(outer_ref[0] == 1)
        def _():
            pair_ref[...] = c_ref[...]
            leaving_ref[...] = c_ref[...]

        @pl.when(outer_ref[0] == 0)
        def _():
            pair_ref[...] = (a_ref[...].astype(F32) + b_ref[...].astype(F32)).astype(BF16)
            leaving_ref[...] = (d_ref[...].astype(F32) + e_ref[...].astype(F32)).astype(BF16)

    steps = 4
    inner_block = pl.BlockSpec((rows, width // steps), lambda i, o: (0, i * (1 - o[0])))
    outer_block = pl.BlockSpec((rows, width // steps), lambda i, o: (0, i * o[0]))
    block = pl.BlockSpec((rows, width // steps), lambda i, o: (0, i))
    return pl.pallas_call(
        kernel,
        grid_spec=pltpu.PrefetchScalarGridSpec(
            num_scalar_prefetch=1,
            grid=(steps,),
            in_specs=[inner_block, inner_block, outer_block, inner_block, inner_block],
            out_specs=[block, block],
        ),
        out_shape=[jax.ShapeDtypeStruct((rows, width), BF16)] * 2,
        name="line_step",
    )(outer.astype(jnp.int32).reshape(1), own_in, sent_in, fresh, own_across, sent_across)


class LineSum:
    def __init__(self):
        self.line = lax.axis_size("dp") == 4
        place = lax.axis_index("dp")
        self.outer = (place == 0) | (place == 3)
        self.inward, self.across, self.outward = [], [], []
        self.sums = []

    def advance(self, arrays, others=()):
        if not self.line:
            self.sums += [lax.psum(a, "dp") for a in arrays]
            return others
        arrays, inward, across, outward, others = tie(
            list(arrays), self.inward, self.across, self.outward, others
        )
        self.inward, self.outward = [], []
        if len(arrays) == 1 and [a.shape for a, _ in inward + across] == [arrays[0].shape] * 2:
            pairs, leaving = line_step(self.outer, *inward[0], arrays[0], *across[0])
            sent = lax.ppermute(leaving, "dp", [(0, 1), (1, 0), (2, 3), (3, 2)])
            self.inward.append((arrays[0], sent))
            self.outward.append((leaving, sent))
            pairs = [pairs]
        else:
            pairs = [add_up(own, sent).astype(BF16) for own, sent in inward]
            totals = [add_up(own, sent).astype(BF16) for own, sent in across]
            self.inward = [(a, lax.ppermute(a, "dp", [(0, 1), (3, 2)])) for a in arrays]
            self.outward = [(a, lax.ppermute(a, "dp", [(1, 0), (2, 3)])) for a in totals]
        self.across = [(a, lax.ppermute(a, "dp", [(1, 2), (2, 1)])) for a in pairs]
        self.sums += [jnp.where(self.outer, sent, own) for own, sent in outward]
        return others


    def leave(self, array):
        return lax.ppermute(array, "dp", [(0, 1), (3, 2)]) if self.line else lax.psum(array, "dp")

    def add(self, array, sent):
        if self.line:
            self.inward.append((array, sent))
        else:
            self.sums.append(sent)

    def advance_and_peek(self):
        self.advance([])
        if not self.line:
            return self.sums[-2]
        own, sent = self.outward[-1]
        return jnp.where(self.outer, sent, own)


def tensor_bits():
    n, bits, bit = lax.axis_size("tensor"), [], 1
    while bit < n:
        bits.append(bit)
        bit *= 2
    return bits


def reduce_blocks(blocks):
    n, me = blocks.shape[0], lax.axis_index("tensor")
    held = [lax.dynamic_index_in_dim(blocks, me ^ r, 0, keepdims=False) for r in range(n)]
    for bit in tensor_bits():
        keep = jnp.stack([held[r] for r in range(len(held)) if r % 2 == 0])
        give = jnp.stack([held[r] for r in range(len(held)) if r % 2 == 1])
        total = add_up(keep, swap(give.astype(BF16), bit))
        held = [total[k] for k in range(total.shape[0])]
    return held[0]


def gather_blocks(block):
    n, me = lax.axis_size("tensor"), lax.axis_index("tensor")
    held = block[None]
    for bit in reversed(tensor_bits()):
        other = swap(held, bit)
        held = jnp.stack([held, other], 1).reshape(2 * held.shape[0], *block.shape)
    result = jnp.zeros_like(held)
    for r in range(n):
        result = lax.dynamic_update_index_in_dim(result, held[r], me ^ r, 0)
    return result


def gather_near(values):
    if lax.axis_size("tensor") != 8:
        return values, values
    return swap(values, 2), swap(values, 4)


def gather_pairs(values):
    parts, bits = [values], tensor_bits()
    for bit in bits:
        parts = parts + [swap(part, bit) for part in parts]
    return [(parts[i], parts[i + 1]) for i in range(0, len(parts), 2)]


def halves(value):
    rows = value.shape[0] // 2
    return value[:rows], value[rows:]


def reduce_begin(count, terms, between):
    n = lax.axis_size("tensor")
    if n != 8:
        parts = []
        for i in range(count):
            own, other = terms(i, None)
            parts.append(add_up(own, swap(other, 1)))
        while len(parts) > 1:
            half = len(parts) // 2
            parts = [add_up(parts[i], swap(parts[half + i].astype(BF16), 2 * half)) for i in range(half)]
        between(parts[0])
        return parts[0], ()
    own_d, other_d = (terms(3, between(None)))
    core_d = swap(other_d, 1)
    own_y, other_y = (terms(2, own_d))
    core_y = swap(other_y, 1)
    diagonal = add_up(own_d, core_d).astype(BF16)
    diagonal, own_y = tie(diagonal, own_y)
    first, second = halves(diagonal)
    from_x, from_y = swap(first, 2), swap(second, 4)
    own_x, other_x = (terms(1, diagonal))
    core_x = swap(other_x, 1)
    own, other = (terms(0, own_x))
    core = swap(other, 1)
    low, high = halves(add_up(own_y, core_y))
    for_y = jnp.concatenate([add_up(low, from_x), high]).astype(BF16)
    low, high = halves(add_up(own_x, core_x))
    for_x = jnp.concatenate([low, add_up(high, from_y)]).astype(BF16)
    return (own, core), (for_x, for_y)


def reduce_end(own, sent):
    if not sent:
        return own
    return add_up(*own, swap(sent[0], 2), swap(sent[1], 4))


def per_device(
    tokens,
    lengths,
    query_weight,
    key_weight,
    value_weight,
    output_weight,
    gate_weight,
    up_weight,
    down_weight,
    gain_attn,
    gain_mlp,
    pair_grad,
    cotangent,
):
    seqs, rows, width = tokens.shape
    n = lax.axis_size("tensor")
    me = lax.axis_index("tensor")
    top = n // 2
    flat = seqs * rows
    local_pos = me * rows + jnp.arange(rows)
    valid = (local_pos[None, :] < lengths[:, None]).astype(F32)[..., None]
    x = tokens.astype(F32)
    attn_gain = gain_attn.astype(F32)
    mlp_gain = gain_mlp.astype(F32)
    grad_y = cotangent.astype(F32)
    kv_weight = jnp.concatenate([key_weight, value_weight], axis=1)

    norm_in = normed(x, attn_gain).astype(BF16).reshape(flat, width)
    far_in = swap(norm_in, top)
    far_in = (far_in, swap(far_in, 1))
    near_in = (norm_in, swap(norm_in, 1))
    def slopes_of(blocks):
        return [dot(block, down_weight, ((1,), (1,))) for block in blocks]

    def with_core(part):
        return part, swap(part, 1)

    grad_out = (valid * grad_y).astype(BF16).reshape(flat, width)
    own_grads = with_core(grad_out)
    own_slopes, query_parts = tie(slopes_of(own_grads), gather_middle(query_weight))
    query_weights = jnp.concatenate(query_parts, axis=1)
    heads_width = query_weights.shape[1]
    own_cos, own_sin = rope_block(me * rows, rows)
    kv_raw = dot(norm_in, kv_weight, ((1,), (0,))).reshape(seqs, rows, 2 * HEAD)
    key_raw = kv_raw[..., :HEAD]
    key_own = key_raw * own_cos + jnp.roll(key_raw, HEAD // 2, axis=-1) * own_sin
    kv_own = jnp.concatenate([key_own, kv_raw[..., HEAD:]], axis=-1).astype(BF16)

    output_weight, kv_own = tie(output_weight, kv_own)
    output_parts = gather_middle(output_weight)
    kv = lax.all_gather(kv_own, "tensor", axis=1, tiled=True)

    def place_of(offset):
        place = jnp.stack([me ^ offset, me ^ (offset + 1)]).astype(jnp.int32)
        blocks = [rope_block(place[i] * rows, rows) for i in range(2)]
        return place, (jnp.stack([b[0] for b in blocks]), jnp.stack([b[1] for b in blocks]))

    def attend(part, place, table):
        return attention_forward(place, lengths, part, query_weights, kv, *table)

    def portions_of(mixed):
        return [dot(mixed[i], output_weights, ((1,), (0,)), BF16) for i in range(2)]

    near_place, near_table = place_of(0)
    far_place, far_table = place_of(top)
    grad_out, _ = tie(grad_out, norm_in)
    grad_far = swap(grad_out, top)
    near_result = attend(near_in, near_place, near_table)
    far_in, _ = tie(far_in, near_result[0])
    far_result = attend(far_in, far_place, far_table)
    output_parts, far_mixed, grad_far = tie(output_parts, far_result[0], grad_far)
    output_weights = jnp.concatenate(output_parts, axis=0)
    far_portions = portions_of(far_mixed)
    for_far = add_up(far_portions[0], swap(far_portions[1], 1)).astype(BF16)
    for_far, near_mixed = tie(for_far, near_result[0])
    from_far = swap(for_far, top)
    near_portions = portions_of(near_mixed)
    near_core = swap(near_portions[1], 1)
    if n == 8:
        grad_out, _ = tie(grad_out, far_mixed)
        grad_side = swap(grad_out, 2)
        size = flat // 2
        from_far, grad_side, grad_far = tie(from_far, grad_side, grad_far)
        grad_diagonal = [swap(grad_side[:size], 4), swap(grad_far[size:], 2)]
    attn_out = add_up(near_portions[0], near_core, from_far)
    hidden = x + valid * attn_out.reshape(seqs, rows, width)

    chips = n // 2
    norm_mid = normed(hidden, mlp_gain).astype(BF16).reshape(flat, width)
    gate_rows, up_rows = gate_weight.T, up_weight.T

    mids, acts, g_gates, g_ups = [], [], [], []

    def forward_blocks(blocks, slopes):
        for mid, slope in zip(blocks, slopes):
            gate = dot(mid, gate_rows, ((1,), (1,)))
            up = dot(mid, up_rows, ((1,), (1,)))
            sig = 1.0 / (1.0 + jnp.exp(-gate))
            silu = gate * sig
            mids.append(mid)
            acts.append((silu * up).astype(BF16))
            g_gates.append((slope * up * sig * (1.0 + gate * (1.0 - sig))).astype(BF16))
            g_ups.append((slope * silu).astype(BF16))

    def diagonal_blocks(parts):
        return [jnp.concatenate(p) for p in zip(*[with_core(part) for part in parts])]

    if n == 8:
        at_x, at_y = gather_near(norm_mid)
        grads = [*own_grads, *with_core(grad_side), *with_core(grad_far)]
        slopes = own_slopes + slopes_of(grads[2:])
        forward_blocks(with_core(norm_mid), slopes[:2])
        at_x, at_y, slopes, acts[1] = tie(at_x, at_y, slopes, acts[1])
        diagonal = [swap(at_x[:size], 4), swap(at_y[size:], 2)]
        forward_blocks((*with_core(at_x), *with_core(at_y)), slopes[2:6])
        grad_down = sum_of_products(acts[:6], grads[:6])
        diagonal, grad_diagonal, grad_down = tie(diagonal, grad_diagonal, grad_down)
        grads += diagonal_blocks(grad_diagonal)
        forward_blocks(diagonal_blocks(diagonal), slopes_of(grads[6:]))
    else:
        grads = [block for pair in gather_pairs(grad_out) for block in pair]
        forward_blocks([block for pair in gather_pairs(norm_mid) for block in pair], slopes_of(grads))
        grad_down = sum_of_products(acts[:-2], grads[:-2])

    def mid_term(r):
        terms = dot(g_gates[r], gate_rows, ((1,), (0,))) + dot(g_ups[r], up_rows, ((1,), (0,)))
        return terms.astype(BF16)

    def mid_terms(i, after):
        for k in (2 * i, 2 * i + 1):
            if after is not None:
                g_gates[k], g_ups[k], _ = tie(g_gates[k], g_ups[k], after)
        return mid_term(2 * i), mid_term(2 * i + 1)

    sums, down_parts = LineSum(), []

    def down_gradient(after):
        last = acts[-2:] if after is None else tie(acts[-2:], after)[0]
        after = last
        down_parts.extend(halves(sum_of_products(last, grads[-2:], grad_down).astype(BF16)))
        after, down_parts[1] = sums.advance([down_parts[0]], (after, down_parts[1]))
        down_parts.append(sums.leave(down_parts[1]))
        return after

    mid_own, mid_sent = reduce_begin(chips, mid_terms, down_gradient)
    grad_mid = reduce_end(mid_own, mid_sent).reshape(seqs, rows, width)

    g_gates, g_ups, mids = sums.advance([], (g_gates, g_ups, mids))
    sums.add(down_parts[1], down_parts[2])
    mid_all = [jnp.concatenate(mids)]
    grad_gate = halves(sum_of_products(g_gates, mid_all).astype(BF16))
    back, mlp_gain_part = norm_back(hidden, mlp_gain, grad_mid)
    grad_hidden = grad_y + back
    grad_attn = (valid * grad_hidden).astype(BF16).reshape(flat, width)
    far_grad = swap(grad_attn, top)
    near_grad = (grad_attn, swap(grad_attn, 1))

    def attend_back(part, result, place, table):
        return attention_backward(
            place, lengths, part, output_weights, query_weights, result[1], result[2], kv, *table
        )

    def product(left, right):
        return dot(jnp.concatenate(left), jnp.concatenate(right), ((0,), (0,)), BF16)

    g_ups, near_grad = sums.advance([grad_gate[0]], (g_ups, near_grad))
    grad_up = halves(sum_of_products(g_ups, mid_all).astype(BF16))
    near_q, near_terms, near_kv = attend_back(near_grad, near_result, near_place, near_table)
    near_core = swap(near_terms[1], 1)

    far_grad, near_q, near_kv = sums.advance([grad_gate[1]], (far_grad, near_q, near_kv))
    far_grad = (far_grad, swap(far_grad, 1))
    far_q, far_terms, far_kv = attend_back(far_grad, far_result, far_place, far_table)
    for_far = add_up(far_terms[0], swap(far_terms[1], 1)).astype(BF16)
    from_far = swap(for_far, top)

    far_grad, far_q, far_kv = sums.advance([grad_up[0]], (far_grad, far_q, far_kv))
    unit = output_weight.shape[0]
    kv_blocks = (near_kv + far_kv).astype(BF16).reshape(seqs, n, rows, 2 * HEAD).swapaxes(0, 1)
    kv_sum = reduce_blocks(kv_blocks)
    wq_full = product([near_q[0], near_q[1], far_q[0], far_q[1]], [*near_in, *far_in])
    wq_full, kv_sum = tie(wq_full, kv_sum)
    wq_part = reduce_middle([wq_full[i * unit : (i + 1) * unit] for i in range(heads_width // unit)])
    wq_part = wq_part.astype(BF16)
    key_grad = kv_sum[..., :HEAD]
    key_grad = key_grad * own_cos - jnp.roll(key_grad, HEAD // 2, axis=-1) * own_sin
    kv_grad = jnp.concatenate([key_grad, kv_sum[..., HEAD:]], -1).astype(BF16).reshape(flat, 2 * HEAD)

    far_grad = sums.advance([grad_up[1]], far_grad)
    grad_in = add_up(near_terms[0], near_core, from_far)
    grad_in = grad_in + dot(kv_grad, kv_weight, ((1,), (1,)))
    kv_portion = dot(norm_in, kv_grad, ((0,), (0,)))
    back, attn_gain_part = norm_back(x, attn_gain, grad_in.reshape(seqs, rows, width))
    grad_tokens = grad_hidden + back
    gains = jnp.concatenate([attn_gain_part, mlp_gain_part]).reshape(-1, 2 * HEAD)
    shared = jnp.concatenate([kv_portion + pair_grad[0, 0], gains])
    shared = jnp.pad(shared, ((0, -shared.shape[0] % (16 * n)), (0, 0))).astype(BF16)
    shared = reduce_blocks(shared.reshape(n, -1, 2 * HEAD)).astype(BF16)


    mixed = [r[0][i] for r in (near_result, far_result) for i in range(2)]
    wo_full = product(mixed, [*near_grad, *far_grad])
    wo_full, shared = tie(wo_full, shared)
    wo_part = reduce_middle([wo_full[i * unit : (i + 1) * unit] for i in range(heads_width // unit)])
    wo_part = wo_part.astype(BF16)

    acts = sums.advance([wq_part, shared], acts)

    def out_terms(i, after):
        left = acts[2 * i : 2 * i + 2]
        left = left if after is None else tie(left, after)[0]
        return [dot(part, down_weight, ((1,), (0,)), BF16) for part in left]

    out_own, out_sent = reduce_begin(chips, out_terms, lambda after: after)
    rows_out = reduce_end(out_own, out_sent)
    output = (hidden + valid * rows_out.reshape(seqs, rows, width)).astype(BF16)
    sums.advance([wo_part])
    shared = sums.advance_and_peek()
    shared = sums.advance([], gather_blocks(shared))
    sums.advance([])
    down_1, down_2, gate_1, gate_2, up_1, up_2, wq_sum, _, wo_sum = sums.sums
    shared = shared.reshape(-1, 2 * HEAD).astype(F32)
    gains = shared[width : width + gains.shape[0]].reshape(2, width)
    return (
        output,
        grad_tokens,
        wq_sum.astype(F32).T,
        shared[:width, :HEAD],
        shared[:width, HEAD:],
        wo_sum.astype(F32),
        jnp.concatenate([gate_1, gate_2]).astype(F32).T,
        jnp.concatenate([up_1, up_2]).astype(F32).T,
        jnp.concatenate([down_1, down_2]).astype(F32),
        gains[0],
        gains[1],
    )


def solution(mesh):
    placed = (
        P("dp", "tensor", None),
        P("dp"),
        P(None, "tensor"),
        P(),
        P(),
        P("tensor", None),
        P(None, "tensor"),
        P(None, "tensor"),
        P("tensor", None),
        P(),
        P(),
        P("dp", "tensor", None, None),
        P("dp", "tensor", None),
    )
    return jax.shard_map(
        per_device,
        mesh=mesh,
        in_specs=placed,
        out_specs=(
            P("dp", "tensor", None),
            P("dp", "tensor", None),
            P(None, "tensor"),
            P(),
            P(),
            P("tensor", None),
            P(None, "tensor"),
            P(None, "tensor"),
            P("tensor", None),
            P(),
            P(),
        ),
        check_vma=False,
    )
```

```python
import functools

import jax
import jax.numpy as jnp
from jax import lax
from jax.experimental import pallas as pl
from jax.experimental.pallas import tpu as pltpu
from jax.sharding import PartitionSpec as P

HEAD = 128
KEY_BLOCK = 256
JOIN_COST = 8_000_000_000
BACK_COST = 1
FORTH_COST = 60
SMALL_SHIFT = 1e-05
ROPE_BASE = 10000.0
NEG_FILL = -1e30
LOG2E = 1.4426950408889634
F32 = jnp.float32
BF16 = jnp.bfloat16


def rms_scale(values):
    return lax.rsqrt(jnp.mean(values * values, axis=-1, keepdims=True) + SMALL_SHIFT)


def normed(values, gain_vec):
    return values * rms_scale(values) * gain_vec


def norm_back(values, gain_vec, grad_vals):
    scale_vals = rms_scale(values)
    scaled = grad_vals * gain_vec
    inner_mean = jnp.mean(scaled * values, axis=-1, keepdims=True)
    grad_values = scale_vals * scaled - values * (scale_vals * scale_vals * scale_vals) * inner_mean
    grad_gain = jnp.sum(grad_vals * values * scale_vals, axis=(0, 1))
    return grad_values, grad_gain


def rope_block(start, rows):
    half = HEAD // 2
    frequency = ROPE_BASE ** (-2.0 * jnp.arange(half, dtype=F32) / HEAD)
    angles = (start + jnp.arange(rows)).astype(F32)[:, None] * frequency[None, :]
    cosine, sine = jnp.cos(angles), jnp.sin(angles)
    return jnp.concatenate([cosine, cosine], 1), jnp.concatenate([-sine, sine], 1)


def swap(values, bit):
    n = lax.axis_size("tensor")
    return lax.ppermute(values, "tensor", [(i, i ^ bit) for i in range(n)])


def dot(a, b, dims, out=F32):
    return lax.dot_general(a, b, (dims, ((), ())), preferred_element_type=F32).astype(out)


def add_up(*parts):
    total = parts[0].astype(F32)
    for part in parts[1:]:
        total = total + part.astype(F32)
    return total


def key_branches(start, rows, span, body):
    blocks = span // KEY_BLOCK
    needed = (start + rows + KEY_BLOCK - 1) // KEY_BLOCK
    for count in range(1, blocks + 1):
        pl.when(needed == count)(functools.partial(body, count * KEY_BLOCK))


def stack_heads(values, heads):
    return jnp.concatenate([values[:, h * HEAD : (h + 1) * HEAD] for h in range(heads)], axis=0)


def matmul(a, b, contract):
    return lax.dot_general(a, b, (contract, ((), ())), preferred_element_type=F32)


def masked_scores(keys, query, start, rows, heads, count):
    scores = matmul(keys, query, ((1,), (1,)))
    key_pos = lax.broadcasted_iota(jnp.int32, (KEY_BLOCK, rows), 0) + (count - KEY_BLOCK)
    row_pos = lax.broadcasted_iota(jnp.int32, (KEY_BLOCK, rows), 1) + start
    allowed = key_pos <= row_pos
    last = scores[count - KEY_BLOCK :]
    last = jnp.concatenate(
        [jnp.where(allowed, last[:, h * rows : (h + 1) * rows], NEG_FILL) for h in range(heads)], axis=1
    )
    if count == KEY_BLOCK:
        return last
    return jnp.concatenate([scores[: count - KEY_BLOCK], last], axis=0)


def forward_kernel(
    place, lengths, x0_ref, x1_ref, wq_ref, kv_ref, cos_ref, sin_ref, mixed_ref, query_ref, lse_ref, raw_ref, vt_ref
):
    a, s = pl.program_id(0), pl.program_id(1)
    seqs, span = kv_ref.shape[0], kv_ref.shape[1]
    rows = x0_ref.shape[0] // seqs
    heads = wq_ref.shape[1] // HEAD
    start = place[a] * rows
    here = pl.ds(pl.multiple_of(s * rows, rows), rows)
    live = start < lengths[s]
    factor = HEAD ** (-0.5) * LOG2E

    for k, x_ref in enumerate((x0_ref, x1_ref)):

        @pl.when((a == k) & (s == 0))
        def _(x_ref=x_ref):
            raw_ref[...] = matmul(x_ref[...], wq_ref[...], ((1,), (0,)))

    @pl.when(a == 0)
    def _():
        vt_ref[s] = kv_ref[s, :, HEAD:].T

    pieces = []
    for h in range(heads):
        raw = raw_ref[here, h * HEAD : (h + 1) * HEAD]
        pieces.append((raw * cos_ref[0] + pltpu.roll(raw, HEAD // 2, 1) * sin_ref[0]).astype(BF16))
    query_ref[0, s] = jnp.concatenate(pieces, axis=0)

    def body(count):
        scores = masked_scores(kv_ref[s, :count, :HEAD], query_ref[0, s], start, rows, heads, count)
        top = jnp.max(scores, axis=0, keepdims=True)
        terms = jnp.exp2((scores - top) * factor)
        total = jnp.sum(terms, axis=0, keepdims=True)
        out = matmul(vt_ref[s, :, :count], terms.astype(BF16), ((1,), (0,))) / total
        lse_ref[0, s] = jnp.broadcast_to(top * factor + jnp.log2(total), lse_ref.shape[2:])
        for h in range(heads):
            piece = out[:, h * rows : (h + 1) * rows].T
            mixed_ref[0, here, h * HEAD : (h + 1) * HEAD] = piece.astype(BF16)

    @pl.when(live)
    def _():
        key_branches(start, rows, span, body)

    @pl.when(jnp.logical_not(live))
    def _():
        mixed_ref[0, here] = jnp.zeros((rows, heads * HEAD), BF16)
        lse_ref[0, s] = jnp.zeros(lse_ref.shape[2:], F32)


def whole(shape):
    return pl.BlockSpec(shape, lambda a, *_: (0,) * len(shape))


def blocked(shape):
    return pl.BlockSpec((1, *shape[1:]), lambda a, *_: (a,) + (0,) * (len(shape) - 1))


def attention_forward(place, lengths, parts, query_weights, kv, cosine, sine):
    flat, width = parts[0].shape
    seqs, span = kv.shape[0], kv.shape[1]
    rows, wide = flat // seqs, query_weights.shape[1]
    heads = wide // HEAD
    shapes = [(2, flat, wide), (2, seqs, heads * rows, HEAD), (2, seqs, 8, heads * rows)]
    return pl.pallas_call(
        forward_kernel,
        grid_spec=pltpu.PrefetchScalarGridSpec(
            num_scalar_prefetch=2,
            grid=(2, seqs),
            in_specs=[
                whole(parts[0].shape),
                whole(parts[1].shape),
                whole(query_weights.shape),
                whole(kv.shape),
                blocked(cosine.shape),
                blocked(sine.shape),
            ],
            out_specs=[blocked(shape) for shape in shapes],
            scratch_shapes=[pltpu.VMEM((flat, wide), F32), pltpu.VMEM((seqs, HEAD, span), BF16)],
        ),
        out_shape=[jax.ShapeDtypeStruct(s, t) for s, t in zip(shapes, (BF16, BF16, F32))],
        compiler_params=pltpu.CompilerParams(vmem_limit_bytes=48 * 1024 * 1024),
        cost_estimate=pl.CostEstimate(flops=FORTH_COST * flat * wide * span, bytes_accessed=kv.size, transcendentals=0),
        name="attention_forward",
    )(place, lengths, *parts, query_weights, kv, cosine, sine)


def backward_kernel(
    place, lengths, g0_ref, g1_ref, wo_ref, wq_ref, query_ref, lse_ref, kv_ref, cos_ref, sin_ref,
    gq_ref, in_ref, gkv_ref, gm_ref, kt_ref,
):
    a, s = pl.program_id(0), pl.program_id(1)
    seqs, span = kv_ref.shape[0], kv_ref.shape[1]
    rows = g0_ref.shape[0] // seqs
    heads = wq_ref.shape[1] // HEAD
    start = place[a] * rows
    here = pl.ds(pl.multiple_of(s * rows, rows), rows)
    live = start < lengths[s]
    scale = HEAD ** (-0.5)
    factor = scale * LOG2E

    for k, g_ref in enumerate((g0_ref, g1_ref)):

        @pl.when((a == k) & (s == 0))
        def _(g_ref=g_ref):
            gm_ref[...] = matmul(g_ref[...], wo_ref[...], ((1,), (1,))).astype(BF16)

    @pl.when(a == 0)
    def _():
        gkv_ref[s] = jnp.zeros(gkv_ref.shape[1:], F32)
        kt_ref[s] = kv_ref[s, :, :HEAD].T

    def body(count):
        query = query_ref[0, s]
        grad = stack_heads(gm_ref[here, :], heads)
        scores = masked_scores(kv_ref[s, :count, :HEAD], query, start, rows, heads, count)
        probs = jnp.exp2(scores * factor - lse_ref[0, s, 0:1, :])
        grad_probs = matmul(kv_ref[s, :count, HEAD:], grad, ((1,), (1,)))
        row_dots = jnp.sum(probs * grad_probs, axis=0, keepdims=True)
        grad_scores = (probs * (grad_probs - row_dots)).astype(BF16)
        gkv_ref[s, :count, :HEAD] += scale * matmul(grad_scores, query, ((1,), (0,)))
        gkv_ref[s, :count, HEAD:] += matmul(probs.astype(BF16), grad, ((1,), (0,)))
        grad_query = matmul(kt_ref[s, :, :count], grad_scores, ((1,), (0,)))
        for h in range(heads):
            piece = grad_query[:, h * rows : (h + 1) * rows].T * scale
            piece = piece * cos_ref[0] - pltpu.roll(piece, HEAD // 2, 1) * sin_ref[0]
            gq_ref[0, here, h * HEAD : (h + 1) * HEAD] = piece.astype(BF16)

    @pl.when(live)
    def _():
        key_branches(start, rows, span, body)

    @pl.when(jnp.logical_not(live))
    def _():
        gq_ref[0, here] = jnp.zeros((rows, heads * HEAD), BF16)

    @pl.when(s == seqs - 1)
    def _():
        in_ref[0] = matmul(gq_ref[0], wq_ref[...], ((1,), (1,))).astype(BF16)


def attention_backward(place, lengths, grads, output_weights, query_weights, query, lse, kv, cosine, sine):
    flat, width = grads[0].shape
    seqs, span = kv.shape[0], kv.shape[1]
    wide = query_weights.shape[1]
    operands = (*grads, output_weights, query_weights, query, lse, kv, cosine, sine)
    specs = [whole(v.shape) for v in operands]
    for k in (4, 5, 7, 8):
        specs[k] = blocked(operands[k].shape)
    return pl.pallas_call(
        backward_kernel,
        grid_spec=pltpu.PrefetchScalarGridSpec(
            num_scalar_prefetch=2,
            grid=(2, seqs),
            in_specs=specs,
            out_specs=[blocked((2, flat, wide)), blocked((2, flat, width)), whole(kv.shape)],
            scratch_shapes=[pltpu.VMEM((flat, wide), BF16), pltpu.VMEM((seqs, HEAD, span), BF16)],
        ),
        out_shape=[
            jax.ShapeDtypeStruct((2, flat, wide), BF16),
            jax.ShapeDtypeStruct((2, flat, width), BF16),
            jax.ShapeDtypeStruct(kv.shape, F32),
        ],
        compiler_params=pltpu.CompilerParams(vmem_limit_bytes=56 * 1024 * 1024),
        cost_estimate=pl.CostEstimate(flops=BACK_COST * flat * wide * span, bytes_accessed=kv.size, transcendentals=0),
        name="attention_backward",
    )(place, lengths, *operands)


def middle_bits(n):
    bits, bit = [], 2
    while bit < n // 2:
        bits.append(bit)
        bit *= 2
    return bits


def gather_middle(values):
    parts = [values]
    for bit in middle_bits(lax.axis_size("tensor")):
        parts = parts + [swap(part, bit) for part in parts]
    return parts


def reduce_middle(parts):
    for bit in reversed(middle_bits(lax.axis_size("tensor"))):
        half = len(parts) // 2
        parts = [add_up(parts[i], swap(parts[half + i].astype(BF16), bit)) for i in range(half)]
    return parts[0]


def sum_of_products(left, right, start=None):
    total = dot(jnp.concatenate(left), jnp.concatenate(right), ((0,), (0,)))
    return total if start is None else start + total


def tie(*values):
    return lax.optimization_barrier(values)


def line_step(outer, own_in, sent_in, fresh, own_across, sent_across):
    rows, width = fresh.shape

    def kernel(outer_ref, a_ref, b_ref, c_ref, d_ref, e_ref, pair_ref, leaving_ref):
        @pl.when(outer_ref[0] == 1)
        def _():
            pair_ref[...] = c_ref[...]
            leaving_ref[...] = c_ref[...]

        @pl.when(outer_ref[0] == 0)
        def _():
            pair_ref[...] = (a_ref[...].astype(F32) + b_ref[...].astype(F32)).astype(BF16)
            leaving_ref[...] = (d_ref[...].astype(F32) + e_ref[...].astype(F32)).astype(BF16)

    steps = 4
    inner_block = pl.BlockSpec((rows, width // steps), lambda i, o: (0, i * (1 - o[0])))
    outer_block = pl.BlockSpec((rows, width // steps), lambda i, o: (0, i * o[0]))
    block = pl.BlockSpec((rows, width // steps), lambda i, o: (0, i))
    return pl.pallas_call(
        kernel,
        grid_spec=pltpu.PrefetchScalarGridSpec(
            num_scalar_prefetch=1,
            grid=(steps,),
            in_specs=[inner_block, inner_block, outer_block, inner_block, inner_block],
            out_specs=[block, block],
        ),
        out_shape=[jax.ShapeDtypeStruct((rows, width), BF16)] * 2,
        name="line_step",
    )(outer.astype(jnp.int32).reshape(1), own_in, sent_in, fresh, own_across, sent_across)


class LineSum:
    def __init__(self):
        self.line = lax.axis_size("dp") == 4
        place = lax.axis_index("dp")
        self.outer = (place == 0) | (place == 3)
        self.inward, self.across, self.outward = [], [], []
        self.sums = []

    def advance(self, arrays, others=()):
        if not self.line:
            self.sums += [lax.psum(a, "dp") for a in arrays]
            return others
        arrays, inward, across, outward, others = tie(
            list(arrays), self.inward, self.across, self.outward, others
        )
        self.inward, self.outward = [], []
        if len(arrays) == 1 and [a.shape for a, _ in inward + across] == [arrays[0].shape] * 2:
            pairs, leaving = line_step(self.outer, *inward[0], arrays[0], *across[0])
            sent = lax.ppermute(leaving, "dp", [(0, 1), (1, 0), (2, 3), (3, 2)])
            self.inward.append((arrays[0], sent))
            self.outward.append((leaving, sent))
            pairs = [pairs]
        else:
            pairs = [add_up(own, sent).astype(BF16) for own, sent in inward]
            totals = [add_up(own, sent).astype(BF16) for own, sent in across]
            self.inward = [(a, lax.ppermute(a, "dp", [(0, 1), (3, 2)])) for a in arrays]
            self.outward = [(a, lax.ppermute(a, "dp", [(1, 0), (2, 3)])) for a in totals]
        self.across = [(a, lax.ppermute(a, "dp", [(1, 2), (2, 1)])) for a in pairs]
        self.sums += [jnp.where(self.outer, sent, own) for own, sent in outward]
        return others


    def leave(self, array):
        return lax.ppermute(array, "dp", [(0, 1), (3, 2)]) if self.line else lax.psum(array, "dp")

    def add(self, array, sent):
        if self.line:
            self.inward.append((array, sent))
        else:
            self.sums.append(sent)

    def advance_and_peek(self):
        self.advance([])
        if not self.line:
            return self.sums[-2]
        own, sent = self.outward[-1]
        return jnp.where(self.outer, sent, own)


def tensor_bits():
    n, bits, bit = lax.axis_size("tensor"), [], 1
    while bit < n:
        bits.append(bit)
        bit *= 2
    return bits


def reduce_blocks(blocks):
    n, me = blocks.shape[0], lax.axis_index("tensor")
    held = [lax.dynamic_index_in_dim(blocks, me ^ r, 0, keepdims=False) for r in range(n)]
    for bit in tensor_bits():
        keep = jnp.stack([held[r] for r in range(len(held)) if r % 2 == 0])
        give = jnp.stack([held[r] for r in range(len(held)) if r % 2 == 1])
        total = add_up(keep, swap(give.astype(BF16), bit))
        held = [total[k] for k in range(total.shape[0])]
    return held[0]


def gather_blocks(block):
    n, me = lax.axis_size("tensor"), lax.axis_index("tensor")
    held = block[None]
    for bit in reversed(tensor_bits()):
        other = swap(held, bit)
        held = jnp.stack([held, other], 1).reshape(2 * held.shape[0], *block.shape)
    result = jnp.zeros_like(held)
    for r in range(n):
        result = lax.dynamic_update_index_in_dim(result, held[r], me ^ r, 0)
    return result


def gather_near(values):
    if lax.axis_size("tensor") != 8:
        return values, values
    return swap(values, 2), swap(values, 4)


def gather_pairs(values):
    parts, bits = [values], tensor_bits()
    for bit in bits:
        parts = parts + [swap(part, bit) for part in parts]
    return [(parts[i], parts[i + 1]) for i in range(0, len(parts), 2)]


def halves(value):
    rows = value.shape[0] // 2
    return value[:rows], value[rows:]


def reduce_begin(count, terms, between):
    n = lax.axis_size("tensor")
    if n != 8:
        parts = []
        for i in range(count):
            own, other = terms(i, None)
            parts.append(add_up(own, swap(other, 1)))
        while len(parts) > 1:
            half = len(parts) // 2
            parts = [add_up(parts[i], swap(parts[half + i].astype(BF16), 2 * half)) for i in range(half)]
        between(parts[0])
        return parts[0], ()
    own_d, other_d = (terms(3, between(None)))
    core_d = swap(other_d, 1)
    own_y, other_y = (terms(2, own_d))
    core_y = swap(other_y, 1)
    diagonal = add_up(own_d, core_d).astype(BF16)
    diagonal, own_y = tie(diagonal, own_y)
    first, second = halves(diagonal)
    from_x, from_y = swap(first, 2), swap(second, 4)
    own_x, other_x = (terms(1, diagonal))
    core_x = swap(other_x, 1)
    own, other = (terms(0, own_x))
    core = swap(other, 1)
    low, high = halves(add_up(own_y, core_y))
    for_y = jnp.concatenate([add_up(low, from_x), high]).astype(BF16)
    low, high = halves(add_up(own_x, core_x))
    for_x = jnp.concatenate([low, add_up(high, from_y)]).astype(BF16)
    return (own, core), (for_x, for_y)


def reduce_end(own, sent):
    if not sent:
        return own
    return add_up(*own, swap(sent[0], 2), swap(sent[1], 4))


def per_device(
    tokens,
    lengths,
    query_weight,
    key_weight,
    value_weight,
    output_weight,
    gate_weight,
    up_weight,
    down_weight,
    gain_attn,
    gain_mlp,
    pair_grad,
    cotangent,
):
    seqs, rows, width = tokens.shape
    n = lax.axis_size("tensor")
    me = lax.axis_index("tensor")
    top = n // 2
    flat = seqs * rows
    local_pos = me * rows + jnp.arange(rows)
    valid = (local_pos[None, :] < lengths[:, None]).astype(F32)[..., None]
    x = tokens.astype(F32)
    attn_gain = gain_attn.astype(F32)
    mlp_gain = gain_mlp.astype(F32)
    grad_y = cotangent.astype(F32)
    kv_weight = jnp.concatenate([key_weight, value_weight], axis=1)

    norm_in = normed(x, attn_gain).astype(BF16).reshape(flat, width)
    far_in = swap(norm_in, top)
    far_in = (far_in, swap(far_in, 1))
    near_in = (norm_in, swap(norm_in, 1))
    def slopes_of(blocks):
        return [dot(block, down_weight, ((1,), (1,))) for block in blocks]

    def with_core(part):
        return part, swap(part, 1)

    grad_out = (valid * grad_y).astype(BF16).reshape(flat, width)
    own_grads = with_core(grad_out)
    own_slopes, query_parts = slopes_of(own_grads), gather_middle(query_weight)
    query_weights = jnp.concatenate(query_parts, axis=1)
    heads_width = query_weights.shape[1]
    own_cos, own_sin = rope_block(me * rows, rows)
    kv_raw = dot(norm_in, kv_weight, ((1,), (0,))).reshape(seqs, rows, 2 * HEAD)
    key_raw = kv_raw[..., :HEAD]
    key_own = key_raw * own_cos + jnp.roll(key_raw, HEAD // 2, axis=-1) * own_sin
    kv_own = jnp.concatenate([key_own, kv_raw[..., HEAD:]], axis=-1).astype(BF16)

    output_weight, kv_own = tie(output_weight, kv_own)
    output_parts = gather_middle(output_weight)
    kv = lax.all_gather(kv_own, "tensor", axis=1, tiled=True)

    def place_of(offset):
        place = jnp.stack([me ^ offset, me ^ (offset + 1)]).astype(jnp.int32)
        blocks = [rope_block(place[i] * rows, rows) for i in range(2)]
        return place, (jnp.stack([b[0] for b in blocks]), jnp.stack([b[1] for b in blocks]))

    def attend(part, place, table):
        return attention_forward(place, lengths, part, query_weights, kv, *table)

    def portions_of(mixed):
        return [dot(mixed[i], output_weights, ((1,), (0,)), BF16) for i in range(2)]

    near_place, near_table = place_of(0)
    far_place, far_table = place_of(top)
    grad_out, _ = tie(grad_out, norm_in)
    grad_far = swap(grad_out, top)
    near_result = attend(near_in, near_place, near_table)
    far_in, _ = tie(far_in, near_result[0])
    far_result = attend(far_in, far_place, far_table)
    output_parts, far_mixed, grad_far = tie(output_parts, far_result[0], grad_far)
    output_weights = jnp.concatenate(output_parts, axis=0)
    far_portions = portions_of(far_mixed)
    for_far = add_up(far_portions[0], swap(far_portions[1], 1)).astype(BF16)
    for_far, near_mixed = tie(for_far, near_result[0])
    from_far = swap(for_far, top)
    near_portions = portions_of(near_mixed)
    near_core = swap(near_portions[1], 1)
    if n == 8:
        grad_out, _ = tie(grad_out, far_mixed)
        grad_side = swap(grad_out, 2)
        size = flat // 2
        from_far, grad_side, grad_far = tie(from_far, grad_side, grad_far)
        grad_diagonal = [swap(grad_side[:size], 4), swap(grad_far[size:], 2)]
    attn_out = add_up(near_portions[0], near_core, from_far)
    hidden = x + valid * attn_out.reshape(seqs, rows, width)

    chips = n // 2
    norm_mid = normed(hidden, mlp_gain).astype(BF16).reshape(flat, width)
    gate_rows, up_rows = gate_weight.T, up_weight.T

    mids, acts, g_gates, g_ups = [], [], [], []

    def forward_blocks(blocks, slopes):
        for mid, slope in zip(blocks, slopes):
            gate = dot(mid, gate_rows, ((1,), (1,)))
            up = dot(mid, up_rows, ((1,), (1,)))
            sig = 1.0 / (1.0 + jnp.exp(-gate))
            silu = gate * sig
            mids.append(mid)
            acts.append((silu * up).astype(BF16))
            g_gates.append((slope * up * sig * (1.0 + gate * (1.0 - sig))).astype(BF16))
            g_ups.append((slope * silu).astype(BF16))

    def diagonal_blocks(parts):
        return [jnp.concatenate(p) for p in zip(*[with_core(part) for part in parts])]

    if n == 8:
        at_x, at_y = gather_near(norm_mid)
        grads = [*own_grads, *with_core(grad_side), *with_core(grad_far)]
        slopes = own_slopes + slopes_of(grads[2:])
        forward_blocks(with_core(norm_mid), slopes[:2])
        at_x, at_y, slopes, acts[1] = tie(at_x, at_y, slopes, acts[1])
        diagonal = [swap(at_x[:size], 4), swap(at_y[size:], 2)]
        forward_blocks((*with_core(at_x), *with_core(at_y)), slopes[2:6])
        grad_down = sum_of_products(acts[:6], grads[:6])
        diagonal, grad_diagonal, grad_down = tie(diagonal, grad_diagonal, grad_down)
        grads += diagonal_blocks(grad_diagonal)
        forward_blocks(diagonal_blocks(diagonal), slopes_of(grads[6:]))
    else:
        grads = [block for pair in gather_pairs(grad_out) for block in pair]
        forward_blocks([block for pair in gather_pairs(norm_mid) for block in pair], slopes_of(grads))
        grad_down = sum_of_products(acts[:-2], grads[:-2])

    def mid_term(r):
        terms = dot(g_gates[r], gate_rows, ((1,), (0,))) + dot(g_ups[r], up_rows, ((1,), (0,)))
        return terms.astype(BF16)

    def mid_terms(i, after):
        for k in (2 * i, 2 * i + 1):
            if after is not None:
                g_gates[k], g_ups[k], _ = tie(g_gates[k], g_ups[k], after)
        return mid_term(2 * i), mid_term(2 * i + 1)

    sums, down_parts = LineSum(), []

    def down_gradient(after):
        last = acts[-2:] if after is None else tie(acts[-2:], after)[0]
        after = last
        down_parts.extend(halves(sum_of_products(last, grads[-2:], grad_down).astype(BF16)))
        after, down_parts[1] = sums.advance([down_parts[0]], (after, down_parts[1]))
        down_parts.append(sums.leave(down_parts[1]))
        return after

    mid_own, mid_sent = reduce_begin(chips, mid_terms, down_gradient)
    grad_mid = reduce_end(mid_own, mid_sent).reshape(seqs, rows, width)

    g_gates, g_ups, mids = sums.advance([], (g_gates, g_ups, mids))
    sums.add(down_parts[1], down_parts[2])
    mid_all = [jnp.concatenate(mids)]
    grad_gate = halves(sum_of_products(g_gates, mid_all).astype(BF16))
    back, mlp_gain_part = norm_back(hidden, mlp_gain, grad_mid)
    grad_hidden = grad_y + back
    grad_attn = (valid * grad_hidden).astype(BF16).reshape(flat, width)
    far_grad = swap(grad_attn, top)
    near_grad = (grad_attn, swap(grad_attn, 1))

    def attend_back(part, result, place, table):
        return attention_backward(
            place, lengths, part, output_weights, query_weights, result[1], result[2], kv, *table
        )

    def product(left, right):
        return dot(jnp.concatenate(left), jnp.concatenate(right), ((0,), (0,)), BF16)

    g_ups, near_grad = sums.advance([grad_gate[0]], (g_ups, near_grad))
    grad_up = halves(sum_of_products(g_ups, mid_all).astype(BF16))
    near_q, near_terms, near_kv = attend_back(near_grad, near_result, near_place, near_table)
    near_core = swap(near_terms[1], 1)

    far_grad, near_q, near_kv = sums.advance([grad_gate[1]], (far_grad, near_q, near_kv))
    far_grad = (far_grad, swap(far_grad, 1))
    far_q, far_terms, far_kv = attend_back(far_grad, far_result, far_place, far_table)
    for_far = add_up(far_terms[0], swap(far_terms[1], 1)).astype(BF16)
    from_far = swap(for_far, top)

    far_grad, far_q, far_kv = sums.advance([grad_up[0]], (far_grad, far_q, far_kv))
    unit = output_weight.shape[0]
    kv_blocks = (near_kv + far_kv).astype(BF16).reshape(seqs, n, rows, 2 * HEAD).swapaxes(0, 1)
    kv_sum = reduce_blocks(kv_blocks)
    wq_full = product([near_q[0], near_q[1], far_q[0], far_q[1]], [*near_in, *far_in])
    wq_full, kv_sum = tie(wq_full, kv_sum)
    wq_part = reduce_middle([wq_full[i * unit : (i + 1) * unit] for i in range(heads_width // unit)])
    wq_part = wq_part.astype(BF16)
    key_grad = kv_sum[..., :HEAD]
    key_grad = key_grad * own_cos - jnp.roll(key_grad, HEAD // 2, axis=-1) * own_sin
    kv_grad = jnp.concatenate([key_grad, kv_sum[..., HEAD:]], -1).astype(BF16).reshape(flat, 2 * HEAD)

    far_grad = sums.advance([grad_up[1]], far_grad)
    grad_in = add_up(near_terms[0], near_core, from_far)
    grad_in = grad_in + dot(kv_grad, kv_weight, ((1,), (1,)))
    kv_portion = dot(norm_in, kv_grad, ((0,), (0,)))
    back, attn_gain_part = norm_back(x, attn_gain, grad_in.reshape(seqs, rows, width))
    grad_tokens = grad_hidden + back
    gains = jnp.concatenate([attn_gain_part, mlp_gain_part]).reshape(-1, 2 * HEAD)
    shared = jnp.concatenate([kv_portion + pair_grad[0, 0], gains])
    shared = jnp.pad(shared, ((0, -shared.shape[0] % (16 * n)), (0, 0))).astype(BF16)
    shared = reduce_blocks(shared.reshape(n, -1, 2 * HEAD)).astype(BF16)


    mixed = [r[0][i] for r in (near_result, far_result) for i in range(2)]
    wo_full = product(mixed, [*near_grad, *far_grad])
    wo_full, shared = tie(wo_full, shared)
    wo_part = reduce_middle([wo_full[i * unit : (i + 1) * unit] for i in range(heads_width // unit)])
    wo_part = wo_part.astype(BF16)

    acts = sums.advance([wq_part, shared], acts)

    def out_terms(i, after):
        left = acts[2 * i : 2 * i + 2]
        left = left if after is None else tie(left, after)[0]
        return [dot(part, down_weight, ((1,), (0,)), BF16) for part in left]

    out_own, out_sent = reduce_begin(chips, out_terms, lambda after: after)
    rows_out = reduce_end(out_own, out_sent)
    output = (hidden + valid * rows_out.reshape(seqs, rows, width)).astype(BF16)
    sums.advance([wo_part])
    shared = sums.advance_and_peek()
    shared = sums.advance([], gather_blocks(shared))
    sums.advance([])
    down_1, down_2, gate_1, gate_2, up_1, up_2, wq_sum, _, wo_sum = sums.sums
    shared = shared.reshape(-1, 2 * HEAD).astype(F32)
    gains = shared[width : width + gains.shape[0]].reshape(2, width)
    return (
        output,
        grad_tokens,
        wq_sum.astype(F32).T,
        shared[:width, :HEAD],
        shared[:width, HEAD:],
        wo_sum.astype(F32),
        jnp.concatenate([gate_1, gate_2]).astype(F32).T,
        jnp.concatenate([up_1, up_2]).astype(F32).T,
        jnp.concatenate([down_1, down_2]).astype(F32),
        gains[0],
        gains[1],
    )


def solution(mesh):
    placed = (
        P("dp", "tensor", None),
        P("dp"),
        P(None, "tensor"),
        P(),
        P(),
        P("tensor", None),
        P(None, "tensor"),
        P(None, "tensor"),
        P("tensor", None),
        P(),
        P(),
        P("dp", "tensor", None, None),
        P("dp", "tensor", None),
    )
    return jax.shard_map(
        per_device,
        mesh=mesh,
        in_specs=placed,
        out_specs=(
            P("dp", "tensor", None),
            P("dp", "tensor", None),
            P(None, "tensor"),
            P(),
            P(),
            P("tensor", None),
            P(None, "tensor"),
            P(None, "tensor"),
            P("tensor", None),
            P(),
            P(),
        ),
        check_vma=False,
    )
```
